32 devices in a mesh: wide: 8 (over y, x, core), narrow: 4 (over z).
Axes of the slice: x: 2, y: 2, z: 4, core: 2. Of those that a mesh axis runs over, the one named last changes fastest.
Arguments:
- clip_tokens: bfloat16 [64, 256, 1152], P(('wide', 'narrow')), may hold values from -6 to 6
- cotangent: bfloat16 [64, 256, 1152], P(None, ('wide', 'narrow')), may hold values from -8 to 8
- qkv_spatial: bfloat16 [1152, 1728], replicated, may hold values from -0.1875 to 0.1875
- proj_spatial: bfloat16 [1152, 576], replicated, may hold values from -0.25 to 0.25
- adaln_spatial: float32 [3, 1152], replicated, may hold values from -4 to 4
- qknorm_spatial: float32 [2, 72], replicated, may hold values from 0.5 to 2.5
- qkv_temporal: bfloat16 [1152, 1728], replicated, may hold values from -0.1875 to 0.1875
- proj_temporal: bfloat16 [1152, 576], replicated, may hold values from -0.25 to 0.25
- adaln_temporal: float32 [3, 1152], replicated, may hold values from -4 to 4
- qknorm_temporal: float32 [2, 72], replicated, may hold values from 0.5 to 2.5
Outputs:
- result: bfloat16 [64, 256, 1152], P(None, ('wide', 'narrow'))
- grad_clip: bfloat16 [64, 256, 1152], P(('wide', 'narrow'))
- grad_qkv_spatial: float32 [1152, 1728], P(('wide', 'narrow'))
- grad_proj_spatial: float32 [1152, 576], P(('wide', 'narrow'))
- grad_qkv_temporal: float32 [1152, 1728], P(('wide', 'narrow'))
- grad_proj_temporal: float32 [1152, 576], P(('wide', 'narrow'))
The draws below stay inside these ranges and needn't reach their ends.
All inputs are finite; a program needn't handle non-finite values.
Results may differ from the reference program's by a relative error of at most 0.015.
The reference program's roundings to bfloat16 on the way count: a program that leaves them out, or rounds other values in their place, can miss the bound.
Values may be sent and summed in bfloat16 or wider, within the bound.
No kernel may reach another device: no remote copies, remote signals or barrier semaphores. Data moves between devices by JAX's collectives and lax.ppermute only.
A program may use at most 192 MiB of HBM per device.

```python
import math
import jax
import jax.numpy as jnp
from jax import lax

D = 1152
HDIM = 72
HEADS = 8
HD = 576
P_SIZE = 256
FRAMES = 64


def spiked(values, stream_key, source, target, shards_of, factor):
    owner, partner = [(jnp.arange(values.shape[axis_at]) // (values.shape[axis_at] // shards_of)).reshape([-1 if axis == axis_at else 1 for axis in range(values.ndim)]) for axis_at in (source, target)]
    chosen = jax.random.permutation(stream_key, shards_of)[partner]
    strong = (owner == chosen) | (owner == (partner + shards_of // 2) % shards_of)
    return jnp.where(strong, factor * values, values)


def block_scale(own_key, shape, shards, low, high):
    level, own = 1.0, jax.random.fold_in(own_key, 6)
    for position, shards_of in shards:
        heights = jnp.exp(jax.random.uniform(jax.random.fold_in(own, position), (shards_of,), jnp.float32, low / len(shards), high / len(shards)))
        level = level * jnp.repeat(heights, shape[position] // shards_of).reshape([-1 if axis == position else 1 for axis in range(len(shape))])
    return level


def bell_draw(rng, shape, deviation, limit, shards=(), kind=jnp.bfloat16):
    entries = deviation * jax.random.normal(rng, shape, jnp.float32)
    if shards:
        entries = entries * block_scale(rng, shape, shards, -0.22, 0.18)
    return jnp.clip(entries, -limit, limit).astype(kind)


def bell_draw_with(rng, dims, deviation, most, cuts, heavy, kind=jnp.bfloat16):
    values = deviation * jax.random.normal(rng, dims, jnp.float32)
    if cuts:
        values = values * block_scale(rng, dims, cuts, -0.22, 0.18)
    return jnp.clip(spiked(values, jax.random.fold_in(rng, 3), *heavy), -most, most).astype(kind)


def setup_inputs(seed: int = 0) -> dict:
    streams_of = jax.random.split(jax.random.key(seed), 11)
    return {
        "clip_tokens": bell_draw(streams_of[0], (FRAMES, P_SIZE, D), 1.0, 6.0, ((0, 32),)),
        "cotangent": bell_draw_with(streams_of[1], (FRAMES, P_SIZE, D), 1.0, 8.0, ((1, 32),), (1, 2, 32, 2.75)),
        "qkv_spatial": bell_draw(streams_of[2], (D, 3 * HD), D ** -0.5, 0.1875),
        "proj_spatial": bell_draw(streams_of[3], (D, HD), HD ** -0.5, 0.25),
        "adaln_spatial": bell_draw(streams_of[4], (3, D), 1.0, 4.0, (), jnp.float32),
        "qknorm_spatial": jnp.clip(jnp.exp(jax.random.uniform(streams_of[5], (2, HDIM), jnp.float32, math.log(0.5), math.log(2.5))), 0.5, 2.5),
        "qkv_temporal": bell_draw(streams_of[6], (D, 3 * HD), D ** -0.5, 0.1875),
        "proj_temporal": bell_draw(streams_of[7], (D, HD), HD ** -0.5, 0.25),
        "adaln_temporal": bell_draw(streams_of[8], (3, D), 1.0, 4.0, (), jnp.float32),
        "qknorm_temporal": jnp.clip(jnp.exp(jax.random.uniform(streams_of[9], (2, HDIM), jnp.float32, math.log(0.5), math.log(2.5))), 0.5, 2.5),
    }


epsilon = 1e-06

def modulate(inputs, modulation):
    values = inputs.astype(jnp.float32)
    centre = values - lax.optimization_barrier(jnp.mean(values, axis=-1, keepdims=True))
    spread = lax.optimization_barrier(jnp.mean(centre * centre, axis=-1, keepdims=True))
    return centre * lax.rsqrt(spread + epsilon) * (1.0 + modulation[1]) + modulation[0]

def rms_scale(vectors, gain):
    return vectors * lax.rsqrt(lax.optimization_barrier(jnp.mean(vectors * vectors, axis=-1, keepdims=True)) + epsilon) * gain

def attend(qkv, norm_gain, seq_first):
    lead, second, _ = qkv.shape
    pieces = qkv.reshape(lead, second, 3, HEADS, HDIM)
    queries = rms_scale(pieces[:, :, 0], norm_gain[0])
    keys_all = rms_scale(pieces[:, :, 1], norm_gain[1])
    values = pieces[:, :, 2]
    if seq_first:
        score_form, mix_form = ('lbhd,mbhd->bhlm', 'bhlm,mbhd->lbhd')
    else:
        score_form, mix_form = ('blhd,bmhd->bhlm', 'bhlm,bmhd->blhd')
    scores = jnp.einsum(score_form, queries, keys_all, precision=lax.Precision.HIGHEST) / jnp.sqrt(jnp.float32(HDIM))
    weights = jnp.exp(scores)
    weights = weights / lax.optimization_barrier(jnp.sum(weights, axis=-1, keepdims=True))
    mixed = jnp.einsum(mix_form, weights, values, precision=lax.Precision.HIGHEST)
    return mixed.reshape(lead, second, HEADS * HDIM)

def block_forward(inputs, qkv_weight, proj_weight, modulation, norm_gain, seq_first):
    lead, second, features = inputs.shape
    normed = modulate(inputs, modulation).astype(jnp.bfloat16)
    qkv = jnp.dot(normed.reshape(lead * second, features), qkv_weight, preferred_element_type=jnp.float32)
    qkv = qkv.reshape(lead, second, qkv_weight.shape[1])
    mixed, pull_back = jax.vjp(lambda inner: attend(inner, norm_gain, seq_first), qkv)
    mixed_low = mixed.astype(jnp.bfloat16)
    projected = lax.dot_general(mixed_low.reshape(lead * second, -1), proj_weight, (((1,), (1,)), ((), ())), preferred_element_type=jnp.float32)
    output = inputs.astype(jnp.float32) + modulation[2] * projected.reshape(lead, second, features)
    return (output.astype(jnp.bfloat16), (normed, mixed_low, pull_back))

def block_backward(inputs, cotangent, qkv_weight, proj_weight, modulation, stored):
    normed, mixed_low, pull_back = stored
    lead, second, features = inputs.shape
    rows = lead * second
    branch = (modulation[2] * cotangent.astype(jnp.float32)).astype(jnp.bfloat16).reshape(rows, features)
    grad_proj = lax.dot_general(branch, mixed_low.reshape(rows, -1), (((0,), (0,)), ((), ())), preferred_element_type=jnp.float32)
    grad_mixed = jnp.dot(branch, proj_weight, preferred_element_type=jnp.float32).reshape(lead, second, -1)
    grad_qkv = pull_back(grad_mixed)[0].astype(jnp.bfloat16).reshape(rows, -1)
    grad_weight = lax.dot_general(normed.reshape(rows, features), grad_qkv, (((0,), (0,)), ((), ())), preferred_element_type=jnp.float32)
    grad_normed = lax.dot_general(grad_qkv, qkv_weight, (((1,), (1,)), ((), ())), preferred_element_type=jnp.float32)
    norm_pull = jax.vjp(lambda inner: modulate(inner, modulation), inputs.astype(jnp.float32))[1]
    grad_inputs = cotangent.astype(jnp.float32) + norm_pull(grad_normed.reshape(lead, second, features))[0]
    return (grad_inputs, grad_weight, grad_proj)

def reference(clip_tokens, cotangent, qkv_spatial, proj_spatial, adaln_spatial, qknorm_spatial, qkv_temporal, proj_temporal, adaln_temporal, qknorm_temporal):
    frames, patches, features = clip_tokens.shape
    block_size = 8
    clip_blocks = clip_tokens.reshape(frames // block_size, block_size, patches, features)

    def spatial_only(block_rows):
        return block_forward(block_rows, qkv_spatial, proj_spatial, adaln_spatial, qknorm_spatial, False)[0]
    middle = lax.map(spatial_only, clip_blocks).reshape(frames, patches, features)
    turned = jnp.transpose(middle, (1, 0, 2)).reshape(patches // block_size, block_size, frames, features)
    cot_turned = jnp.transpose(cotangent, (1, 0, 2)).reshape(patches // block_size, block_size, frames, features)
    empty = (jnp.zeros(qkv_temporal.shape, jnp.float32), jnp.zeros(proj_temporal.shape, jnp.float32))

    def temporal_step(totals, block_pair):
        block_rows, block_cot = block_pair
        output, stored = block_forward(block_rows, qkv_temporal, proj_temporal, adaln_temporal, qknorm_temporal, False)
        grad_rows, grad_weight, grad_proj = block_backward(block_rows, block_cot, qkv_temporal, proj_temporal, adaln_temporal, stored)
        return ((totals[0] + grad_weight, totals[1] + grad_proj), (output, grad_rows.astype(jnp.bfloat16)))
    temporal_totals, (outputs, grad_turned) = lax.scan(temporal_step, empty, (turned, cot_turned))
    result = jnp.transpose(outputs.reshape(patches, frames, features), (1, 0, 2))
    grad_middle = jnp.transpose(grad_turned.reshape(patches, frames, features), (1, 0, 2))
    grad_blocks = grad_middle.reshape(frames // block_size, block_size, patches, features)

    def spatial_step(totals, block_pair):
        block_rows, block_cot = block_pair
        stored = block_forward(block_rows, qkv_spatial, proj_spatial, adaln_spatial, qknorm_spatial, False)[1]
        grad_rows, grad_weight, grad_proj = block_backward(block_rows, block_cot, qkv_spatial, proj_spatial, adaln_spatial, stored)
        return ((totals[0] + grad_weight, totals[1] + grad_proj), grad_rows.astype(jnp.bfloat16))
    spatial_totals, grad_rows = lax.scan(spatial_step, (jnp.zeros(qkv_spatial.shape, jnp.float32), jnp.zeros(proj_spatial.shape, jnp.float32)), (clip_blocks, grad_blocks))
    grad_clip = grad_rows.reshape(frames, patches, features)
    factor = 1.0 / jnp.sqrt(jnp.float32(frames * patches))
    return (result, grad_clip, spatial_totals[0] * factor, spatial_totals[1] * factor, temporal_totals[0] * factor, temporal_totals[1] * factor)
```

```python
import functools
import math

import jax
import jax.numpy as jnp
from jax import lax
from jax.experimental import pallas as pl
from jax.experimental.pallas import tpu as pltpu
from jax.sharding import PartitionSpec as P

EPS = 1e-06
BF = jnp.bfloat16
F32 = jnp.float32
VMEM_LIMIT = 56 * 1024 * 1024
LOG2E = math.log2(math.e)


def nn(a, b):
    return lax.dot_general(a, b, (((1,), (0,)), ((), ())), preferred_element_type=F32)


def nt(a, b):
    return lax.dot_general(a, b, (((1,), (1,)), ((), ())), preferred_element_type=F32)


def tn(a, b):
    return lax.dot_general(a, b, (((0,), (0,)), ((), ())), preferred_element_type=F32)


def standardize(x):
    centre = x - jnp.mean(x, axis=-1, keepdims=True)
    rate = lax.rsqrt(jnp.mean(centre * centre, axis=-1, keepdims=True) + EPS)
    return centre * rate, rate


def modulated(x, mod_ref):
    return (standardize(x)[0] * (1.0 + mod_ref[1:2, :]) + mod_ref[0:1, :]).astype(BF)


def modulate_vjp(x, mod_ref, grad):
    unit, rate = standardize(x)
    scaled = grad * (1.0 + mod_ref[1:2, :])
    inner = jnp.mean(unit * scaled, axis=-1, keepdims=True)
    return rate * (scaled - jnp.mean(scaled, axis=-1, keepdims=True) - unit * inner)


def column(row):
    n = row.shape[1]
    same = lax.broadcasted_iota(jnp.int32, (n, n), 0) == lax.broadcasted_iota(jnp.int32, (n, n), 1)
    return jnp.sum(jnp.where(same, jnp.broadcast_to(row, (n, n)), 0.0), axis=1, keepdims=True)


def unit_rms(vectors):
    rate = lax.rsqrt(jnp.mean(vectors * vectors, axis=0, keepdims=True) + EPS)
    return vectors * rate, rate


def same_column(rows, stride):
    first = lax.broadcasted_iota(jnp.int32, (rows, rows), 0)
    second = lax.broadcasted_iota(jnp.int32, (rows, rows), 1)
    return lax.rem(first, stride) == lax.rem(second, stride)


def head_parts(qkv_ref, head, hd, width):
    at = head * hd
    return (
        qkv_ref[at : at + hd, :],
        qkv_ref[width + at : width + at + hd, :],
        qkv_ref[2 * width + at : 2 * width + at + hd, :],
    )


def head_weights(q_unit, k_unit, gq, gk, mask, hd):
    qn = (q_unit * (gq * (LOG2E / math.sqrt(hd)))).astype(BF)
    kn = (k_unit * gk).astype(BF)
    weights = jnp.exp2(tn(kn, qn))
    if mask is not None:
        weights = jnp.where(mask, weights, 0.0)
    return (weights * (1.0 / jnp.sum(weights, axis=0, keepdims=True))).astype(BF)


def head_vjp(q, k, v16, weights, grad, gq, gk, hd):
    q_unit, q_rate = unit_rms(q)
    k_unit, k_rate = unit_rms(k)
    scale = 1.0 / math.sqrt(hd)
    grad16 = grad.astype(BF)
    d_v = nt(grad16, weights)
    w32 = weights.astype(F32)
    weighted = w32 * tn(v16, grad16)
    d_s = (weighted - w32 * jnp.sum(weighted, axis=0, keepdims=True)).astype(BF)
    d_q = nn((k_unit * gk).astype(BF), d_s) * (gq * scale)
    d_k = nt((q_unit * gq).astype(BF), d_s) * (gk * scale)
    d_q = q_rate * (d_q - q_unit * jnp.mean(q_unit * d_q, axis=0, keepdims=True))
    d_k = k_rate * (d_k - k_unit * jnp.mean(k_unit * d_k, axis=0, keepdims=True))
    return d_q, d_k, d_v


def spatial_forward_kernel(
    dims, x_ref, w_ref, p_ref, mod_ref, gain_ref,
    send_ref, normed_ref, qkv_ref, att_ref, mixed_ref, mid_scr, mixed_scr,
):
    steps, heads, hd, per_device, group = dims
    step = pl.program_id(0)
    rows = x_ref.shape[1]
    width = heads * hd
    x = x_ref[0].astype(F32)
    normed = modulated(x, mod_ref)
    normed_ref[0] = normed
    qkv = qkv_ref.at[0]
    qkv[...] = nt(w_ref[...], normed)
    gq, gk = column(gain_ref[0:1, :]), column(gain_ref[1:2, :])
    for head in range(heads):
        q, k, v = head_parts(qkv, head, hd, width)
        weights = head_weights(unit_rms(q)[0], unit_rms(k)[0], gq, gk, None, hd)
        att_ref[0, head] = weights
        mixed_scr[head * hd : (head + 1) * hd, :] = nn(v.astype(BF), weights)
    mixed = mixed_scr[...].astype(BF)
    mixed_ref[0] = mixed
    mid_scr[pl.ds(pl.multiple_of(step * rows, rows), rows), :] = (
        x + mod_ref[2:3, :] * tn(mixed, p_ref[...])
    ).astype(BF)

    @pl.when(step == steps - 1)
    def _():
        out_rows, in_rows = send_ref.shape[1], mid_scr.shape[0]
        out = lax.broadcasted_iota(jnp.int32, (out_rows, in_rows), 0)
        src = lax.broadcasted_iota(jnp.int32, (out_rows, in_rows), 1)
        each = steps * group
        owner, rest = out // each, lax.rem(out, each)
        base = (rest // group) * rows + owner * per_device + lax.rem(rest, group)
        for part in range(send_ref.shape[0]):
            pick = (src == base + part * group).astype(F32).astype(BF)
            send_ref[part] = nn(pick, mid_scr[...]).astype(BF)


def cotangent_kernel(dims, cot_ref, p_ref, mod_ref, turned_ref, branch_ref, grad_ref):
    per_device, group = dims
    part = pl.program_id(0)
    out_rows, in_rows = turned_ref.shape[1], cot_ref.shape[0]
    out = lax.broadcasted_iota(jnp.int32, (out_rows, in_rows), 0)
    src = lax.broadcasted_iota(jnp.int32, (out_rows, in_rows), 1)
    base = (out // group) * per_device + lax.rem(out, group) + part * group
    turned = nn((src == base).astype(F32).astype(BF), cot_ref[...])
    turned_ref[0] = turned.astype(BF)
    branch = (mod_ref[2:3, :] * turned).astype(BF)
    branch_ref[0] = branch
    grad_ref[0] = nt(p_ref[...], branch)


def temporal_kernel(
    dims, mid_ref, turned_ref, grad_ref, w_ref, mod_ref, gain_ref,
    dmid_ref, normed_ref, dqkv_ref, mixed_ref, qkv_scr, mixed_scr, dqkv_scr,
):
    heads, hd, group = dims
    width = heads * hd
    rows = mid_ref.shape[0]
    x = mid_ref[...].astype(F32)
    normed = modulated(x, mod_ref)
    normed_ref[...] = normed
    qkv_scr[...] = nt(w_ref[...], normed)
    gq, gk = column(gain_ref[0:1, :]), column(gain_ref[1:2, :])
    mask = same_column(rows, group) if group > 1 else None
    for head in range(heads):
        q, k, v = head_parts(qkv_scr, head, hd, width)
        at = head * hd
        v16 = v.astype(BF)
        weights = head_weights(unit_rms(q)[0], unit_rms(k)[0], gq, gk, mask, hd)
        mixed_scr[at : at + hd, :] = nn(v16, weights)
        d_q, d_k, d_v = head_vjp(q, k, v16, weights, grad_ref[0, at : at + hd, :], gq, gk, hd)
        dqkv_scr[at : at + hd, :] = d_q
        dqkv_scr[width + at : width + at + hd, :] = d_k
        dqkv_scr[2 * width + at : 2 * width + at + hd, :] = d_v
    mixed_ref[...] = mixed_scr[...].astype(BF)
    dqkv = dqkv_scr[...].astype(BF)
    dqkv_ref[...] = dqkv
    grad = modulate_vjp(x, mod_ref, tn(dqkv, w_ref[...]))
    dmid_ref[...] = (turned_ref[0].astype(F32) + grad).astype(BF)


def result_kernel(dims, mid_ref, mixed_ref, p_ref, mod_ref, out_ref, scr):
    per_device, group, parts = dims
    rows = mid_ref.shape[1]
    for part in range(parts):
        scr[part * rows : (part + 1) * rows, :] = (
            mid_ref[part].astype(F32) + mod_ref[2:3, :] * tn(mixed_ref[part], p_ref[...])
        ).astype(BF)
    out_rows = out_ref.shape[0]
    out = lax.broadcasted_iota(jnp.int32, (out_rows, out_rows), 0)
    src = lax.broadcasted_iota(jnp.int32, (out_rows, out_rows), 1)
    col = lax.rem(out, per_device)
    base = (col // group) * rows + (out // per_device) * group + lax.rem(col, group)
    out_ref[...] = nn((src == base).astype(F32).astype(BF), scr[...]).astype(BF)


def weight_grad_kernel(
    dims, bit_ref, normed_ref, branch_ref, dqkv_ref, mixed_ref, first_ref, second_ref
):
    parts, heads, hd, blocks = dims
    width = heads * hd
    bit = bit_ref[0]
    qk = v = o = 0.0
    for part in range(parts):
        normed_t = normed_ref[part].astype(F32).T.astype(BF)
        branch_t = branch_ref[part].astype(F32).T.astype(BF)
        qk += nt(normed_t, dqkv_ref[part, : 2 * width, :])
        v += nt(normed_t, dqkv_ref[part, 2 * width :, :])
        o += nt(branch_t, mixed_ref[part])
    size = normed_ref.shape[2] // blocks
    for block in range(blocks):
        at = slice(block * size, (block + 1) * size)
        side = (block % 2 + bit) % 2
        first_ref[side, block // 2] = qk[at].astype(BF)
        second_ref[side, block // 2, :, :width] = v[at].astype(BF)
        second_ref[side, block // 2, :, width:] = o[at].astype(BF)


def spatial_attention_vjp_kernel(
    dims, recv0_ref, recv1_ref, qkv_ref, att_ref, p_ref, mod_ref, gain_ref,
    dmid_ref, branch_ref, dqkv_ref, grad_scr, dqkv_scr,
):
    heads, hd, steps, per_device, group = dims
    width = heads * hd
    step = pl.program_id(0)
    rows, in_rows = dmid_ref.shape[1], recv0_ref.shape[0]
    out = lax.broadcasted_iota(jnp.int32, (rows, in_rows), 0)
    src = lax.broadcasted_iota(jnp.int32, (rows, in_rows), 1)
    owner, col = out // per_device, lax.rem(out, per_device)
    base = owner * (steps * group) + step * group + lax.rem(col, group)
    base = jnp.where(src == base, col // group, -1)
    dmid = nn((base == 0).astype(F32).astype(BF), recv0_ref[...])
    dmid += nn((base == 1).astype(F32).astype(BF), recv1_ref[...])
    dmid_ref[0] = dmid.astype(BF)
    branch = (mod_ref[2:3, :] * dmid).astype(BF)
    branch_ref[0] = branch
    grad_scr[...] = nt(p_ref[...], branch)
    gq, gk = column(gain_ref[0:1, :]), column(gain_ref[1:2, :])
    for head in range(heads):
        q, k, v = head_parts(qkv_ref.at[0], head, hd, width)
        at = head * hd
        d_q, d_k, d_v = head_vjp(
            q, k, v.astype(BF), att_ref[0, head], grad_scr[at : at + hd, :], gq, gk, hd
        )
        dqkv_scr[at : at + hd, :] = d_q
        dqkv_scr[width + at : width + at + hd, :] = d_k
        dqkv_scr[2 * width + at : 2 * width + at + hd, :] = d_v
    dqkv_ref[0] = dqkv_scr[...].astype(BF)


def grad_clip_kernel(x_ref, dmid_ref, dqkv_ref, w_ref, mod_ref, out_ref):
    grad = modulate_vjp(x_ref[0].astype(F32), mod_ref, tn(dqkv_ref[0], w_ref[...]))
    out_ref[0] = (dmid_ref[0].astype(F32) + grad).astype(BF)


def params():
    return pltpu.CompilerParams(vmem_limit_bytes=VMEM_LIMIT)


def cost(flops, *arrays):
    moved = sum(math.prod(a.shape) * jnp.dtype(a.dtype).itemsize for a in arrays)
    return pl.CostEstimate(flops=int(flops), bytes_accessed=int(moved), transcendentals=0)


def whole(array):
    return pl.BlockSpec(array.shape, lambda *_, n=len(array.shape): (0,) * n)


def each(array):
    n = len(array.shape)
    return pl.BlockSpec((1,) + tuple(array.shape[1:]), lambda i, *_: (i,) + (0,) * (n - 1))


def shape(dims, kind=BF):
    return jax.ShapeDtypeStruct(tuple(dims), kind)


def call(kernel, grid, ins, in_each, outs, out_each, scratch, flops):
    return pl.pallas_call(
        kernel,
        grid=grid,
        in_specs=[each(a) if e else whole(a) for a, e in zip(ins, in_each)],
        out_specs=[each(a) if e else whole(a) for a, e in zip(outs, out_each)],
        out_shape=outs,
        scratch_shapes=scratch,
        compiler_params=params(),
        cost_estimate=cost(flops, *ins, *outs),
    )(*ins)


def weight_grads(normed, branch, dqkv, mixed, heads, hd):
    parts, rows, depth = normed.shape
    width = heads * hd
    count = lax.axis_size("wide")
    bit = (lax.axis_index("wide") % 2).astype(jnp.int32).reshape(1)
    kernel = functools.partial(weight_grad_kernel, (parts, heads, hd, count))
    out = shape((2, count // 2, depth // count, 2 * width))
    ins = (bit, normed, branch, dqkv, mixed)
    return pl.pallas_call(
        kernel,
        in_specs=[pl.BlockSpec(memory_space=pltpu.SMEM)] + [pl.BlockSpec(memory_space=pltpu.VMEM)] * 4,
        out_specs=[pl.BlockSpec(memory_space=pltpu.VMEM)] * 2,
        out_shape=[out, out],
        compiler_params=params(),
        cost_estimate=cost(2 * parts * rows * depth * 4 * width, *ins, out, out),
    )(*ins)


def exchange(value, axis, bit):
    count = lax.axis_size(axis)
    return lax.ppermute(value, axis, [(i, i ^ (1 << bit)) for i in range(count)])


def reduce_halving(pair, upward):
    total = (pair[0].astype(F32) + exchange(pair[1], "wide", 0).astype(F32)).astype(BF)
    bits = int(math.log2(lax.axis_size("wide")))
    rows, columns = total.shape[1:]
    left = list(range(bits - 1, 0, -1))
    total = total.reshape((2,) * len(left) + (rows, columns))
    me = lax.axis_index("wide")
    for bit in sorted(left, reverse=not upward):
        at = left.index(bit)
        mine = (me >> bit) & 1
        sent = lax.dynamic_index_in_dim(total, 1 - mine, at, keepdims=False)
        kept = lax.dynamic_index_in_dim(total, mine, at, keepdims=False)
        total = (kept.astype(F32) + exchange(sent, "wide", bit).astype(F32)).astype(BF)
        left.remove(bit)
    count = lax.axis_size("narrow")
    total = total.reshape(count, rows // count, columns)
    terms = lax.all_to_all(total, "narrow", split_axis=0, concat_axis=0, tiled=True)
    return jnp.sum(terms.astype(F32), axis=0)


def body(
    clip_tokens,
    cotangent,
    qkv_spatial,
    proj_spatial,
    adaln_spatial,
    qknorm_spatial,
    qkv_temporal,
    proj_temporal,
    adaln_temporal,
    qknorm_temporal,
):
    steps, patches, depth = clip_tokens.shape
    frames, per_device, _ = cotangent.shape
    hd = qknorm_spatial.shape[1]
    width = proj_spatial.shape[1]
    heads = width // hd
    axes = ("wide", "narrow")
    devices = lax.axis_size("wide") * lax.axis_size("narrow")
    parts = 2
    group = per_device // parts
    rows = frames * group
    w_s, p_s, w_t, p_t = qkv_spatial.T, proj_spatial.T, qkv_temporal.T, proj_temporal.T
    dense = 2 * depth * 3 * width
    pair = 2 * 128 * heads

    send, normed_s, qkv_s, att_s, mixed_s = call(
        functools.partial(spatial_forward_kernel, (steps, heads, hd, per_device, group)),
        (steps,),
        (clip_tokens, w_s, p_s, adaln_spatial, qknorm_spatial),
        (1, 0, 0, 0, 0),
        [
            shape((parts, devices * steps * group, depth)),
            shape((steps, patches, depth)),
            shape((steps, 3 * width, patches), F32),
            shape((steps, heads, patches, patches)),
            shape((steps, width, patches)),
        ],
        (0, 1, 1, 1, 1),
        [pltpu.VMEM((steps * patches, depth), BF), pltpu.VMEM((width, patches), F32)],
        steps * patches * (dense * 4 // 3 + 4 * pair * patches),
    )

    def turn(value):
        value = value.reshape(devices, steps * group, depth)
        value = lax.all_to_all(value, axes, split_axis=0, concat_axis=0, tiled=True)
        return value.reshape(rows, depth)

    middle = [turn(send[part]) for part in range(parts)]

    flat_cot = cotangent.reshape(frames * per_device, depth)
    turned, branch_t, dmixed_t = call(
        functools.partial(cotangent_kernel, (per_device, group)),
        (parts,),
        (flat_cot, p_t, adaln_temporal),
        (0, 0, 0),
        [shape((parts, rows, depth)), shape((parts, rows, depth)), shape((parts, width, rows), F32)],
        (1, 1, 1),
        [],
        parts * rows * (dense // 3 + 2 * depth * frames * per_device),
    )

    received, saved = [], []
    for part in range(parts):
        pick = lambda a: pl.BlockSpec((1,) + a.shape[1:], lambda *_, p=part: (p, 0, 0))
        ins = (middle[part], turned, dmixed_t, w_t, adaln_temporal, qknorm_temporal)
        outs = [
            shape((rows, depth)), shape((rows, depth)),
            shape((3 * width, rows)), shape((width, rows)),
        ]
        dmid, *keep = pl.pallas_call(
            functools.partial(temporal_kernel, (heads, hd, group)),
            grid=(1,),
            in_specs=[whole(ins[0]), pick(turned), pick(dmixed_t)] + [whole(a) for a in ins[3:]],
            out_specs=[whole(a) for a in outs],
            out_shape=outs,
            scratch_shapes=[
                pltpu.VMEM((3 * width, rows), F32),
                pltpu.VMEM((width, rows), F32),
                pltpu.VMEM((3 * width, rows), F32),
            ],
            compiler_params=params(),
            cost_estimate=cost(rows * (2 * dense + 14 * pair * rows), *ins, *outs),
        )(*ins)
        received.append(turn(dmid))
        saved.append(keep)

    normed_t, dqkv_t, mixed_t = (jnp.stack(list(a)) for a in zip(*saved))
    grads_t = weight_grads(normed_t, branch_t, dqkv_t, mixed_t, heads, hd)
    (result,) = call(
        functools.partial(result_kernel, (per_device, group, parts)),
        (1,),
        (jnp.stack(middle), mixed_t, p_t, adaln_temporal),
        (0, 0, 0, 0),
        [shape((frames * per_device, depth))],
        (0,),
        [pltpu.VMEM((parts * rows, depth), BF)],
        parts * rows * (dense // 3 + 2 * depth * rows * parts),
    )

    dmid_s, branch_s, dqkv_s = call(
        functools.partial(spatial_attention_vjp_kernel, (heads, hd, steps, per_device, group)),
        (steps,),
        (*received, qkv_s, att_s, p_s, adaln_spatial, qknorm_spatial),
        (0, 0, 1, 1, 0, 0, 0),
        [
            shape((steps, patches, depth)),
            shape((steps, patches, depth)),
            shape((steps, 3 * width, patches)),
        ],
        (1, 1, 1),
        [pltpu.VMEM((width, patches), F32), pltpu.VMEM((3 * width, patches), F32)],
        steps * patches * (dense // 3 + 10 * pair * patches),
    )
    grads_s = weight_grads(normed_s, branch_s, dqkv_s, mixed_s, heads, hd)
    (grad_clip,) = call(
        grad_clip_kernel,
        (steps,),
        (clip_tokens, dmid_s, dqkv_s, w_s, adaln_spatial),
        (1, 1, 1, 0, 0),
        [shape((steps, patches, depth))],
        (1,),
        [],
        steps * patches * dense,
    )

    factor = 1.0 / math.sqrt(frames * patches)
    outs = []
    for first, second in (grads_s, grads_t):
        first = reduce_halving(first, True) * factor
        second = reduce_halving(second, False) * factor
        outs.append(jnp.concatenate([first, second[:, :width]], axis=1))
        outs.append(second[:, width:])
    return (result.reshape(frames, per_device, depth), grad_clip, *outs)


def solution(mesh):
    tokens = P(("wide", "narrow"), None, None)
    columns = P(None, ("wide", "narrow"), None)
    own = P(("wide", "narrow"), None)
    return jax.shard_map(
        body,
        mesh=mesh,
        in_specs=(tokens, columns) + (P(),) * 8,
        out_specs=(columns, tokens, own, own, own, own),
        check_vma=False,
    )
```

```python
import functools
import math

import jax
import jax.numpy as jnp
from jax import lax
from jax.experimental import pallas as pl
from jax.experimental.pallas import tpu as pltpu
from jax.sharding import PartitionSpec as P

EPS = 1e-06
BF = jnp.bfloat16
F32 = jnp.float32
VMEM_LIMIT = 56 * 1024 * 1024
LOG2E = math.log2(math.e)


def nn(a, b):
    return lax.dot_general(a, b, (((1,), (0,)), ((), ())), preferred_element_type=F32)


def nt(a, b):
    return lax.dot_general(a, b, (((1,), (1,)), ((), ())), preferred_element_type=F32)


def tn(a, b):
    return lax.dot_general(a, b, (((0,), (0,)), ((), ())), preferred_element_type=F32)


def standardize(x):
    centre = x - jnp.mean(x, axis=-1, keepdims=True)
    rate = lax.rsqrt(jnp.mean(centre * centre, axis=-1, keepdims=True) + EPS)
    return centre * rate, rate


def modulated(x, mod_ref):
    return (standardize(x)[0] * (1.0 + mod_ref[1:2, :]) + mod_ref[0:1, :]).astype(BF)


def modulate_vjp(x, mod_ref, grad):
    unit, rate = standardize(x)
    scaled = grad * (1.0 + mod_ref[1:2, :])
    inner = jnp.mean(unit * scaled, axis=-1, keepdims=True)
    return rate * (scaled - jnp.mean(scaled, axis=-1, keepdims=True) - unit * inner)


def column(row):
    n = row.shape[1]
    same = lax.broadcasted_iota(jnp.int32, (n, n), 0) == lax.broadcasted_iota(jnp.int32, (n, n), 1)
    return jnp.sum(jnp.where(same, jnp.broadcast_to(row, (n, n)), 0.0), axis=1, keepdims=True)


def unit_rms(vectors):
    rate = lax.rsqrt(jnp.mean(vectors * vectors, axis=0, keepdims=True) + EPS)
    return vectors * rate, rate


def same_column(rows, stride):
    first = lax.broadcasted_iota(jnp.int32, (rows, rows), 0)
    second = lax.broadcasted_iota(jnp.int32, (rows, rows), 1)
    return lax.rem(first, stride) == lax.rem(second, stride)


def head_parts(qkv_ref, head, hd, width):
    at = head * hd
    return (
        qkv_ref[at : at + hd, :],
        qkv_ref[width + at : width + at + hd, :],
        qkv_ref[2 * width + at : 2 * width + at + hd, :],
    )


def head_weights(q_unit, k_unit, gq, gk, mask, hd):
    qn = (q_unit * (gq * (LOG2E / math.sqrt(hd)))).astype(BF)
    kn = (k_unit * gk).astype(BF)
    weights = jnp.exp2(tn(kn, qn))
    if mask is not None:
        weights = jnp.where(mask, weights, 0.0)
    return (weights * (1.0 / jnp.sum(weights, axis=0, keepdims=True))).astype(BF)


def score_vjp(q, k, v16, weights, grad16, gq, gk, hd):
    q_unit, q_rate = unit_rms(q)
    k_unit, k_rate = unit_rms(k)
    scale = 1.0 / math.sqrt(hd)
    w32 = weights.astype(F32)
    weighted = w32 * tn(v16, grad16)
    d_s = (weighted - w32 * jnp.sum(weighted, axis=0, keepdims=True)).astype(BF)
    d_q = nn((k_unit * gk).astype(BF), d_s) * (gq * scale)
    d_k = nt((q_unit * gq).astype(BF), d_s) * (gk * scale)
    d_q = q_rate * (d_q - q_unit * jnp.mean(q_unit * d_q, axis=0, keepdims=True))
    d_k = k_rate * (d_k - k_unit * jnp.mean(k_unit * d_k, axis=0, keepdims=True))
    return d_q, d_k


def arrange(tr_ref, lhs_ref, me, count):
    size = lhs_ref.shape[0] // count
    for slot in range(count):
        place = (slot % (count // 2)) * 2 + slot // (count // 2)
        start = pl.multiple_of(jnp.bitwise_xor(me, place) * size, 8)
        lhs_ref[slot * size : (slot + 1) * size, :] = tr_ref[pl.ds(start, size), :].astype(BF)


def put_halves(value, keep_ref, send_ref, columns):
    half, size = keep_ref.shape[0], keep_ref.shape[1]
    for slot in range(half):
        keep_ref[slot, :, columns] = value[slot * size : (slot + 1) * size].astype(BF)
        send_ref[slot, :, columns] = value[(half + slot) * size : (half + slot + 1) * size].astype(BF)


def pick_group(dims, part, mid_ref, send_ref):
    steps, per_device, group = dims
    out_rows, in_rows = send_ref.shape[0], mid_ref.shape[0]
    out = lax.broadcasted_iota(jnp.int32, (out_rows, in_rows), 0)
    src = lax.broadcasted_iota(jnp.int32, (out_rows, in_rows), 1)
    owner, rest = out // (steps * group), lax.rem(out, steps * group)
    base = (rest // group) * (in_rows // steps) + owner * per_device + lax.rem(rest, group)
    pick = (src == base + part * group).astype(F32).astype(BF)
    send_ref[...] = nn(pick, mid_ref[...]).astype(BF)


def spatial_forward_kernel(
    dims, x_ref, w_ref, p_ref, mod_ref, gain_ref,
    mid_ref, send_ref, normed_ref, qkv_ref, att_ref, mixed_ref, mixed_scr,
):
    steps, heads, hd, per_device, group = dims
    step = pl.program_id(0)
    rows = x_ref.shape[1]
    width = heads * hd
    x = x_ref[0].astype(F32)
    normed = modulated(x, mod_ref)
    normed_ref[0] = normed
    qkv = qkv_ref.at[0]
    qkv[...] = nt(w_ref[...], normed)
    gq, gk = column(gain_ref[0:1, :]), column(gain_ref[1:2, :])
    for head in range(heads):
        q, k, v = head_parts(qkv, head, hd, width)
        weights = head_weights(unit_rms(q)[0], unit_rms(k)[0], gq, gk, None, hd)
        att_ref[0, head] = weights
        mixed_scr[head * hd : (head + 1) * hd, :] = nn(v.astype(BF), weights)
    mixed = mixed_scr[...].astype(BF)
    mixed_ref[...] = mixed
    mid_ref[pl.ds(pl.multiple_of(step * rows, rows), rows), :] = (
        x + mod_ref[2:3, :] * tn(mixed, p_ref[...])
    ).astype(BF)

    @pl.when(step == steps - 1)
    def _():
        pick_group((steps, per_device, group), 0, mid_ref, send_ref)


def between_kernel(
    dims, me_ref, mid_ref, normed_ref, cot_ref, p_ref, mod_ref,
    send_ref, lhs_ref, turned_ref, branch_ref, grad_ref, tr_scr,
):
    steps, per_device, group, count = dims
    pick_group((steps, per_device, group), 1, mid_ref, send_ref)
    out_rows, in_rows = turned_ref.shape[1], cot_ref.shape[0]
    out = lax.broadcasted_iota(jnp.int32, (out_rows, in_rows), 0)
    src = lax.broadcasted_iota(jnp.int32, (out_rows, in_rows), 1)
    base = (out // group) * per_device + lax.rem(out, group)
    for part in range(turned_ref.shape[0]):
        turned = nn((src == base + part * group).astype(F32).astype(BF), cot_ref[...])
        turned_ref[part] = turned.astype(BF)
        branch = (mod_ref[2:3, :] * turned).astype(BF)
        branch_ref[part] = branch
        grad_ref[part] = nt(p_ref[...], branch)
    rows = normed_ref.shape[1]
    for step in range(steps):
        tr_scr[:, step * rows : (step + 1) * rows] = normed_ref[step].astype(F32).T
    arrange(tr_scr, lhs_ref, me_ref[0], count)


def temporal_kernel(
    dims, part, mid_ref, turned_ref, grad_ref, w_ref, mod_ref, gain_ref,
    dmid_ref, normed_ref, dqkv_ref, mixed_ref, qkv_scr, mixed_scr, dqkv_scr,
):
    heads, hd, group = dims
    width = heads * hd
    rows = mid_ref.shape[0]
    x = mid_ref[...].astype(F32)
    normed = modulated(x, mod_ref)
    normed_ref[...] = normed
    qkv_scr[...] = nt(w_ref[...], normed)
    gq, gk = column(gain_ref[0:1, :]), column(gain_ref[1:2, :])
    mask = same_column(rows, group) if group > 1 else None
    for head in range(heads):
        q, k, v = head_parts(qkv_scr, head, hd, width)
        at = head * hd
        v16 = v.astype(BF)
        weights = head_weights(unit_rms(q)[0], unit_rms(k)[0], gq, gk, mask, hd)
        mixed_scr[at : at + hd, :] = nn(v16, weights)
        grad16 = grad_ref[0, at : at + hd, :].astype(BF)
        d_q, d_k = score_vjp(q, k, v16, weights, grad16, gq, gk, hd)
        dqkv_scr[at : at + hd, :] = d_q
        dqkv_scr[width + at : width + at + hd, :] = d_k
        dqkv_scr[2 * width + at : 2 * width + at + hd, :] = nt(grad16, weights)
    mixed_ref[...] = mixed_scr[...].astype(BF)
    dqkv = dqkv_scr[...].astype(BF)
    dqkv_ref[...] = dqkv
    grad = modulate_vjp(x, mod_ref, tn(dqkv, w_ref[...]))
    dmid_ref[...] = (turned_ref[0].astype(F32) + grad).astype(BF)


def temporal_grad_kernel(
    dims, me_ref, normed0_ref, normed1_ref, dqkv0_ref, dqkv1_ref, mixed0_ref, mixed1_ref,
    branch_ref, after_ref, keep_a_ref, send_a_ref, keep_b_ref, send_b_ref,
    tr_scr, lhs_scr, dqkv_scr, mixed_scr,
):
    width, count = dims
    rows = normed0_ref.shape[0]
    for part, (normed, dqkv, mixed) in enumerate(
        ((normed0_ref, dqkv0_ref, mixed0_ref), (normed1_ref, dqkv1_ref, mixed1_ref))
    ):
        at = slice(part * rows, (part + 1) * rows)
        tr_scr[:, at] = normed[...].astype(F32).T
        dqkv_scr[:, at] = dqkv[...]
        mixed_scr[:, at] = mixed[...]
    arrange(tr_scr, lhs_scr, me_ref[0], count)
    put_halves(nt(lhs_scr[...], dqkv_scr[: 2 * width, :]), keep_a_ref, send_a_ref, slice(None))
    put_halves(nt(lhs_scr[...], dqkv_scr[2 * width :, :]), keep_b_ref, send_b_ref, slice(0, width))
    for part in range(2):
        tr_scr[:, part * rows : (part + 1) * rows] = branch_ref[part].astype(F32).T
    arrange(tr_scr, lhs_scr, me_ref[0], count)
    put_halves(nt(lhs_scr[...], mixed_scr[...]), keep_b_ref, send_b_ref, slice(width, 2 * width))


def result_kernel(
    dims, mid0_ref, mid1_ref, mixed0_ref, mixed1_ref, p_ref, mod_ref, after_ref, out_ref, scr
):
    per_device, group = dims
    rows = mid0_ref.shape[0]
    for part, (mid, mixed) in enumerate(((mid0_ref, mixed0_ref), (mid1_ref, mixed1_ref))):
        scr[part * rows : (part + 1) * rows, :] = (
            mid[...].astype(F32) + mod_ref[2:3, :] * tn(mixed[...], p_ref[...])
        ).astype(BF)
    out_rows = out_ref.shape[0]
    out = lax.broadcasted_iota(jnp.int32, (out_rows, out_rows), 0)
    src = lax.broadcasted_iota(jnp.int32, (out_rows, out_rows), 1)
    col = lax.rem(out, per_device)
    base = (col // group) * rows + (out // per_device) * group + lax.rem(col, group)
    out_ref[...] = nn((src == base).astype(F32).astype(BF), scr[...]).astype(BF)


def spatial_value_kernel(
    dims, me_ref, recv0_ref, recv1_ref, att_ref, p_ref, mod_ref, lhs_ref, mixed_ref,
    after0_ref, after1_ref,
    dmid_ref, grad_ref, dv_ref, keep_ref, send_ref,
    grad_scr, dv_scr, dv_all, tr_scr, lhs_scr,
):
    heads, hd, steps, per_device, group, count = dims
    width = heads * hd
    step = pl.program_id(0)
    rows, in_rows = dmid_ref.shape[1], recv0_ref.shape[0]
    out = lax.broadcasted_iota(jnp.int32, (rows, in_rows), 0)
    src = lax.broadcasted_iota(jnp.int32, (rows, in_rows), 1)
    owner, col = out // per_device, lax.rem(out, per_device)
    base = owner * (steps * group) + step * group + lax.rem(col, group)
    part = jnp.where(src == base, col // group, -1)
    dmid = nn((part == 0).astype(F32).astype(BF), recv0_ref[...])
    dmid += nn((part == 1).astype(F32).astype(BF), recv1_ref[...])
    dmid_ref[0] = dmid.astype(BF)
    branch = (mod_ref[2:3, :] * dmid).astype(BF)
    here = pl.ds(pl.multiple_of(step * rows, rows), rows)
    tr_scr[:, here] = branch.astype(F32).T
    grad_scr[...] = nt(p_ref[...], branch)
    grad_ref[0] = grad_scr[...].astype(BF)
    for head in range(heads):
        at = slice(head * hd, (head + 1) * hd)
        dv_scr[at, :] = nt(grad_scr[at, :].astype(BF), att_ref[0, head])
    d_v = dv_scr[...].astype(BF)
    dv_ref[...] = d_v
    dv_all[:, here] = d_v

    @pl.when(step == steps - 1)
    def _():
        put_halves(nt(lhs_ref[...], dv_all[...]), keep_ref, send_ref, slice(0, width))
        arrange(tr_scr, lhs_scr, me_ref[0], count)
        put_halves(nt(lhs_scr[...], mixed_ref[...]), keep_ref, send_ref, slice(width, 2 * width))


def spatial_score_kernel(
    dims, qkv_ref, att_ref, grad_ref, gain_ref, lhs_ref, after0_ref, after1_ref,
    dqk_ref, keep_ref, send_ref, dqk_scr, dqk_all,
):
    heads, hd, steps = dims
    width = heads * hd
    step = pl.program_id(0)
    rows = qkv_ref.shape[2]
    gq, gk = column(gain_ref[0:1, :]), column(gain_ref[1:2, :])
    for head in range(heads):
        q, k, v = head_parts(qkv_ref.at[0], head, hd, width)
        at = head * hd
        grad16 = grad_ref[0, at : at + hd, :]
        d_q, d_k = score_vjp(q, k, v.astype(BF), att_ref[0, head], grad16, gq, gk, hd)
        dqk_scr[at : at + hd, :] = d_q
        dqk_scr[width + at : width + at + hd, :] = d_k
    dqk = dqk_scr[...].astype(BF)
    dqk_ref[...] = dqk
    dqk_all[:, pl.ds(pl.multiple_of(step * rows, rows), rows)] = dqk

    @pl.when(step == steps - 1)
    def _():
        put_halves(nt(lhs_ref[...], dqk_all[...]), keep_ref, send_ref, slice(None))


def grad_clip_kernel(x_ref, dmid_ref, dqk_ref, dv_ref, w_ref, mod_ref, after0_ref, out_ref):
    cut = dqk_ref.shape[0]
    grad = tn(dqk_ref[...], w_ref[:cut, :]) + tn(dv_ref[...], w_ref[cut:, :])
    grad = modulate_vjp(x_ref[0].astype(F32), mod_ref, grad)
    out_ref[0] = (dmid_ref[0].astype(F32) + grad).astype(BF)


def shape(dims, kind=BF):
    return jax.ShapeDtypeStruct(tuple(dims), kind)


def whole(array):
    return pl.BlockSpec(array.shape, lambda *_, n=len(array.shape): (0,) * n)


def each(array):
    n = len(array.shape)
    return pl.BlockSpec((1,) + tuple(array.shape[1:]), lambda i, *_: (i,) + (0,) * (n - 1))


def one(part):
    def spec(array):
        n = len(array.shape)
        return pl.BlockSpec((1,) + tuple(array.shape[1:]), lambda *_: (part,) + (0,) * (n - 1))

    return spec


def lanes(steps):
    def spec(array):
        return pl.BlockSpec((array.shape[0], array.shape[1] // steps), lambda i, *_: (0, i))

    return spec


def scalar(array):
    return pl.BlockSpec(memory_space=pltpu.SMEM)


def unused(array):
    return pl.BlockSpec(memory_space=pl.ANY)


def call(kernel, grid, ins, outs, scratch, flops):
    arrays = [a for a, _ in ins]
    moved = [a for a, s in ins if s is not unused] + [a for a, _ in outs]
    size = sum(math.prod(a.shape) * jnp.dtype(a.dtype).itemsize for a in moved)
    return pl.pallas_call(
        kernel,
        grid=grid,
        in_specs=[s(a) for a, s in ins],
        out_specs=[s(a) for a, s in outs],
        out_shape=[a for a, _ in outs],
        scratch_shapes=[pltpu.VMEM(d, k) for d, k in scratch],
        compiler_params=pltpu.CompilerParams(vmem_limit_bytes=VMEM_LIMIT),
        cost_estimate=pl.CostEstimate(flops=int(flops), bytes_accessed=int(size), transcendentals=0),
    )(*arrays)


def exchange(value, axis, bit):
    count = lax.axis_size(axis)
    return lax.ppermute(value, axis, [(i, i ^ (1 << bit)) for i in range(count)])


def add(first, second):
    return (first.astype(F32) + second.astype(F32)).astype(BF)


def take(value, at, index):
    return lax.index_in_dim(value, index, at, keepdims=False)


def wide_bits():
    return int(math.log2(lax.axis_size("wide")))


def halve(first, second, left, bit):
    at = left.index(bit)
    got = exchange(add(take(first, at, 1), take(second, at, 1)), "wide", bit)
    return add(take(first, at, 0), take(second, at, 0)), got, [b for b in left if b != bit]


def cut_bits(value):
    bits = wide_bits() - 1
    return value.reshape((2,) * bits + value.shape[1:])


def narrow_sum(total):
    count = lax.axis_size("narrow")
    total = total.reshape(count, total.shape[0] // count, total.shape[1])
    terms = lax.all_to_all(total, "narrow", split_axis=0, concat_axis=0, tiled=True)
    return jnp.sum(terms.astype(F32), axis=0)


class Halving:
    def __init__(self, keep, send, ranges):
        first, second = cut_bits(keep), cut_bits(exchange(send, "wide", 0))
        left = list(range(wide_bits() - 1, 0, -1))
        self.state = [
            (first[..., at], second[..., at], left, order) for at, order in ranges
        ]

    def step(self):
        self.state = [
            halve(a, b, left, order[0]) + (order[1:],) if order else (a, b, left, order)
            for a, b, left, order in self.state
        ]

    def pending(self):
        return bool(self.state[0][3])

    def sums(self):
        return [add(a, b) for a, b, _, _ in self.state]


def body(
    clip_tokens,
    cotangent,
    qkv_spatial,
    proj_spatial,
    adaln_spatial,
    qknorm_spatial,
    qkv_temporal,
    proj_temporal,
    adaln_temporal,
    qknorm_temporal,
):
    steps, patches, depth = clip_tokens.shape
    frames, per_device, _ = cotangent.shape
    hd = qknorm_spatial.shape[1]
    width = proj_spatial.shape[1]
    heads = width // hd
    axes = ("wide", "narrow")
    count = lax.axis_size("wide")
    devices = count * lax.axis_size("narrow")
    parts = 2
    group = per_device // parts
    rows = frames * group
    tokens = steps * patches
    w_s, p_s, w_t, p_t = qkv_spatial.T, proj_spatial.T, qkv_temporal.T, proj_temporal.T
    dense = 2 * depth * 3 * width
    pair = 2 * 256 * heads
    me = lax.axis_index("wide").astype(jnp.int32).reshape(1)
    half = shape((count // 2, depth // count, 2 * width))
    lane = lanes(steps)

    middle, send0, normed_s, qkv_s, att_s, mixed_s = call(
        functools.partial(spatial_forward_kernel, (steps, heads, hd, per_device, group)),
        (steps,),
        [(clip_tokens, each), (w_s, whole), (p_s, whole), (adaln_spatial, whole),
         (qknorm_spatial, whole)],
        [(shape((tokens, depth)), whole), (shape((rows, depth)), whole),
         (shape((steps, patches, depth)), each),
         (shape((steps, 3 * width, patches), F32), each),
         (shape((steps, heads, patches, patches)), each), (shape((width, tokens)), lane)],
        [((width, patches), F32)],
        tokens * (dense * 4 // 3 + 2 * pair * patches),
    )

    def turn(value):
        value = value.reshape(devices, steps * group, depth)
        value = lax.all_to_all(value, axes, split_axis=0, concat_axis=0, tiled=True)
        return value.reshape(rows, depth)

    flat_cot = cotangent.reshape(frames * per_device, depth)
    send1, lhs_s, turned, branch_t, dmixed_t = call(
        functools.partial(between_kernel, (steps, per_device, group, count)),
        (1,),
        [(me, scalar), (middle, whole), (normed_s, whole), (flat_cot, whole), (p_t, whole),
         (adaln_temporal, whole)],
        [(shape((rows, depth)), whole), (shape((depth, tokens)), whole),
         (shape((parts, rows, depth)), whole), (shape((parts, rows, depth)), whole),
         (shape((parts, width, rows), F32), whole)],
        [((depth, tokens), F32)],
        parts * rows * (dense // 3 + 4 * depth * tokens),
    )
    middles = [turn(send0), turn(send1)]

    received, saved = [], []
    for part in range(parts):
        dmid, *keep = call(
            functools.partial(temporal_kernel, (heads, hd, group), part),
            (1,),
            [(middles[part], whole), (turned, one(part)), (dmixed_t, one(part)), (w_t, whole),
             (adaln_temporal, whole), (qknorm_temporal, whole)],
            [(shape((rows, depth)), whole), (shape((rows, depth)), whole),
             (shape((3 * width, rows)), whole), (shape((width, rows)), whole)],
            [((3 * width, rows), F32), ((width, rows), F32), ((3 * width, rows), F32)],
            rows * (2 * dense + 7 * pair * rows),
        )
        received.append(turn(dmid))
        saved.append(keep)
    (normed0, dqkv0, mixed0), (normed1, dqkv1, mixed1) = saved

    keep_a, send_a, keep_b, send_b = call(
        functools.partial(temporal_grad_kernel, (width, count)),
        (1,),
        [(me, scalar), (normed0, whole), (normed1, whole), (dqkv0, whole), (dqkv1, whole),
         (mixed0, whole), (mixed1, whole), (branch_t, whole), (received[0], unused)],
        [(half, whole)] * 4,
        [((depth, parts * rows), F32), ((depth, parts * rows), BF),
         ((3 * width, parts * rows), BF), ((width, parts * rows), BF)],
        parts * rows * dense * 4 // 3,
    )
    every = slice(None)
    upward = list(range(1, wide_bits()))
    downward = upward[::-1]
    sum_ta = Halving(keep_a, send_a, [(every, upward)])
    sum_tb = Halving(keep_b, send_b, [(every, downward)])
    (result,) = call(
        functools.partial(result_kernel, (per_device, group)),
        (1,),
        [(middles[0], whole), (middles[1], whole), (mixed0, whole), (mixed1, whole), (p_t, whole),
         (adaln_temporal, whole), (send_a, unused)],
        [(shape((frames * per_device, depth)), whole)],
        [((parts * rows, depth), BF)],
        parts * rows * (dense // 3 + 2 * depth * rows * parts),
    )

    sum_ta.step()
    sum_tb.step()
    dmid_s, dmixed_s, dv_s, keep_b, send_b = call(
        functools.partial(spatial_value_kernel, (heads, hd, steps, per_device, group, count)),
        (steps,),
        [(me, scalar), (received[0], whole), (received[1], whole), (att_s, each), (p_s, whole),
         (adaln_spatial, whole), (lhs_s, whole), (mixed_s, whole),
         (sum_ta.state[0][0], unused), (sum_tb.state[0][0], unused)],
        [(shape((steps, patches, depth)), each), (shape((steps, width, patches)), each),
         (shape((width, tokens)), lane), (half, whole), (half, whole)],
        [((width, patches), F32), ((width, patches), F32), ((width, tokens), BF),
         ((depth, tokens), F32), ((depth, tokens), BF)],
        tokens * (dense + pair * patches),
    )
    cut = 128 * -(-2 * width // 256)
    ranges = [(slice(0, cut), upward), (slice(cut, None), downward)]
    sum_sb = Halving(keep_b, send_b, ranges)
    while sum_ta.pending():
        sum_ta.step()
        sum_tb.step()
    dqk_s, keep_a, send_a = call(
        functools.partial(spatial_score_kernel, (heads, hd, steps)),
        (steps,),
        [(qkv_s, each), (att_s, each), (dmixed_s, each), (qknorm_spatial, whole), (lhs_s, whole),
         (sum_ta.state[0][0], unused), (sum_tb.state[0][0], unused)],
        [(shape((2 * width, tokens)), lane), (half, whole), (half, whole)],
        [((2 * width, patches), F32), ((2 * width, tokens), BF)],
        tokens * (dense * 2 // 3 + 4 * pair * patches),
    )
    sum_sa = Halving(keep_a, send_a, ranges)
    sum_sb.step()
    (grad_clip,) = call(
        grad_clip_kernel,
        (steps,),
        [(clip_tokens, each), (dmid_s, each), (dqk_s, lane), (dv_s, lane), (w_s, whole),
         (adaln_spatial, whole), (sum_sb.state[0][0], unused)],
        [(shape((steps, patches, depth)), each)],
        [],
        tokens * dense,
    )
    while sum_sb.pending():
        sum_sb.step()
    while sum_sa.pending():
        sum_sa.step()

    factor = 1.0 / math.sqrt(frames * patches)
    sums = []
    for piece in ([sum_ta, sum_tb], [sum_sb], [sum_sa]):
        sums.append(narrow_sum(jnp.concatenate([a for s in piece for a in s.sums()], axis=1)) * factor)
    both_t, second, first = sums
    return (
        result.reshape(frames, per_device, depth),
        grad_clip,
        jnp.concatenate([first, second[:, :width]], axis=1),
        second[:, width:],
        both_t[:, : 3 * width],
        both_t[:, 3 * width :],
    )


def solution(mesh):
    tokens = P(("wide", "narrow"), None, None)
    columns = P(None, ("wide", "narrow"), None)
    own = P(("wide", "narrow"), None)
    return jax.shard_map(
        body,
        mesh=mesh,
        in_specs=(tokens, columns) + (P(),) * 8,
        out_specs=(columns, tokens, own, own, own, own),
        check_vma=False,
    )
```

```python
import functools
import math

import jax
import jax.numpy as jnp
from jax import lax
from jax.experimental import pallas as pl
from jax.experimental.pallas import tpu as pltpu
from jax.sharding import PartitionSpec as P

EPS = 1e-06
BF = jnp.bfloat16
F32 = jnp.float32
VMEM_LIMIT = 32 * 1024 * 1024
FLOPS_PER_MICRO = 1.15e9
LOG2E = math.log2(math.e)


def nn(a, b):
    return lax.dot_general(a, b, (((1,), (0,)), ((), ())), preferred_element_type=F32)


def nt(a, b):
    return lax.dot_general(a, b, (((1,), (1,)), ((), ())), preferred_element_type=F32)


def tn(a, b):
    return lax.dot_general(a, b, (((0,), (0,)), ((), ())), preferred_element_type=F32)


def standardize(x):
    centre = x - jnp.mean(x, axis=-1, keepdims=True)
    rate = lax.rsqrt(jnp.mean(centre * centre, axis=-1, keepdims=True) + EPS)
    return centre * rate, rate


def modulated(x, mod_ref):
    return (standardize(x)[0] * (1.0 + mod_ref[1:2, :]) + mod_ref[0:1, :]).astype(BF)


def modulate_vjp(x, mod_ref, grad):
    unit, rate = standardize(x)
    scaled = grad * (1.0 + mod_ref[1:2, :])
    inner = jnp.mean(unit * scaled, axis=-1, keepdims=True)
    return rate * (scaled - jnp.mean(scaled, axis=-1, keepdims=True) - unit * inner)


def column(row):
    n = row.shape[1]
    same = lax.broadcasted_iota(jnp.int32, (n, n), 0) == lax.broadcasted_iota(jnp.int32, (n, n), 1)
    return jnp.sum(jnp.where(same, jnp.broadcast_to(row, (n, n)), 0.0), axis=1, keepdims=True)


def unit_rms(vectors):
    rate = lax.rsqrt(jnp.mean(vectors * vectors, axis=0, keepdims=True) + EPS)
    return vectors * rate, rate


def same_column(rows, stride):
    first = lax.broadcasted_iota(jnp.int32, (rows, rows), 0)
    second = lax.broadcasted_iota(jnp.int32, (rows, rows), 1)
    return lax.rem(first, stride) == lax.rem(second, stride)


def head_parts(qkv_ref, head, hd, width):
    at = head * hd
    return (
        qkv_ref[at : at + hd, :],
        qkv_ref[width + at : width + at + hd, :],
        qkv_ref[2 * width + at : 2 * width + at + hd, :],
    )


def head_weights(q_unit, k_unit, gq, gk, mask, hd):
    qn = (q_unit * (gq * (LOG2E / math.sqrt(hd)))).astype(BF)
    kn = (k_unit * gk).astype(BF)
    weights = jnp.exp2(tn(kn, qn))
    if mask is not None:
        weights = jnp.where(mask, weights, 0.0)
    return (weights * (1.0 / jnp.sum(weights, axis=0, keepdims=True))).astype(BF)


def score_vjp(q, k, v16, weights, grad16, gq, gk, hd):
    q_unit, q_rate = unit_rms(q)
    k_unit, k_rate = unit_rms(k)
    scale = 1.0 / math.sqrt(hd)
    w32 = weights.astype(F32)
    weighted = w32 * tn(v16, grad16)
    d_s = (weighted - w32 * jnp.sum(weighted, axis=0, keepdims=True)).astype(BF)
    d_q = nn((k_unit * gk).astype(BF), d_s) * (gq * scale)
    d_k = nt((q_unit * gq).astype(BF), d_s) * (gk * scale)
    d_q = q_rate * (d_q - q_unit * jnp.mean(q_unit * d_q, axis=0, keepdims=True))
    d_k = k_rate * (d_k - k_unit * jnp.mean(k_unit * d_k, axis=0, keepdims=True))
    return d_q, d_k


def arrange(tr_ref, lhs_ref, me, count):
    size = lhs_ref.shape[0] // count
    for slot in range(count):
        place = (slot % (count // 2)) * 2 + slot // (count // 2)
        start = pl.multiple_of(jnp.bitwise_xor(me, place) * size, 8)
        lhs_ref[slot * size : (slot + 1) * size, :] = tr_ref[pl.ds(start, size), :].astype(BF)


def put_halves(value, keep_ref, send_ref, columns):
    half, size = keep_ref.shape[0], keep_ref.shape[1]
    for slot in range(half):
        keep_ref[slot, :, columns] = value[slot * size : (slot + 1) * size].astype(BF)
        send_ref[slot, :, columns] = value[(half + slot) * size : (half + slot + 1) * size].astype(BF)


def pick_group(dims, part, mid_ref, send_ref):
    steps, per_device, group = dims
    out_rows, in_rows = send_ref.shape[0], mid_ref.shape[0]
    out = lax.broadcasted_iota(jnp.int32, (out_rows, in_rows), 0)
    src = lax.broadcasted_iota(jnp.int32, (out_rows, in_rows), 1)
    owner, rest = out // (steps * group), lax.rem(out, steps * group)
    base = (rest // group) * (in_rows // steps) + owner * per_device + lax.rem(rest, group)
    pick = (src == base + part * group).astype(F32).astype(BF)
    send_ref[...] = nn(pick, mid_ref[...]).astype(BF)


def spatial_forward_kernel(
    dims, x_ref, w_ref, p_ref, mod_ref, gain_ref,
    mid_ref, send_ref, normed_ref, qkv_ref, att_ref, mixed_ref, mixed_scr,
):
    steps, heads, hd, per_device, group = dims
    step = pl.program_id(0)
    rows = x_ref.shape[1]
    width = heads * hd
    x = x_ref[0].astype(F32)
    normed = modulated(x, mod_ref)
    normed_ref[0] = normed
    qkv = qkv_ref.at[0]
    qkv[...] = nt(w_ref[...], normed)
    gq, gk = column(gain_ref[0:1, :]), column(gain_ref[1:2, :])
    for head in range(heads):
        q, k, v = head_parts(qkv, head, hd, width)
        weights = head_weights(unit_rms(q)[0], unit_rms(k)[0], gq, gk, None, hd)
        att_ref[0, head] = weights
        mixed_scr[head * hd : (head + 1) * hd, :] = nn(v.astype(BF), weights)
    mixed = mixed_scr[...].astype(BF)
    mixed_ref[...] = mixed
    mid_ref[pl.ds(pl.multiple_of(step * rows, rows), rows), :] = (
        x + mod_ref[2:3, :] * tn(mixed, p_ref[...])
    ).astype(BF)

    @pl.when(step == steps - 1)
    def _():
        pick_group((steps, per_device, group), 0, mid_ref, send_ref)


def between_kernel(
    dims, me_ref, mid_ref, normed_ref, cot_ref, p_ref, mod_ref,
    send_ref, lhs_ref, turned_ref, branch_ref, grad_ref, tr_scr,
):
    steps, per_device, group, count = dims
    pick_group((steps, per_device, group), 1, mid_ref, send_ref)
    out_rows, in_rows = turned_ref.shape[1], cot_ref.shape[0]
    out = lax.broadcasted_iota(jnp.int32, (out_rows, in_rows), 0)
    src = lax.broadcasted_iota(jnp.int32, (out_rows, in_rows), 1)
    base = (out // group) * per_device + lax.rem(out, group)
    for part in range(turned_ref.shape[0]):
        turned = nn((src == base + part * group).astype(F32).astype(BF), cot_ref[...])
        turned_ref[part] = turned.astype(BF)
        branch = (mod_ref[2:3, :] * turned).astype(BF)
        branch_ref[part] = branch
        grad_ref[part] = nt(p_ref[...], branch)
    rows = normed_ref.shape[1]
    for step in range(steps):
        tr_scr[:, step * rows : (step + 1) * rows] = normed_ref[step].astype(F32).T
    arrange(tr_scr, lhs_ref, me_ref[0], count)


def temporal_kernel(
    dims, part, mid_ref, turned_ref, grad_ref, w_ref, mod_ref, gain_ref,
    dmid_ref, normed_ref, dqkv_ref, mixed_ref, qkv_scr, mixed_scr, dqkv_scr,
):
    heads, hd, group = dims
    width = heads * hd
    rows = mid_ref.shape[0]
    x = mid_ref[...].astype(F32)
    normed = modulated(x, mod_ref)
    normed_ref[...] = normed
    qkv_scr[...] = nt(w_ref[...], normed)
    gq, gk = column(gain_ref[0:1, :]), column(gain_ref[1:2, :])
    mask = same_column(rows, group) if group > 1 else None
    for head in range(heads):
        q, k, v = head_parts(qkv_scr, head, hd, width)
        at = head * hd
        v16 = v.astype(BF)
        weights = head_weights(unit_rms(q)[0], unit_rms(k)[0], gq, gk, mask, hd)
        mixed_scr[at : at + hd, :] = nn(v16, weights)
        grad16 = grad_ref[0, at : at + hd, :].astype(BF)
        d_q, d_k = score_vjp(q, k, v16, weights, grad16, gq, gk, hd)
        dqkv_scr[at : at + hd, :] = d_q
        dqkv_scr[width + at : width + at + hd, :] = d_k
        dqkv_scr[2 * width + at : 2 * width + at + hd, :] = nt(grad16, weights)
    mixed_ref[...] = mixed_scr[...].astype(BF)
    dqkv = dqkv_scr[...].astype(BF)
    dqkv_ref[...] = dqkv
    grad = modulate_vjp(x, mod_ref, tn(dqkv, w_ref[...]))
    dmid_ref[...] = (turned_ref[0].astype(F32) + grad).astype(BF)


def temporal_grad_kernel(
    dims, me_ref, normed0_ref, normed1_ref, dqkv0_ref, dqkv1_ref, mixed0_ref, mixed1_ref,
    branch_ref, keep_ref, send_ref,
    tr_scr, lhs_scr, dqkv_scr, mixed_scr,
):
    width, count = dims
    rows = normed0_ref.shape[0]
    for part, (normed, dqkv, mixed) in enumerate(
        ((normed0_ref, dqkv0_ref, mixed0_ref), (normed1_ref, dqkv1_ref, mixed1_ref))
    ):
        at = slice(part * rows, (part + 1) * rows)
        tr_scr[:, at] = normed[...].astype(F32).T
        dqkv_scr[:, at] = dqkv[...]
        mixed_scr[:, at] = mixed[...]
    arrange(tr_scr, lhs_scr, me_ref[0], count)
    put_halves(nt(lhs_scr[...], dqkv_scr[...]), keep_ref, send_ref, slice(0, 3 * width))
    for part in range(2):
        tr_scr[:, part * rows : (part + 1) * rows] = branch_ref[part].astype(F32).T
    arrange(tr_scr, lhs_scr, me_ref[0], count)
    put_halves(nt(lhs_scr[...], mixed_scr[...]), keep_ref, send_ref, slice(3 * width, 4 * width))


def result_kernel(
    dims, mid0_ref, mid1_ref, mixed0_ref, mixed1_ref, p_ref, mod_ref, out_ref, scr
):
    per_device, group = dims
    rows = mid0_ref.shape[0]
    for part, (mid, mixed) in enumerate(((mid0_ref, mixed0_ref), (mid1_ref, mixed1_ref))):
        scr[part * rows : (part + 1) * rows, :] = (
            mid[...].astype(F32) + mod_ref[2:3, :] * tn(mixed[...], p_ref[...])
        ).astype(BF)
    out_rows = out_ref.shape[0]
    out = lax.broadcasted_iota(jnp.int32, (out_rows, out_rows), 0)
    src = lax.broadcasted_iota(jnp.int32, (out_rows, out_rows), 1)
    col = lax.rem(out, per_device)
    base = (col // group) * rows + (out // per_device) * group + lax.rem(col, group)
    out_ref[...] = nn((src == base).astype(F32).astype(BF), scr[...]).astype(BF)


def spatial_value_kernel(
    dims, me_ref, recv0_ref, recv1_ref, att_ref, p_ref, mod_ref, lhs_ref, mixed_ref,
    dmid_ref, grad_ref, dv_ref, keep_ref, send_ref,
    grad_scr, dv_scr, dv_all, tr_scr, lhs_scr,
):
    heads, hd, steps, per_device, group, count = dims
    width = heads * hd
    step = pl.program_id(0)
    rows, in_rows = dmid_ref.shape[1], recv0_ref.shape[0]
    out = lax.broadcasted_iota(jnp.int32, (rows, in_rows), 0)
    src = lax.broadcasted_iota(jnp.int32, (rows, in_rows), 1)
    owner, col = out // per_device, lax.rem(out, per_device)
    base = owner * (steps * group) + step * group + lax.rem(col, group)
    part = jnp.where(src == base, col // group, -1)
    dmid = nn((part == 0).astype(F32).astype(BF), recv0_ref[...])
    dmid += nn((part == 1).astype(F32).astype(BF), recv1_ref[...])
    dmid_ref[0] = dmid.astype(BF)
    branch = (mod_ref[2:3, :] * dmid).astype(BF)
    here = pl.ds(pl.multiple_of(step * rows, rows), rows)
    tr_scr[:, here] = branch.astype(F32).T
    grad_scr[...] = nt(p_ref[...], branch)
    grad_ref[0] = grad_scr[...].astype(BF)
    for head in range(heads):
        at = slice(head * hd, (head + 1) * hd)
        dv_scr[at, :] = nt(grad_scr[at, :].astype(BF), att_ref[0, head])
    d_v = dv_scr[...].astype(BF)
    dv_ref[...] = d_v
    dv_all[:, here] = d_v

    @pl.when(step == steps - 1)
    def _():
        put_halves(nt(lhs_ref[...], dv_all[...]), keep_ref, send_ref, slice(0, width))
        arrange(tr_scr, lhs_scr, me_ref[0], count)
        put_halves(nt(lhs_scr[...], mixed_ref[...]), keep_ref, send_ref, slice(width, 2 * width))


def spatial_score_kernel(
    dims, qkv_ref, att_ref, grad_ref, gain_ref, lhs_ref,
    dqk_ref, keep_ref, send_ref, dqk_scr, dqk_all,
):
    heads, hd, steps = dims
    width = heads * hd
    step = pl.program_id(0)
    rows = qkv_ref.shape[2]
    gq, gk = column(gain_ref[0:1, :]), column(gain_ref[1:2, :])
    for head in range(heads):
        q, k, v = head_parts(qkv_ref.at[0], head, hd, width)
        at = head * hd
        grad16 = grad_ref[0, at : at + hd, :]
        d_q, d_k = score_vjp(q, k, v.astype(BF), att_ref[0, head], grad16, gq, gk, hd)
        dqk_scr[at : at + hd, :] = d_q
        dqk_scr[width + at : width + at + hd, :] = d_k
    dqk = dqk_scr[...].astype(BF)
    dqk_ref[...] = dqk
    dqk_all[:, pl.ds(pl.multiple_of(step * rows, rows), rows)] = dqk

    @pl.when(step == steps - 1)
    def _():
        put_halves(nt(lhs_ref[...], dqk_all[...]), keep_ref, send_ref, slice(None))


def grad_clip_kernel(x_ref, dmid_ref, dqk_ref, dv_ref, w_ref, mod_ref, out_ref):
    cut = dqk_ref.shape[0]
    grad = tn(dqk_ref[...], w_ref[:cut, :]) + tn(dv_ref[...], w_ref[cut:, :])
    grad = modulate_vjp(x_ref[0].astype(F32), mod_ref, grad)
    out_ref[0] = (dmid_ref[0].astype(F32) + grad).astype(BF)


def shape(dims, kind=BF):
    return jax.ShapeDtypeStruct(tuple(dims), kind)


def whole(array):
    n = len(array.shape)
    return pl.BlockSpec(array.shape, lambda *_: (0,) * n, pipeline_mode=pl.Buffered(1))


def each(array):
    n = len(array.shape)
    return pl.BlockSpec((1,) + tuple(array.shape[1:]), lambda i, *_: (i,) + (0,) * (n - 1))


def one(part):
    def spec(array):
        n = len(array.shape)
        return pl.BlockSpec(
            (1,) + tuple(array.shape[1:]), lambda *_: (part,) + (0,) * (n - 1),
            pipeline_mode=pl.Buffered(1),
        )

    return spec


def lanes(steps):
    def spec(array):
        return pl.BlockSpec((array.shape[0], array.shape[1] // steps), lambda i, *_: (0, i))

    return spec


def scalar(array):
    return pl.BlockSpec(memory_space=pltpu.SMEM)


def unused(array):
    return pl.BlockSpec(memory_space=pl.ANY)


def call(kernel, grid, ins, outs, scratch, micros, after=()):
    first, arrays = len(ins), [a for a, _ in ins]

    def run(*refs):
        kernel(*refs[:first], *refs[first + len(after) :])

    return pl.pallas_call(
        run,
        grid=grid,
        in_specs=[s(a) for a, s in ins] + [unused(a) for a in after],
        out_specs=[s(a) for a, s in outs],
        out_shape=[a for a, _ in outs],
        scratch_shapes=[pltpu.VMEM(d, k) for d, k in scratch],
        compiler_params=pltpu.CompilerParams(vmem_limit_bytes=VMEM_LIMIT),
        cost_estimate=pl.CostEstimate(
            flops=int(micros * FLOPS_PER_MICRO), bytes_accessed=0, transcendentals=0
        ),
    )(*arrays, *after)


def exchange(value, axis, flip):
    count = lax.axis_size(axis)
    return lax.ppermute(value, axis, [(i, i ^ flip) for i in range(count)])


def core_kernel(keep_ref, got_ref, *out_refs):
    for slot, out_ref in enumerate(out_refs):
        out_ref[...] = (keep_ref[slot].astype(F32) + got_ref[slot].astype(F32)).astype(BF)


def chip_kernel(count, place_ref, *refs):
    terms, outs = refs[:-count], refs[-count:]
    total = sum((r[...].astype(F32) for r in terms[1:]), terms[0][...].astype(F32))
    size = outs[0].shape[0]
    pieces = [total[i * size : (i + 1) * size] for i in range(count)]
    place = place_ref[0]
    for flip, out_ref in enumerate(outs):
        value = pieces[0]
        for i in range(1, count):
            value = jnp.where(jnp.bitwise_xor(place, flip) == i, pieces[i], value)
        out_ref[...] = value.astype(BF)


def total_kernel(*refs):
    terms, out_ref = refs[:-1], refs[-1]
    out_ref[...] = sum((r[...].astype(F32) for r in terms[1:]), terms[0][...].astype(F32)).astype(BF)


def stack_kernel(count, done_ref, *refs):
    terms, out_ref = refs[:-1], refs[-1]
    total = sum((r[...].astype(F32) for r in terms[1:]), terms[0][...].astype(F32))
    done = done_ref[...].astype(F32)
    cut, size = done.shape[1], out_ref.shape[1]
    for i in range(count):
        at = slice(i * size, (i + 1) * size)
        out_ref[i, :, :cut] = done[at].astype(BF)
        out_ref[i, :, cut:] = total[at].astype(BF)


def scaled_sum(terms, factor):
    return sum((t.astype(F32) for t in terms[1:]), terms[0].astype(F32)) * factor


def stacked_last_kernel(width, factor, terms_ref, qkv_ref, proj_ref, part_ref):
    total = scaled_sum([terms_ref[i] for i in range(terms_ref.shape[0])], factor)
    qkv_ref[...] = total[:, : 3 * width]
    proj_ref[...] = total[:, 3 * width : 4 * width]
    part_ref[...] = total[:, 4 * width :]


def last_kernel(width, factor, part_ref, *refs):
    terms, (qkv_ref, proj_ref) = refs[:-2], refs[-2:]
    qkv_ref[:, : 2 * width] = scaled_sum([r[...] for r in terms], factor)
    qkv_ref[:, 2 * width :] = part_ref[:, :width]
    proj_ref[...] = part_ref[:, width:]


def core_step(keep, send, after=()):
    half, size, columns = keep.shape
    return call(
        core_kernel, (1,), [(keep, whole), (exchange(send, "wide", 1), whole)],
        [(shape((size, columns)), whole)] * half, [], 0, after,
    )


def chip_exchange(blocks):
    return [exchange(b, "wide", 2 * i) if i else b for i, b in enumerate(blocks)]


def body(
    clip_tokens,
    cotangent,
    qkv_spatial,
    proj_spatial,
    adaln_spatial,
    qknorm_spatial,
    qkv_temporal,
    proj_temporal,
    adaln_temporal,
    qknorm_temporal,
):
    steps, patches, depth = clip_tokens.shape
    frames, per_device, _ = cotangent.shape
    hd = qknorm_spatial.shape[1]
    width = proj_spatial.shape[1]
    heads = width // hd
    axes = ("wide", "narrow")
    count = lax.axis_size("wide")
    devices = count * lax.axis_size("narrow")
    parts = 2
    group = per_device // parts
    rows = frames * group
    tokens = steps * patches
    w_s, p_s, w_t, p_t = qkv_spatial.T, proj_spatial.T, qkv_temporal.T, proj_temporal.T
    me = lax.axis_index("wide").astype(jnp.int32).reshape(1)
    half = shape((count // 2, depth // count, 2 * width))
    both = shape((count // 2, depth // count, 4 * width))
    lane = lanes(steps)

    middle, send0, normed_s, qkv_s, att_s, mixed_s = call(
        functools.partial(spatial_forward_kernel, (steps, heads, hd, per_device, group)),
        (steps,),
        [(clip_tokens, each), (w_s, whole), (p_s, whole), (adaln_spatial, whole),
         (qknorm_spatial, whole)],
        [(shape((tokens, depth)), whole), (shape((rows, depth)), whole),
         (shape((steps, patches, depth)), each),
         (shape((steps, 3 * width, patches), F32), each),
         (shape((steps, heads, patches, patches)), each), (shape((width, tokens)), lane)],
        [((width, patches), F32)],
        17,
    )

    def turn(value):
        value = value.reshape(devices, steps * group, depth)
        value = lax.all_to_all(value, axes, split_axis=0, concat_axis=0, tiled=True)
        return value.reshape(rows, depth)

    flat_cot = cotangent.reshape(frames * per_device, depth)
    send1, lhs_s, turned, branch_t, dmixed_t = call(
        functools.partial(between_kernel, (steps, per_device, group, count)),
        (1,),
        [(me, scalar), (middle, whole), (normed_s, whole), (flat_cot, whole), (p_t, whole),
         (adaln_temporal, whole)],
        [(shape((rows, depth)), whole), (shape((depth, tokens)), whole),
         (shape((parts, rows, depth)), whole), (shape((parts, rows, depth)), whole),
         (shape((parts, width, rows), F32), whole)],
        [((depth, tokens), F32)],
        6,
    )
    middles = [turn(send0), turn(send1)]

    received, saved = [], []
    for part in range(parts):
        dmid, *keep = call(
            functools.partial(temporal_kernel, (heads, hd, group), part),
            (1,),
            [(middles[part], whole), (turned, one(part)), (dmixed_t, one(part)), (w_t, whole),
             (adaln_temporal, whole), (qknorm_temporal, whole)],
            [(shape((rows, depth)), whole), (shape((rows, depth)), whole),
             (shape((3 * width, rows)), whole), (shape((width, rows)), whole)],
            [((3 * width, rows), F32), ((width, rows), F32), ((3 * width, rows), F32)],
            13,
        )
        received.append(turn(dmid))
        saved.append(keep)
    (normed0, dqkv0, mixed0), (normed1, dqkv1, mixed1) = saved

    keep_t, send_t = call(
        functools.partial(temporal_grad_kernel, (width, count)),
        (1,),
        [(me, scalar), (normed0, whole), (normed1, whole), (dqkv0, whole), (dqkv1, whole),
         (mixed0, whole), (mixed1, whole), (branch_t, whole)],
        [(both, whole)] * 2,
        [((depth, parts * rows), F32), ((depth, parts * rows), BF),
         ((3 * width, parts * rows), BF), ((width, parts * rows), BF)],
        0,
        [received[0]],
    )
    blocks_t = core_step(keep_t, send_t)
    dmid_s, dmixed_s, dv_s, keep_b, send_b = call(
        functools.partial(spatial_value_kernel, (heads, hd, steps, per_device, group, count)),
        (steps,),
        [(me, scalar), (received[0], whole), (received[1], whole), (att_s, each), (p_s, whole),
         (adaln_spatial, whole), (lhs_s, whole), (mixed_s, whole)],
        [(shape((steps, patches, depth)), each), (shape((steps, width, patches)), each),
         (shape((width, tokens)), lane), (half, whole), (half, whole)],
        [((width, patches), F32), ((width, patches), F32), ((width, tokens), BF),
         ((depth, tokens), F32), ((depth, tokens), BF)],
        10,
        [blocks_t[0]],
    )
    (sum_t,) = call(
        total_kernel, (1,), [(a, whole) for a in chip_exchange(blocks_t)],
        [(shape(blocks_t[0].shape), whole)], [], 20, [send_b],
    )
    blocks_b = core_step(keep_b, send_b, [sum_t])
    dqk_s, keep_a, send_a = call(
        functools.partial(spatial_score_kernel, (heads, hd, steps)),
        (steps,),
        [(qkv_s, each), (att_s, each), (dmixed_s, each), (qknorm_spatial, whole), (lhs_s, whole)],
        [(shape((2 * width, tokens)), lane), (half, whole), (half, whole)],
        [((2 * width, patches), F32), ((2 * width, tokens), BF)],
        11,
        [blocks_b[0], sum_t],
    )
    narrow = lax.axis_size("narrow")
    factor = 1.0 / math.sqrt(frames * patches)
    share = depth // devices
    (stack,) = call(
        functools.partial(stack_kernel, narrow), (1,),
        [(sum_t, whole)] + [(a, whole) for a in chip_exchange(blocks_b)],
        [(shape((narrow, share, 6 * width)), whole)], [], 20, [send_a],
    )
    stack_terms = lax.all_to_all(stack, "narrow", split_axis=0, concat_axis=0, tiled=True)
    blocks_a = core_step(keep_a, send_a, [stack])
    (result,) = call(
        functools.partial(result_kernel, (per_device, group)),
        (1,),
        [(middles[0], whole), (middles[1], whole), (mixed0, whole), (mixed1, whole), (p_t, whole),
         (adaln_temporal, whole)],
        [(shape((frames * per_device, depth)), whole)],
        [((parts * rows, depth), BF)],
        1,
        [blocks_a[0]],
    )
    (grad_clip,) = call(
        grad_clip_kernel,
        (steps,),
        [(clip_tokens, each), (dmid_s, each), (dqk_s, lane), (dv_s, lane), (w_s, whole),
         (adaln_spatial, whole)],
        [(shape((steps, patches, depth)), each)],
        [],
        1,
        [result],
    )
    place = lax.axis_index("narrow").astype(jnp.int32).reshape(1)
    pieces = call(
        functools.partial(chip_kernel, narrow), (1,),
        [(place, scalar)] + [(a, whole) for a in chip_exchange(blocks_a)],
        [(shape((share, 2 * width)), whole)] * narrow, [], 2, [grad_clip],
    )
    whole_grad, part_grad = shape((share, 3 * width), F32), shape((share, width), F32)
    grad_qkv_t, grad_proj_t, rest = call(
        functools.partial(stacked_last_kernel, width, factor), (1,), [(stack_terms, whole)],
        [(whole_grad, whole), (part_grad, whole), (shape((share, 2 * width), F32), whole)], [], 2,
        [pieces[0]],
    )
    grad_qkv_s, grad_proj_s = call(
        functools.partial(last_kernel, width, factor), (1,),
        [(rest, whole)]
        + [(exchange(p, "narrow", i) if i else p, whole) for i, p in enumerate(pieces)],
        [(whole_grad, whole), (part_grad, whole)], [], 2,
    )
    return (
        result.reshape(frames, per_device, depth),
        grad_clip,
        grad_qkv_s,
        grad_proj_s,
        grad_qkv_t,
        grad_proj_t,
    )


def solution(mesh):
    tokens = P(("wide", "narrow"), None, None)
    columns = P(None, ("wide", "narrow"), None)
    own = P(("wide", "narrow"), None)
    return jax.shard_map(
        body,
        mesh=mesh,
        in_specs=(tokens, columns) + (P(),) * 8,
        out_specs=(columns, tokens, own, own, own, own),
        check_vma=False,
    )
```

```python
import functools
import math

import jax
import jax.numpy as jnp
from jax import lax
from jax.experimental import pallas as pl
from jax.experimental.pallas import tpu as pltpu
from jax.sharding import PartitionSpec as P

EPS = 1e-06
BF = jnp.bfloat16
F32 = jnp.float32
VMEM_LIMIT = 56 * 1024 * 1024
SMALL_LIMIT = 24 * 1024 * 1024
FLOPS_PER_MICRO = 1.15e9
LOG2E = math.log2(math.e)


def nn(a, b):
    return lax.dot_general(a, b, (((1,), (0,)), ((), ())), preferred_element_type=F32)


def nt(a, b):
    return lax.dot_general(a, b, (((1,), (1,)), ((), ())), preferred_element_type=F32)


def tn(a, b):
    return lax.dot_general(a, b, (((0,), (0,)), ((), ())), preferred_element_type=F32)


def standardize(x):
    centre = x - jnp.mean(x, axis=-1, keepdims=True)
    rate = lax.rsqrt(jnp.mean(centre * centre, axis=-1, keepdims=True) + EPS)
    return centre * rate, rate


def modulated(x, mod_ref):
    return (standardize(x)[0] * (1.0 + mod_ref[1:2, :]) + mod_ref[0:1, :]).astype(BF)


def modulate_vjp(x, mod_ref, grad):
    unit, rate = standardize(x)
    scaled = grad * (1.0 + mod_ref[1:2, :])
    inner = jnp.mean(unit * scaled, axis=-1, keepdims=True)
    return rate * (scaled - jnp.mean(scaled, axis=-1, keepdims=True) - unit * inner)


def column(row):
    n = row.shape[1]
    same = lax.broadcasted_iota(jnp.int32, (n, n), 0) == lax.broadcasted_iota(jnp.int32, (n, n), 1)
    return jnp.sum(jnp.where(same, jnp.broadcast_to(row, (n, n)), 0.0), axis=1, keepdims=True)


def unit_rms(vectors):
    rate = lax.rsqrt(jnp.mean(vectors * vectors, axis=0, keepdims=True) + EPS)
    return vectors * rate, rate


def same_column(rows, stride):
    first = lax.broadcasted_iota(jnp.int32, (rows, rows), 0)
    second = lax.broadcasted_iota(jnp.int32, (rows, rows), 1)
    return lax.rem(first, stride) == lax.rem(second, stride)


def head_parts(qkv_ref, head, hd, width):
    at = head * hd
    return (
        qkv_ref[at : at + hd, :],
        qkv_ref[width + at : width + at + hd, :],
        qkv_ref[2 * width + at : 2 * width + at + hd, :],
    )


def head_weights(q_unit, k_unit, gq, gk, mask, hd):
    qn = (q_unit * (gq * (LOG2E / math.sqrt(hd)))).astype(BF)
    kn = (k_unit * gk).astype(BF)
    weights = jnp.exp2(tn(kn, qn))
    if mask is not None:
        weights = jnp.where(mask, weights, 0.0)
    return (weights * (1.0 / jnp.sum(weights, axis=0, keepdims=True))).astype(BF)


def score_vjp(q, k, v16, weights, grad16, gq, gk, hd):
    q_unit, q_rate = unit_rms(q)
    k_unit, k_rate = unit_rms(k)
    scale = 1.0 / math.sqrt(hd)
    w32 = weights.astype(F32)
    weighted = w32 * tn(v16, grad16)
    d_s = (weighted - w32 * jnp.sum(weighted, axis=0, keepdims=True)).astype(BF)
    d_q = nn((k_unit * gk).astype(BF), d_s) * (gq * scale)
    d_k = nt((q_unit * gq).astype(BF), d_s) * (gk * scale)
    d_q = q_rate * (d_q - q_unit * jnp.mean(q_unit * d_q, axis=0, keepdims=True))
    d_k = k_rate * (d_k - k_unit * jnp.mean(k_unit * d_k, axis=0, keepdims=True))
    return d_q, d_k


def arrange(tr_ref, lhs_ref, me, count):
    size = lhs_ref.shape[0] // count
    for slot in range(count):
        place = (slot % (count // 2)) * 2 + slot // (count // 2)
        start = pl.multiple_of(jnp.bitwise_xor(me, place) * size, 8)
        lhs_ref[slot * size : (slot + 1) * size, :] = tr_ref[pl.ds(start, size), :].astype(BF)


def put_halves(value, keep_ref, send_ref, columns):
    half, size = keep_ref.shape[0], keep_ref.shape[1]
    for slot in range(half):
        keep_ref[slot, :, columns] = value[slot * size : (slot + 1) * size].astype(BF)
        send_ref[slot, :, columns] = value[(half + slot) * size : (half + slot + 1) * size].astype(BF)


def pick_group(dims, part, mid_ref, send_ref):
    steps, per_device, group = dims
    out_rows, in_rows = send_ref.shape[0], mid_ref.shape[0]
    out = lax.broadcasted_iota(jnp.int32, (out_rows, in_rows), 0)
    src = lax.broadcasted_iota(jnp.int32, (out_rows, in_rows), 1)
    owner, rest = out // (steps * group), lax.rem(out, steps * group)
    base = (rest // group) * (in_rows // steps) + owner * per_device + lax.rem(rest, group)
    pick = (src == base + part * group).astype(F32).astype(BF)
    send_ref[...] = nn(pick, mid_ref[...]).astype(BF)


def spatial_forward_kernel(
    dims, x_ref, w_ref, p_ref, mod_ref, gain_ref,
    mid_ref, send_ref, normed_ref, qkv_ref, att_ref, mixed_ref, mixed_scr,
):
    steps, heads, hd, per_device, group = dims
    rows = x_ref.shape[1]
    width = heads * hd
    gq, gk = column(gain_ref[0:1, :]), column(gain_ref[1:2, :])
    for step in range(steps):
        x = x_ref[step].astype(F32)
        normed = modulated(x, mod_ref)
        normed_ref.put(step, normed)
        qkv_ref.put(step, nt(w_ref[...], normed))
        for head in range(heads):
            q, k, v = head_parts(qkv_ref.ref(step), head, hd, width)
            weights = head_weights(unit_rms(q)[0], unit_rms(k)[0], gq, gk, None, hd)
            att_ref[step, head] = weights
            mixed_scr[head * hd : (head + 1) * hd, :] = nn(v.astype(BF), weights)
        att_ref.flush(step)
        mixed = mixed_scr[...].astype(BF)
        mixed_ref[:, step * rows : (step + 1) * rows] = mixed
        mixed_ref.flush(step)
        mid_ref[step * rows : (step + 1) * rows, :] = (
            x + mod_ref[2:3, :] * tn(mixed, p_ref[...])
        ).astype(BF)
    mid_ref.flush()
    pick_group((steps, per_device, group), 0, mid_ref, send_ref)


def between_kernel(
    dims, me_ref, mid_ref, normed_ref, cot_ref, p_ref, mod_ref,
    send_ref, lhs_ref, turned_ref, branch_ref, grad_ref, tr_scr,
):
    steps, per_device, group, count = dims
    pick_group((steps, per_device, group), 1, mid_ref, send_ref)
    send_ref.flush()
    out_rows, in_rows = turned_ref.shape[1], cot_ref.shape[0]
    out = lax.broadcasted_iota(jnp.int32, (out_rows, in_rows), 0)
    src = lax.broadcasted_iota(jnp.int32, (out_rows, in_rows), 1)
    base = (out // group) * per_device + lax.rem(out, group)
    for part in range(turned_ref.shape[0]):
        turned = nn((src == base + part * group).astype(F32).astype(BF), cot_ref[...])
        turned_ref.put(part, turned.astype(BF))
        branch = (mod_ref[2:3, :] * turned).astype(BF)
        branch_ref.put(part, branch)
        grad_ref.put(part, nt(p_ref[...], branch))
    rows = normed_ref.shape[1]
    for step in range(steps):
        tr_scr[:, step * rows : (step + 1) * rows] = normed_ref[step].astype(F32).T
    arrange(tr_scr, lhs_ref, me_ref[0], count)


def temporal_kernel(
    dims, part, mid_ref, turned_ref, grad_ref, w_ref, mod_ref, gain_ref,
    dmid_ref, normed_ref, dqkv_ref, mixed_ref, qkv_scr, mixed_scr, dqkv_scr,
):
    heads, hd, group = dims
    width = heads * hd
    rows = mid_ref.shape[0]
    x = mid_ref[...].astype(F32)
    normed = modulated(x, mod_ref)
    normed_ref.put(..., normed)
    qkv_scr[...] = nt(w_ref[...], normed)
    gq, gk = column(gain_ref[0:1, :]), column(gain_ref[1:2, :])
    mask = same_column(rows, group) if group > 1 else None
    for head in range(heads):
        q, k, v = head_parts(qkv_scr, head, hd, width)
        at = head * hd
        v16 = v.astype(BF)
        weights = head_weights(unit_rms(q)[0], unit_rms(k)[0], gq, gk, mask, hd)
        mixed_scr[at : at + hd, :] = nn(v16, weights)
        grad16 = grad_ref[0, at : at + hd, :].astype(BF)
        d_q, d_k = score_vjp(q, k, v16, weights, grad16, gq, gk, hd)
        dqkv_scr[at : at + hd, :] = d_q
        dqkv_scr[width + at : width + at + hd, :] = d_k
        dqkv_scr[2 * width + at : 2 * width + at + hd, :] = nt(grad16, weights)
    mixed_ref.put(..., mixed_scr[...].astype(BF))
    dqkv = dqkv_scr[...].astype(BF)
    dqkv_ref.put(..., dqkv)
    grad = modulate_vjp(x, mod_ref, tn(dqkv, w_ref[...]))
    dmid_ref[...] = (turned_ref[0].astype(F32) + grad).astype(BF)


def temporal_grad_kernel(
    dims, me_ref, normed0_ref, normed1_ref, dqkv0_ref, dqkv1_ref, mixed0_ref, mixed1_ref,
    branch_ref, keep_ref, send_ref,
    tr_scr, lhs_scr, dqkv_scr, mixed_scr,
):
    width, count = dims
    rows = normed0_ref.shape[0]
    for part, (normed, dqkv, mixed) in enumerate(
        ((normed0_ref, dqkv0_ref, mixed0_ref), (normed1_ref, dqkv1_ref, mixed1_ref))
    ):
        at = slice(part * rows, (part + 1) * rows)
        tr_scr[:, at] = normed[...].astype(F32).T
        dqkv_scr[:, at] = dqkv[...]
        mixed_scr[:, at] = mixed[...]
    arrange(tr_scr, lhs_scr, me_ref[0], count)
    put_halves(nt(lhs_scr[...], dqkv_scr[...]), keep_ref, send_ref, slice(0, 3 * width))
    for part in range(2):
        tr_scr[:, part * rows : (part + 1) * rows] = branch_ref[part].astype(F32).T
    arrange(tr_scr, lhs_scr, me_ref[0], count)
    put_halves(nt(lhs_scr[...], mixed_scr[...]), keep_ref, send_ref, slice(3 * width, 4 * width))


def result_kernel(
    dims, mid0_ref, mid1_ref, mixed0_ref, mixed1_ref, p_ref, mod_ref, out_ref, scr
):
    per_device, group = dims
    rows = mid0_ref.shape[0]
    for part, (mid, mixed) in enumerate(((mid0_ref, mixed0_ref), (mid1_ref, mixed1_ref))):
        scr[part * rows : (part + 1) * rows, :] = (
            mid[...].astype(F32) + mod_ref[2:3, :] * tn(mixed[...], p_ref[...])
        ).astype(BF)
    out_rows = out_ref.shape[0]
    out = lax.broadcasted_iota(jnp.int32, (out_rows, out_rows), 0)
    src = lax.broadcasted_iota(jnp.int32, (out_rows, out_rows), 1)
    col = lax.rem(out, per_device)
    base = (col // group) * rows + (out // per_device) * group + lax.rem(col, group)
    out_ref[...] = nn((src == base).astype(F32).astype(BF), scr[...]).astype(BF)


def spatial_value_kernel(
    dims, me_ref, recv0_ref, recv1_ref, att_ref, p_ref, mod_ref, lhs_ref, mixed_ref,
    dmid_ref, grad_ref, dv_ref, keep_ref, send_ref,
    grad_scr, dv_scr, tr_scr, lhs_scr,
):
    heads, hd, steps, per_device, group, count = dims
    width = heads * hd
    rows, in_rows = dmid_ref.shape[1], recv0_ref.shape[0]
    out = lax.broadcasted_iota(jnp.int32, (rows, in_rows), 0)
    src = lax.broadcasted_iota(jnp.int32, (rows, in_rows), 1)
    owner, col = out // per_device, lax.rem(out, per_device)
    for step in range(steps):
        base = owner * (steps * group) + step * group + lax.rem(col, group)
        part = jnp.where(src == base, col // group, -1)
        dmid = nn((part == 0).astype(F32).astype(BF), recv0_ref[...])
        dmid += nn((part == 1).astype(F32).astype(BF), recv1_ref[...])
        dmid_ref.put(step, dmid.astype(BF))
        branch = (mod_ref[2:3, :] * dmid).astype(BF)
        here = slice(step * rows, (step + 1) * rows)
        tr_scr[:, here] = branch.astype(F32).T
        grad_scr[...] = nt(p_ref[...], branch)
        grad_ref.put(step, grad_scr[...].astype(BF))
        for head in range(heads):
            at = slice(head * hd, (head + 1) * hd)
            dv_scr[at, :] = nt(grad_scr[at, :].astype(BF), att_ref[step, head])
        dv_ref[:, here] = dv_scr[...].astype(BF)
        dv_ref.flush(step)
    put_halves(nt(lhs_ref[...], dv_ref[...]), keep_ref, send_ref, slice(0, width))
    arrange(tr_scr, lhs_scr, me_ref[0], count)
    put_halves(nt(lhs_scr[...], mixed_ref[...]), keep_ref, send_ref, slice(width, 2 * width))


def spatial_score_kernel(
    dims, qkv_ref, att_ref, grad_ref, gain_ref, lhs_ref,
    dqk_ref, keep_ref, send_ref, dqk_scr,
):
    heads, hd, steps = dims
    width = heads * hd
    rows = qkv_ref.shape[2]
    gq, gk = column(gain_ref[0:1, :]), column(gain_ref[1:2, :])
    for step in range(steps):
        for head in range(heads):
            q, k, v = head_parts(qkv_ref.ref(step), head, hd, width)
            at = head * hd
            grad16 = grad_ref[step, at : at + hd, :]
            d_q, d_k = score_vjp(q, k, v.astype(BF), att_ref[step, head], grad16, gq, gk, hd)
            dqk_scr[at : at + hd, :] = d_q
            dqk_scr[width + at : width + at + hd, :] = d_k
        dqk_ref[:, step * rows : (step + 1) * rows] = dqk_scr[...].astype(BF)
        dqk_ref.flush(step)
    put_halves(nt(lhs_ref[...], dqk_ref[...]), keep_ref, send_ref, slice(None))


def grad_clip_kernel(x_ref, dmid_ref, dqk_ref, dv_ref, w_ref, mod_ref, out_ref):
    cut = dqk_ref.shape[0]
    for step in range(x_ref.shape[0]):
        grad = tn(dqk_ref.lanes(step), w_ref[:cut, :]) + tn(dv_ref.lanes(step), w_ref[cut:, :])
        grad = modulate_vjp(x_ref[step].astype(F32), mod_ref, grad)
        out_ref.put(step, (dmid_ref[step].astype(F32) + grad).astype(BF))


def shape(dims, kind=BF):
    return jax.ShapeDtypeStruct(tuple(dims), kind)


def whole(array):
    n = len(array.shape)
    return pl.BlockSpec(array.shape, lambda *_: (0,) * n, pipeline_mode=pl.Buffered(1))


def each(array):
    pass


def lane(array):
    pass


def scalar(array):
    return pl.BlockSpec(memory_space=pltpu.SMEM)


def unused(array):
    return pl.BlockSpec(memory_space=pl.ANY)


def in_place(array):
    large = math.prod(array.shape) > 600000
    return pl.BlockSpec(memory_space=pltpu.HBM if large else pl.ANY)


def small_call(kernel, grid, ins, outs, scratch, micros, after=()):
    first, arrays = len(ins), [a for a, _ in ins]

    def run(*refs):
        kernel(*refs[:first], *refs[first + len(after) :])

    return pl.pallas_call(
        run,
        grid=grid,
        in_specs=[s(a) for a, s in ins] + [in_place(a) for a in after],
        out_specs=[s(a) for a, s in outs],
        out_shape=[a for a, _ in outs],
        scratch_shapes=[pltpu.VMEM(d, k) for d, k in scratch],
        compiler_params=pltpu.CompilerParams(vmem_limit_bytes=SMALL_LIMIT),
        cost_estimate=pl.CostEstimate(
            flops=int(micros * FLOPS_PER_MICRO), bytes_accessed=0, transcendentals=0
        ),
    )(*arrays, *after)


class Source:
    def __init__(self, hbm, buf, pairs, sems, first):
        self.buf, self.shape = buf, buf.shape
        self.copies = [pltpu.make_async_copy(a, b, sems.at[first + i]) for i, (a, b) in enumerate(pairs)]
        self.waiting = set(range(len(self.copies)))

    def wait(self, index):
        wanted = [index] if isinstance(index, int) and len(self.copies) > 1 else range(len(self.copies))
        for i in wanted:
            if i in self.waiting:
                self.copies[i].wait()
                self.waiting.remove(i)

    def __getitem__(self, index):
        self.wait(index[0] if isinstance(index, tuple) else index)
        return self.buf[index]

    def ref(self, index):
        self.wait(index)
        return self.buf.at[index]

    def lanes(self, index):
        self.wait(index)
        size = self.shape[1] // len(self.copies)
        return self.buf[:, index * size : (index + 1) * size]


class Sink:
    def __init__(self, hbm, buf, pairs, sems, first):
        self.buf, self.shape = buf, buf.shape
        self.copies = [pltpu.make_async_copy(b, a, sems.at[first + i]) for i, (a, b) in enumerate(pairs)]
        self.left = set(range(len(self.copies)))

    def __getitem__(self, index):
        return self.buf[index]

    def __setitem__(self, index, value):
        self.buf[index] = value

    def ref(self, index):
        return self.buf.at[index]

    def flush(self, index=None):
        for i in sorted(self.left) if index is None else [index]:
            self.copies[i].start()
            self.left.remove(i)

    def put(self, index, value):
        self.buf[index] = value
        self.flush(index if len(self.copies) > 1 else None)


def cuts(hbm, buf, kind, steps):
    if kind is each:
        return [(hbm.at[i], buf.at[i]) for i in range(buf.shape[0])]
    if kind is lane:
        size = buf.shape[1] // steps
        return [(hbm.at[:, pl.ds(i * size, size)], buf.at[:, pl.ds(i * size, size)]) for i in range(steps)]
    if isinstance(kind, int):
        return [(hbm.at[pl.ds(kind, 1)], buf)]
    return [(hbm, buf)]


def count_cuts(array, kind, steps):
    return array.shape[0] if kind is each else steps if kind is lane else 1


def call(kernel, steps, ins, outs, scratch, micros, after=()):
    arrays = [a for a, _ in ins]
    moved = [(a, k) for a, k in ins if k is not scalar]
    first_of, total = [], 0
    for a, k in moved + list(outs):
        first_of.append(total)
        total += count_cuts(a, k, steps)

    def buffer(array, kind):
        dims = (1,) + tuple(array.shape[1:]) if isinstance(kind, int) else tuple(array.shape)
        return pltpu.VMEM(dims, array.dtype)

    def run(*refs):
        given, refs = refs[: len(ins)], refs[len(ins) + len(after) :]
        results, refs = refs[: len(outs)], refs[len(outs) :]
        own, refs = refs[: len(scratch)], refs[len(scratch) :]
        sems, bufs = refs[-1], list(refs[:-1])
        firsts = list(first_of)
        sources = []
        for ref, (_, kind) in zip(given, ins):
            if kind is scalar:
                sources.append(ref)
            else:
                buf = bufs.pop(0)
                sources.append(Source(ref, buf, cuts(ref, buf, kind, steps), sems, firsts.pop(0)))
        sinks = []
        for ref, (_, kind) in zip(results, outs):
            buf = bufs.pop(0)
            sinks.append(Sink(ref, buf, cuts(ref, buf, kind, steps), sems, firsts.pop(0)))
        live = [x for x in sources if isinstance(x, Source)]
        live.sort(key=lambda x: math.prod(x.shape) > 16384)
        for i in range(max(len(x.copies) for x in live)):
            for x in live:
                if i < len(x.copies):
                    x.copies[i].start()
        kernel(*sources, *sinks, *own)
        for x in live:
            for i in sorted(x.waiting):
                x.copies[i].wait()
        for x in sinks:
            x.flush()
        for x in sinks:
            for copy in x.copies:
                copy.wait()

    return pl.pallas_call(
        run,
        in_specs=[scalar(a) if k is scalar else unused(a) for a, k in ins] + [unused(a) for a in after],
        out_specs=[unused(a) for a, _ in outs],
        out_shape=[a for a, _ in outs],
        scratch_shapes=[pltpu.VMEM(d, k) for d, k in scratch]
        + [buffer(a, k) for a, k in moved + list(outs)]
        + [pltpu.SemaphoreType.DMA((total,))],
        compiler_params=pltpu.CompilerParams(vmem_limit_bytes=VMEM_LIMIT),
        cost_estimate=pl.CostEstimate(
            flops=int(micros * FLOPS_PER_MICRO), bytes_accessed=0, transcendentals=0
        ),
    )(*arrays, *after)


def exchange(value, axis, flip):
    count = lax.axis_size(axis)
    return lax.ppermute(value, axis, [(i, i ^ flip) for i in range(count)])


def core_kernel(keep_ref, got_ref, *out_refs):
    for slot, out_ref in enumerate(out_refs):
        out_ref[...] = (keep_ref[slot].astype(F32) + got_ref[slot].astype(F32)).astype(BF)


def chip_kernel(count, place_ref, *refs):
    terms, outs = refs[:-count], refs[-count:]
    total = sum((r[...].astype(F32) for r in terms[1:]), terms[0][...].astype(F32))
    size = outs[0].shape[0]
    pieces = [total[i * size : (i + 1) * size] for i in range(count)]
    place = place_ref[0]
    for flip, out_ref in enumerate(outs):
        value = pieces[0]
        for i in range(1, count):
            value = jnp.where(jnp.bitwise_xor(place, flip) == i, pieces[i], value)
        out_ref[...] = value.astype(BF)


def total_kernel(*refs):
    terms, out_ref = refs[:-1], refs[-1]
    out_ref[...] = sum((r[...].astype(F32) for r in terms[1:]), terms[0][...].astype(F32)).astype(BF)


def stack_kernel(count, done_ref, *refs):
    terms, out_ref = refs[:-1], refs[-1]
    total = sum((r[...].astype(F32) for r in terms[1:]), terms[0][...].astype(F32))
    done = done_ref[...].astype(F32)
    cut, size = done.shape[1], out_ref.shape[1]
    for i in range(count):
        at = slice(i * size, (i + 1) * size)
        out_ref[i, :, :cut] = done[at].astype(BF)
        out_ref[i, :, cut:] = total[at].astype(BF)


def scaled_sum(terms, factor):
    return sum((t.astype(F32) for t in terms[1:]), terms[0].astype(F32)) * factor


def stacked_last_kernel(width, factor, terms_ref, qkv_ref, proj_ref, part_ref):
    total = scaled_sum([terms_ref[i] for i in range(terms_ref.shape[0])], factor)
    qkv_ref[...] = total[:, : 3 * width]
    proj_ref[...] = total[:, 3 * width : 4 * width]
    part_ref[...] = total[:, 4 * width :]


def last_kernel(width, factor, part_ref, *refs):
    terms, (qkv_ref, proj_ref) = refs[:-2], refs[-2:]
    qkv_ref[:, : 2 * width] = scaled_sum([r[...] for r in terms], factor)
    qkv_ref[:, 2 * width :] = part_ref[:, :width]
    proj_ref[...] = part_ref[:, width:]


def core_step(keep, send, after=()):
    half, size, columns = keep.shape
    return small_call(
        core_kernel, (1,), [(keep, whole), (exchange(send, "wide", 1), whole)],
        [(shape((size, columns)), whole)] * half, [], 0, after,
    )


def chip_exchange(blocks):
    return [exchange(b, "wide", 2 * i) if i else b for i, b in enumerate(blocks)]


def body(
    clip_tokens,
    cotangent,
    qkv_spatial,
    proj_spatial,
    adaln_spatial,
    qknorm_spatial,
    qkv_temporal,
    proj_temporal,
    adaln_temporal,
    qknorm_temporal,
):
    steps, patches, depth = clip_tokens.shape
    frames, per_device, _ = cotangent.shape
    hd = qknorm_spatial.shape[1]
    width = proj_spatial.shape[1]
    heads = width // hd
    axes = ("wide", "narrow")
    count = lax.axis_size("wide")
    devices = count * lax.axis_size("narrow")
    parts = 2
    group = per_device // parts
    rows = frames * group
    tokens = steps * patches
    w_s, p_s, w_t, p_t = qkv_spatial.T, proj_spatial.T, qkv_temporal.T, proj_temporal.T
    me = lax.axis_index("wide").astype(jnp.int32).reshape(1)
    half = shape((count // 2, depth // count, 2 * width))
    both = shape((count // 2, depth // count, 4 * width))

    middle, send0, normed_s, qkv_s, att_s, mixed_s = call(
        functools.partial(spatial_forward_kernel, (steps, heads, hd, per_device, group)),
        steps,
        [(clip_tokens, each), (w_s, whole), (p_s, whole), (adaln_spatial, whole),
         (qknorm_spatial, whole)],
        [(shape((tokens, depth)), whole), (shape((rows, depth)), whole),
         (shape((steps, patches, depth)), each),
         (shape((steps, 3 * width, patches), F32), each),
         (shape((steps, heads, patches, patches)), each), (shape((width, tokens)), lane)],
        [((width, patches), F32)],
        17,
    )

    def turn(value):
        value = value.reshape(devices, steps * group, depth)
        value = lax.all_to_all(value, axes, split_axis=0, concat_axis=0, tiled=True)
        return value.reshape(rows, depth)

    flat_cot = cotangent.reshape(frames * per_device, depth)
    send1, lhs_s, turned, branch_t, dmixed_t = call(
        functools.partial(between_kernel, (steps, per_device, group, count)),
        steps,
        [(me, scalar), (middle, whole), (normed_s, whole), (flat_cot, whole), (p_t, whole),
         (adaln_temporal, whole)],
        [(shape((rows, depth)), whole), (shape((depth, tokens)), whole),
         (shape((parts, rows, depth)), each), (shape((parts, rows, depth)), each),
         (shape((parts, width, rows), F32), each)],
        [((depth, tokens), F32)],
        6,
    )
    middles = [turn(send0), turn(send1)]

    received, saved = [], []
    for part in range(parts):
        dmid, *keep = call(
            functools.partial(temporal_kernel, (heads, hd, group), part),
            (1,),
            [(middles[part], whole), (turned, part), (dmixed_t, part), (w_t, whole),
             (adaln_temporal, whole), (qknorm_temporal, whole)],
            [(shape((rows, depth)), whole), (shape((rows, depth)), whole),
             (shape((3 * width, rows)), whole), (shape((width, rows)), whole)],
            [((3 * width, rows), F32), ((width, rows), F32), ((3 * width, rows), F32)],
            13,
        )
        received.append(turn(dmid))
        saved.append(keep)
    (normed0, dqkv0, mixed0), (normed1, dqkv1, mixed1) = saved

    keep_t, send_t = call(
        functools.partial(temporal_grad_kernel, (width, count)),
        steps,
        [(me, scalar), (normed0, whole), (normed1, whole), (dqkv0, whole), (dqkv1, whole),
         (mixed0, whole), (mixed1, whole), (branch_t, whole)],
        [(both, whole)] * 2,
        [((depth, parts * rows), F32), ((depth, parts * rows), BF),
         ((3 * width, parts * rows), BF), ((width, parts * rows), BF)],
        0,
        [received[0]],
    )
    blocks_t = core_step(keep_t, send_t)
    dmid_s, dmixed_s, dv_s, keep_b, send_b = call(
        functools.partial(spatial_value_kernel, (heads, hd, steps, per_device, group, count)),
        steps,
        [(me, scalar), (received[0], whole), (received[1], whole), (att_s, each), (p_s, whole),
         (adaln_spatial, whole), (lhs_s, whole), (mixed_s, whole)],
        [(shape((steps, patches, depth)), each), (shape((steps, width, patches)), each),
         (shape((width, tokens)), lane), (half, whole), (half, whole)],
        [((width, patches), F32), ((width, patches), F32),
         ((depth, tokens), F32), ((depth, tokens), BF)],
        10,
        [blocks_t[0]],
    )
    (sum_t,) = small_call(
        total_kernel, (1,), [(a, whole) for a in chip_exchange(blocks_t)],
        [(shape(blocks_t[0].shape), whole)], [], 20, [send_b],
    )
    blocks_b = core_step(keep_b, send_b, [sum_t])
    dqk_s, keep_a, send_a = call(
        functools.partial(spatial_score_kernel, (heads, hd, steps)),
        steps,
        [(qkv_s, each), (att_s, each), (dmixed_s, each), (qknorm_spatial, whole), (lhs_s, whole)],
        [(shape((2 * width, tokens)), lane), (half, whole), (half, whole)],
        [((2 * width, patches), F32)],
        11,
        [blocks_b[0], sum_t],
    )
    narrow = lax.axis_size("narrow")
    factor = 1.0 / math.sqrt(frames * patches)
    share = depth // devices
    (stack,) = small_call(
        functools.partial(stack_kernel, narrow), (1,),
        [(sum_t, whole)] + [(a, whole) for a in chip_exchange(blocks_b)],
        [(shape((narrow, share, 6 * width)), whole)], [], 20, [send_a],
    )
    stack_terms = lax.all_to_all(stack, "narrow", split_axis=0, concat_axis=0, tiled=True)
    blocks_a = core_step(keep_a, send_a, [stack])
    (result,) = call(
        functools.partial(result_kernel, (per_device, group)),
        steps,
        [(middles[0], whole), (middles[1], whole), (mixed0, whole), (mixed1, whole), (p_t, whole),
         (adaln_temporal, whole)],
        [(shape((frames * per_device, depth)), whole)],
        [((parts * rows, depth), BF)],
        1,
        [blocks_a[0]],
    )
    (grad_clip,) = call(
        grad_clip_kernel,
        steps,
        [(clip_tokens, each), (dmid_s, each), (dqk_s, lane), (dv_s, lane), (w_s, whole),
         (adaln_spatial, whole)],
        [(shape((steps, patches, depth)), each)],
        [],
        1,
        [result],
    )
    place = lax.axis_index("narrow").astype(jnp.int32).reshape(1)
    pieces = small_call(
        functools.partial(chip_kernel, narrow), (1,),
        [(place, scalar)] + [(a, whole) for a in chip_exchange(blocks_a)],
        [(shape((share, 2 * width)), whole)] * narrow, [], 2, [grad_clip],
    )
    whole_grad, part_grad = shape((share, 3 * width), F32), shape((share, width), F32)
    grad_qkv_t, grad_proj_t, rest = small_call(
        functools.partial(stacked_last_kernel, width, factor), (1,), [(stack_terms, whole)],
        [(whole_grad, whole), (part_grad, whole), (shape((share, 2 * width), F32), whole)], [], 2,
        [pieces[0]],
    )
    grad_qkv_s, grad_proj_s = small_call(
        functools.partial(last_kernel, width, factor), (1,),
        [(rest, whole)]
        + [(exchange(p, "narrow", i) if i else p, whole) for i, p in enumerate(pieces)],
        [(whole_grad, whole), (part_grad, whole)], [], 2,
    )
    return (
        result.reshape(frames, per_device, depth),
        grad_clip,
        grad_qkv_s,
        grad_proj_s,
        grad_qkv_t,
        grad_proj_t,
    )


def solution(mesh):
    tokens = P(("wide", "narrow"), None, None)
    columns = P(None, ("wide", "narrow"), None)
    own = P(("wide", "narrow"), None)
    return jax.shard_map(
        body,
        mesh=mesh,
        in_specs=(tokens, columns) + (P(),) * 8,
        out_specs=(columns, tokens, own, own, own, own),
        check_vma=False,
    )
```

```python
import functools
import math

import jax
import jax.numpy as jnp
from jax import lax
from jax.experimental import pallas as pl
from jax.experimental.pallas import tpu as pltpu
from jax.sharding import PartitionSpec as P

EPS = 1e-06
BF = jnp.bfloat16
F32 = jnp.float32
VMEM_LIMIT = 56 * 1024 * 1024
SMALL_LIMIT = 24 * 1024 * 1024
FLOPS_PER_MICRO = 1.15e9
LOG2E = math.log2(math.e)


def nn(a, b):
    return lax.dot_general(a, b, (((1,), (0,)), ((), ())), preferred_element_type=F32)


def nt(a, b):
    return lax.dot_general(a, b, (((1,), (1,)), ((), ())), preferred_element_type=F32)


def tn(a, b):
    return lax.dot_general(a, b, (((0,), (0,)), ((), ())), preferred_element_type=F32)


def standardize(x):
    centre = x - jnp.mean(x, axis=-1, keepdims=True)
    rate = lax.rsqrt(jnp.mean(centre * centre, axis=-1, keepdims=True) + EPS)
    return centre * rate, rate


def modulated(x, mod_ref):
    return (standardize(x)[0] * (1.0 + mod_ref[1:2, :]) + mod_ref[0:1, :]).astype(BF)


def modulate_vjp(x, mod_ref, grad):
    unit, rate = standardize(x)
    scaled = grad * (1.0 + mod_ref[1:2, :])
    inner = jnp.mean(unit * scaled, axis=-1, keepdims=True)
    return rate * (scaled - jnp.mean(scaled, axis=-1, keepdims=True) - unit * inner)


def column(row):
    n = row.shape[1]
    same = lax.broadcasted_iota(jnp.int32, (n, n), 0) == lax.broadcasted_iota(jnp.int32, (n, n), 1)
    return jnp.sum(jnp.where(same, jnp.broadcast_to(row, (n, n)), 0.0), axis=1, keepdims=True)


def unit_rms(vectors):
    rate = lax.rsqrt(jnp.mean(vectors * vectors, axis=0, keepdims=True) + EPS)
    return vectors * rate, rate


def same_column(rows, stride):
    first = lax.broadcasted_iota(jnp.int32, (rows, rows), 0)
    second = lax.broadcasted_iota(jnp.int32, (rows, rows), 1)
    return lax.rem(first, stride) == lax.rem(second, stride)


def head_parts(qkv_ref, head, hd, width):
    at = head * hd
    return (
        qkv_ref[at : at + hd, :],
        qkv_ref[width + at : width + at + hd, :],
        qkv_ref[2 * width + at : 2 * width + at + hd, :],
    )


def head_weights(q_unit, k_unit, gq, gk, mask, hd):
    qn = (q_unit * (gq * (LOG2E / math.sqrt(hd)))).astype(BF)
    kn = (k_unit * gk).astype(BF)
    weights = jnp.exp2(tn(kn, qn))
    if mask is not None:
        weights = jnp.where(mask, weights, 0.0)
    return (weights * (1.0 / jnp.sum(weights, axis=0, keepdims=True))).astype(BF)


def score_vjp(q, k, v16, weights, grad16, gq, gk, hd):
    q_unit, q_rate = unit_rms(q)
    k_unit, k_rate = unit_rms(k)
    scale = 1.0 / math.sqrt(hd)
    w32 = weights.astype(F32)
    weighted = w32 * tn(v16, grad16)
    d_s = (weighted - w32 * jnp.sum(weighted, axis=0, keepdims=True)).astype(BF)
    d_q = nn((k_unit * gk).astype(BF), d_s) * (gq * scale)
    d_k = nt((q_unit * gq).astype(BF), d_s) * (gk * scale)
    d_q = q_rate * (d_q - q_unit * jnp.mean(q_unit * d_q, axis=0, keepdims=True))
    d_k = k_rate * (d_k - k_unit * jnp.mean(k_unit * d_k, axis=0, keepdims=True))
    return d_q, d_k


def arrange(tr_ref, lhs_ref, me, count):
    size = lhs_ref.shape[0] // count
    for slot in range(count):
        place = (slot % (count // 2)) * 2 + slot // (count // 2)
        start = pl.multiple_of(jnp.bitwise_xor(me, place) * size, 8)
        lhs_ref[slot * size : (slot + 1) * size, :] = tr_ref[pl.ds(start, size), :].astype(BF)


def put_halves(value, keep_ref, send_ref, columns):
    half, size = keep_ref.shape[0], keep_ref.shape[1]
    for slot in range(half):
        keep_ref[slot, :, columns] = value[slot * size : (slot + 1) * size].astype(BF)
        send_ref[slot, :, columns] = value[(half + slot) * size : (half + slot + 1) * size].astype(BF)


def pick_group(dims, part, mid_ref, send_ref):
    steps, per_device, group = dims
    out_rows, in_rows = send_ref.shape[0], mid_ref.shape[0]
    out = lax.broadcasted_iota(jnp.int32, (out_rows, in_rows), 0)
    src = lax.broadcasted_iota(jnp.int32, (out_rows, in_rows), 1)
    owner, rest = out // (steps * group), lax.rem(out, steps * group)
    base = (rest // group) * (in_rows // steps) + owner * per_device + lax.rem(rest, group)
    pick = (src == base + part * group).astype(F32).astype(BF)
    send_ref[...] = nn(pick, mid_ref[...]).astype(BF)


def spatial_forward_kernel(
    dims, x_ref, w_ref, p_ref, mod_ref, gain_ref,
    mid_ref, send_ref, normed_ref, qkv_ref, att_ref, mixed_ref, mixed_scr,
):
    steps, heads, hd, per_device, group = dims
    rows = x_ref.shape[1]
    width = heads * hd
    gq, gk = column(gain_ref[0:1, :]), column(gain_ref[1:2, :])
    for step in range(steps):
        x = x_ref[step].astype(F32)
        normed = modulated(x, mod_ref)
        normed_ref.put(step, normed)
        qkv_ref.put(step, nt(w_ref[...], normed))
        for head in range(heads):
            q, k, v = head_parts(qkv_ref.ref(step), head, hd, width)
            weights = head_weights(unit_rms(q)[0], unit_rms(k)[0], gq, gk, None, hd)
            att_ref[step, head] = weights
            mixed_scr[head * hd : (head + 1) * hd, :] = nn(v.astype(BF), weights)
        att_ref.flush(step)
        mixed = mixed_scr[...].astype(BF)
        mixed_ref[:, step * rows : (step + 1) * rows] = mixed
        mixed_ref.flush(step)
        mid_ref[step * rows : (step + 1) * rows, :] = (
            x + mod_ref[2:3, :] * tn(mixed, p_ref[...])
        ).astype(BF)
    mid_ref.flush()
    pick_group((steps, per_device, group), 0, mid_ref, send_ref)


def between_kernel(
    dims, me_ref, mid_ref, normed_ref, cot_ref, p_ref, mod_ref,
    send_ref, lhs_ref, turned_ref, branch_ref, grad_ref, tr_scr,
):
    steps, per_device, group, count = dims
    pick_group((steps, per_device, group), 1, mid_ref, send_ref)
    send_ref.flush()
    out_rows, in_rows = turned_ref.shape[1], cot_ref.shape[0]
    out = lax.broadcasted_iota(jnp.int32, (out_rows, in_rows), 0)
    src = lax.broadcasted_iota(jnp.int32, (out_rows, in_rows), 1)
    base = (out // group) * per_device + lax.rem(out, group)
    for part in range(turned_ref.shape[0]):
        turned = nn((src == base + part * group).astype(F32).astype(BF), cot_ref[...])
        turned_ref.put(part, turned.astype(BF))
        branch = (mod_ref[2:3, :] * turned).astype(BF)
        branch_ref.put(part, branch)
        grad_ref.put(part, nt(p_ref[...], branch))
    rows = normed_ref.shape[1]
    for step in range(steps):
        tr_scr[:, step * rows : (step + 1) * rows] = normed_ref[step].astype(F32).T
    arrange(tr_scr, lhs_ref, me_ref[0], count)


def temporal_kernel(
    dims, part, mid_ref, turned_ref, grad_ref, w_ref, mod_ref, gain_ref,
    dmid_ref, normed_ref, dqkv_ref, mixed_ref, qkv_scr, mixed_scr, dqkv_scr,
):
    heads, hd, group = dims
    width = heads * hd
    rows = mid_ref.shape[0]
    x = mid_ref[...].astype(F32)
    normed = modulated(x, mod_ref)
    normed_ref.put(..., normed)
    qkv_scr[...] = nt(w_ref[...], normed)
    gq, gk = column(gain_ref[0:1, :]), column(gain_ref[1:2, :])
    mask = same_column(rows, group) if group > 1 else None
    for head in range(heads):
        q, k, v = head_parts(qkv_scr, head, hd, width)
        at = head * hd
        v16 = v.astype(BF)
        weights = head_weights(unit_rms(q)[0], unit_rms(k)[0], gq, gk, mask, hd)
        mixed_scr[at : at + hd, :] = nn(v16, weights)
        grad16 = grad_ref[0, at : at + hd, :].astype(BF)
        d_q, d_k = score_vjp(q, k, v16, weights, grad16, gq, gk, hd)
        dqkv_scr[at : at + hd, :] = d_q
        dqkv_scr[width + at : width + at + hd, :] = d_k
        dqkv_scr[2 * width + at : 2 * width + at + hd, :] = nt(grad16, weights)
    mixed_ref.put(..., mixed_scr[...].astype(BF))
    dqkv = dqkv_scr[...].astype(BF)
    dqkv_ref.put(..., dqkv)
    grad = modulate_vjp(x, mod_ref, tn(dqkv, w_ref[...]))
    dmid_ref[...] = (turned_ref[0].astype(F32) + grad).astype(BF)


def temporal_grad_kernel(
    dims, me_ref, normed0_ref, normed1_ref, dqkv0_ref, dqkv1_ref, mixed0_ref, mixed1_ref,
    branch_ref, keep_ref, send_ref,
    tr_scr, lhs_scr, dqkv_scr, mixed_scr,
):
    width, count = dims
    rows = normed0_ref.shape[0]
    for part, (normed, dqkv, mixed) in enumerate(
        ((normed0_ref, dqkv0_ref, mixed0_ref), (normed1_ref, dqkv1_ref, mixed1_ref))
    ):
        at = slice(part * rows, (part + 1) * rows)
        tr_scr[:, at] = normed[...].astype(F32).T
        dqkv_scr[:, at] = dqkv[...]
        mixed_scr[:, at] = mixed[...]
    arrange(tr_scr, lhs_scr, me_ref[0], count)
    put_halves(nt(lhs_scr[...], dqkv_scr[...]), keep_ref, send_ref, slice(0, 3 * width))
    for part in range(2):
        tr_scr[:, part * rows : (part + 1) * rows] = branch_ref[part].astype(F32).T
    arrange(tr_scr, lhs_scr, me_ref[0], count)
    put_halves(nt(lhs_scr[...], mixed_scr[...]), keep_ref, send_ref, slice(3 * width, 4 * width))


def result_kernel(
    dims, mid0_ref, mid1_ref, mixed0_ref, mixed1_ref, p_ref, mod_ref, out_ref, scr
):
    per_device, group = dims
    rows = mid0_ref.shape[0]
    for part, (mid, mixed) in enumerate(((mid0_ref, mixed0_ref), (mid1_ref, mixed1_ref))):
        scr[part * rows : (part + 1) * rows, :] = (
            mid[...].astype(F32) + mod_ref[2:3, :] * tn(mixed[...], p_ref[...])
        ).astype(BF)
    out_rows = out_ref.shape[0]
    out = lax.broadcasted_iota(jnp.int32, (out_rows, out_rows), 0)
    src = lax.broadcasted_iota(jnp.int32, (out_rows, out_rows), 1)
    col = lax.rem(out, per_device)
    base = (col // group) * rows + (out // per_device) * group + lax.rem(col, group)
    out_ref[...] = nn((src == base).astype(F32).astype(BF), scr[...]).astype(BF)


def spatial_value_kernel(
    dims, me_ref, recv0_ref, recv1_ref, att_ref, p_ref, mod_ref, lhs_ref, mixed_ref,
    dmid_ref, grad_ref, dv_ref, keep_ref, send_ref,
    grad_scr, dv_scr, tr_scr, lhs_scr,
):
    heads, hd, steps, per_device, group, count = dims
    width = heads * hd
    rows, in_rows = dmid_ref.shape[1], recv0_ref.shape[0]
    out = lax.broadcasted_iota(jnp.int32, (rows, in_rows), 0)
    src = lax.broadcasted_iota(jnp.int32, (rows, in_rows), 1)
    owner, col = out // per_device, lax.rem(out, per_device)
    for step in range(steps):
        base = owner * (steps * group) + step * group + lax.rem(col, group)
        part = jnp.where(src == base, col // group, -1)
        dmid = nn((part == 0).astype(F32).astype(BF), recv0_ref[...])
        dmid += nn((part == 1).astype(F32).astype(BF), recv1_ref[...])
        dmid_ref.put(step, dmid.astype(BF))
        branch = (mod_ref[2:3, :] * dmid).astype(BF)
        here = slice(step * rows, (step + 1) * rows)
        tr_scr[:, here] = branch.astype(F32).T
        grad_scr[...] = nt(p_ref[...], branch)
        grad_ref.put(step, grad_scr[...].astype(BF))
        for head in range(heads):
            at = slice(head * hd, (head + 1) * hd)
            dv_scr[at, :] = nt(grad_scr[at, :].astype(BF), att_ref[step, head])
        dv_ref[:, here] = dv_scr[...].astype(BF)
        dv_ref.flush(step)
    put_halves(nt(lhs_ref[...], dv_ref[...]), keep_ref, send_ref, slice(0, width))
    arrange(tr_scr, lhs_scr, me_ref[0], count)
    put_halves(nt(lhs_scr[...], mixed_ref[...]), keep_ref, send_ref, slice(width, 2 * width))


def spatial_score_kernel(
    dims, qkv_ref, att_ref, grad_ref, gain_ref, lhs_ref,
    dqk_ref, keep_ref, send_ref, dqk_scr,
):
    heads, hd, steps = dims
    width = heads * hd
    rows = qkv_ref.shape[2]
    gq, gk = column(gain_ref[0:1, :]), column(gain_ref[1:2, :])
    for step in range(steps):
        for head in range(heads):
            q, k, v = head_parts(qkv_ref.ref(step), head, hd, width)
            at = head * hd
            grad16 = grad_ref[step, at : at + hd, :]
            d_q, d_k = score_vjp(q, k, v.astype(BF), att_ref[step, head], grad16, gq, gk, hd)
            dqk_scr[at : at + hd, :] = d_q
            dqk_scr[width + at : width + at + hd, :] = d_k
        dqk_ref[:, step * rows : (step + 1) * rows] = dqk_scr[...].astype(BF)
        dqk_ref.flush(step)
    put_halves(nt(lhs_ref[...], dqk_ref[...]), keep_ref, send_ref, slice(None))


def grad_clip_kernel(x_ref, dmid_ref, dqk_ref, dv_ref, w_ref, mod_ref, out_ref):
    cut = dqk_ref.shape[0]
    for step in range(x_ref.shape[0]):
        grad = tn(dqk_ref.lanes(step), w_ref[:cut, :]) + tn(dv_ref.lanes(step), w_ref[cut:, :])
        grad = modulate_vjp(x_ref[step].astype(F32), mod_ref, grad)
        out_ref.put(step, (dmid_ref[step].astype(F32) + grad).astype(BF))


def shape(dims, kind=BF):
    return jax.ShapeDtypeStruct(tuple(dims), kind)


def whole(array):
    n = len(array.shape)
    return pl.BlockSpec(array.shape, lambda *_: (0,) * n, pipeline_mode=pl.Buffered(1))


def each(array):
    pass


def lane(array):
    pass


def scalar(array):
    return pl.BlockSpec(memory_space=pltpu.SMEM)


def unused(array):
    return pl.BlockSpec(memory_space=pl.ANY)


def small_call(kernel, grid, ins, outs, scratch, micros, after=()):
    first, arrays = len(ins), [a for a, _ in ins]

    def run(*refs):
        kernel(*refs[:first], *refs[first + len(after) :])

    return pl.pallas_call(
        run,
        grid=grid,
        in_specs=[s(a) for a, s in ins] + [unused(a) for a in after],
        out_specs=[s(a) for a, s in outs],
        out_shape=[a for a, _ in outs],
        scratch_shapes=[pltpu.VMEM(d, k) for d, k in scratch],
        compiler_params=pltpu.CompilerParams(vmem_limit_bytes=SMALL_LIMIT),
        cost_estimate=pl.CostEstimate(
            flops=int(micros * FLOPS_PER_MICRO), bytes_accessed=0, transcendentals=0
        ),
    )(*arrays, *after)


class Source:
    def __init__(self, hbm, buf, pairs, sems, first):
        self.buf, self.shape = buf, buf.shape
        self.copies = [pltpu.make_async_copy(a, b, sems.at[first + i]) for i, (a, b) in enumerate(pairs)]
        self.waiting = set(range(len(self.copies)))

    def wait(self, index):
        wanted = [index] if isinstance(index, int) and len(self.copies) > 1 else range(len(self.copies))
        for i in wanted:
            if i in self.waiting:
                self.copies[i].wait()
                self.waiting.remove(i)

    def __getitem__(self, index):
        self.wait(index[0] if isinstance(index, tuple) else index)
        return self.buf[index]

    def ref(self, index):
        self.wait(index)
        return self.buf.at[index]

    def lanes(self, index):
        self.wait(index)
        size = self.shape[1] // len(self.copies)
        return self.buf[:, index * size : (index + 1) * size]


class Sink:
    def __init__(self, hbm, buf, pairs, sems, first):
        self.buf, self.shape = buf, buf.shape
        self.copies = [pltpu.make_async_copy(b, a, sems.at[first + i]) for i, (a, b) in enumerate(pairs)]
        self.left = set(range(len(self.copies)))

    def __getitem__(self, index):
        return self.buf[index]

    def __setitem__(self, index, value):
        self.buf[index] = value

    def ref(self, index):
        return self.buf.at[index]

    def flush(self, index=None):
        for i in sorted(self.left) if index is None else [index]:
            self.copies[i].start()
            self.left.remove(i)

    def put(self, index, value):
        self.buf[index] = value
        self.flush(index if len(self.copies) > 1 else None)


def cuts(hbm, buf, kind, steps):
    if kind is each:
        return [(hbm.at[i], buf.at[i]) for i in range(buf.shape[0])]
    if kind is lane:
        size = buf.shape[1] // steps
        return [(hbm.at[:, pl.ds(i * size, size)], buf.at[:, pl.ds(i * size, size)]) for i in range(steps)]
    if isinstance(kind, int):
        return [(hbm.at[pl.ds(kind, 1)], buf)]
    if isinstance(kind, tuple):
        size = buf.shape[1]
        return [(hbm.at[:, pl.ds(kind[0] * size, size)], buf)]
    return [(hbm, buf)]


def count_cuts(array, kind, steps):
    return array.shape[0] if kind is each else steps if kind is lane else 1


def call(kernel, steps, ins, outs, scratch, micros, after=(), aliases=None):
    arrays = [a for a, _ in ins]
    moved = [(a, k) for a, k in ins if k is not scalar]
    first_of, total = [], 0
    for a, k in moved + list(outs):
        first_of.append(total)
        total += count_cuts(a, k, steps)

    def buffer(array, kind):
        dims = tuple(array.shape)
        if isinstance(kind, int):
            dims = (1,) + dims[1:]
        if isinstance(kind, tuple):
            dims = (dims[0], dims[1] // steps)
        return pltpu.VMEM(dims, array.dtype)

    def run(*refs):
        given, refs = refs[: len(ins)], refs[len(ins) + len(after) :]
        results, refs = refs[: len(outs)], refs[len(outs) :]
        refs[0][...] = jnp.zeros_like(refs[0])
        refs = refs[1:]
        own, refs = refs[: len(scratch)], refs[len(scratch) :]
        sems, bufs = refs[-1], list(refs[:-1])
        firsts = list(first_of)
        sources = []
        for ref, (_, kind) in zip(given, ins):
            if kind is scalar:
                sources.append(ref)
            else:
                buf = bufs.pop(0)
                sources.append(Source(ref, buf, cuts(ref, buf, kind, steps), sems, firsts.pop(0)))
        sinks = []
        for ref, (_, kind) in zip(results, outs):
            buf = bufs.pop(0)
            sinks.append(Sink(ref, buf, cuts(ref, buf, kind, steps), sems, firsts.pop(0)))
        live = [x for x in sources if isinstance(x, Source)]
        live.sort(key=lambda x: math.prod(x.shape) > 16384)
        for i in range(max(len(x.copies) for x in live)):
            for x in live:
                if i < len(x.copies):
                    x.copies[i].start()
        kernel(*sources, *sinks, *own)
        for x in live:
            for i in sorted(x.waiting):
                x.copies[i].wait()
        for x in sinks:
            x.flush()
        for x in sinks:
            for copy in x.copies:
                copy.wait()

    return pl.pallas_call(
        run,
        in_specs=[scalar(a) if k is scalar else unused(a) for a, k in ins] + [unused(a) for a in after],
        out_specs=[unused(a) for a, _ in outs] + [pl.BlockSpec(memory_space=pltpu.VMEM)],
        out_shape=[a for a, _ in outs] + [shape((8, 128), F32)],
        input_output_aliases=aliases or {},
        scratch_shapes=[pltpu.VMEM(d, k) for d, k in scratch]
        + [buffer(a, k) for a, k in moved + list(outs)]
        + [pltpu.SemaphoreType.DMA((total,))],
        compiler_params=pltpu.CompilerParams(vmem_limit_bytes=VMEM_LIMIT),
        cost_estimate=pl.CostEstimate(
            flops=int(micros * FLOPS_PER_MICRO), bytes_accessed=0, transcendentals=0
        ),
    )(*arrays, *after)


def exchange(value, axis, flip):
    count = lax.axis_size(axis)
    return lax.ppermute(value, axis, [(i, i ^ flip) for i in range(count)])


def token_kernel(out_ref):
    out_ref[...] = jnp.zeros_like(out_ref)


def added(first, second):
    return first.astype(F32) + second.astype(F32)


def halve_kernel(picks, *refs):
    count = len(refs) - 2 * len(picks)
    terms, outs = refs[:count], refs[count:]
    for at, (pair, columns, kept, sent) in enumerate(picks):
        first, second = terms[pair], terms[pair + 1]
        for out_ref, blocks in ((outs[2 * at], kept), (outs[2 * at + 1], sent)):
            for slot, block in enumerate(blocks):
                out_ref[slot] = added(first[block, :, columns], second[block, :, columns]).astype(BF)


def halved_total(refs):
    return jnp.concatenate(
        [added(refs[i][0], refs[i + 1][0]) for i in range(0, len(refs), 2)], axis=1
    )


def stack_kernel(count, *refs):
    total, out_ref = halved_total(refs[:-1]), refs[-1]
    size = out_ref.shape[1]
    for i in range(count):
        out_ref[i] = total[i * size : (i + 1) * size].astype(BF)


def piece_kernel(count, place_ref, *refs):
    total, outs = halved_total(refs[:-count]), refs[-count:]
    size = outs[0].shape[0]
    pieces = [total[i * size : (i + 1) * size] for i in range(count)]
    place = place_ref[0]
    for flip, out_ref in enumerate(outs):
        value = pieces[0]
        for i in range(1, count):
            value = jnp.where(jnp.bitwise_xor(place, flip) == i, pieces[i], value)
        out_ref[...] = value.astype(BF)


def scaled_sum(terms, factor):
    return sum((t.astype(F32) for t in terms[1:]), terms[0].astype(F32)) * factor


def stacked_last_kernel(width, factor, terms_ref, qkv_ref, proj_ref):
    total = scaled_sum([terms_ref[i] for i in range(terms_ref.shape[0])], factor)
    qkv_ref[...] = total[:, : 3 * width]
    proj_ref[...] = total[:, 3 * width :]


def last_kernel(width, factor, *refs):
    terms, (qkv_ref, proj_ref) = refs[:-2], refs[-2:]
    half = len(terms) // 2
    qkv_ref[:, : 2 * width] = scaled_sum([r[...] for r in terms[:half]], factor)
    other = scaled_sum([r[...] for r in terms[half:]], factor)
    qkv_ref[:, 2 * width :] = other[:, :width]
    proj_ref[...] = other[:, width:]


class Halving:
    def __init__(self, keep, send, cut):
        bits = int(math.log2(lax.axis_size("wide"))) - 1
        self.terms = [keep, exchange(send, "wide", 1)]
        self.pairs = [(0, slice(0, cut)), (0, slice(cut, keep.shape[2]))]
        self.left = [list(range(bits))[::-1]] * 2
        self.orders = [list(range(bits)), list(range(bits))[::-1]]
        self.size = keep.shape[1]

    def pending(self):
        return bool(self.orders[0])

    def step(self, after=(), micros=0):
        picks, outs, flips = [], [], []
        for at, (pair, columns) in enumerate(self.pairs):
            bit, left = self.orders[at][0], self.left[at]
            shift = len(left) - 1 - left.index(bit)
            blocks = range(2 ** len(left))
            kept = [i for i in blocks if not (i >> shift) & 1]
            sent = [i for i in blocks if (i >> shift) & 1]
            picks.append((pair, columns, kept, sent))
            wide = len(range(*columns.indices(self.terms[pair].shape[2])))
            outs += [(shape((len(kept), self.size, wide)), whole)] * 2
            flips.append(2 << bit)
        got = small_call(
            functools.partial(halve_kernel, picks), (1,), [(a, whole) for a in self.terms],
            outs, [], micros, after,
        )
        self.terms = []
        for at, flip in enumerate(flips):
            self.terms += [got[2 * at], exchange(got[2 * at + 1], "wide", flip)]
            bit = self.orders[at][0]
            self.left[at] = [b for b in self.left[at] if b != bit]
            self.orders[at] = self.orders[at][1:]
        self.pairs = [(0, slice(None)), (2, slice(None))]
        self.done = got[0]

    def rest(self, after=(), micros=0):
        while self.pending():
            self.step(after, micros)


def body(
    clip_tokens,
    cotangent,
    qkv_spatial,
    proj_spatial,
    adaln_spatial,
    qknorm_spatial,
    qkv_temporal,
    proj_temporal,
    adaln_temporal,
    qknorm_temporal,
):
    steps, patches, depth = clip_tokens.shape
    frames, per_device, _ = cotangent.shape
    hd = qknorm_spatial.shape[1]
    width = proj_spatial.shape[1]
    heads = width // hd
    axes = ("wide", "narrow")
    count = lax.axis_size("wide")
    devices = count * lax.axis_size("narrow")
    parts = 2
    group = per_device // parts
    rows = frames * group
    tokens = steps * patches
    w_s, p_s, w_t, p_t = qkv_spatial.T, proj_spatial.T, qkv_temporal.T, proj_temporal.T
    me = lax.axis_index("wide").astype(jnp.int32).reshape(1)
    half = shape((count // 2, depth // count, 2 * width))
    both = shape((count // 2, depth // count, 4 * width))

    middle, send0, normed_s, qkv_s, att_s, mixed_s, _ = call(
        functools.partial(spatial_forward_kernel, (steps, heads, hd, per_device, group)),
        steps,
        [(clip_tokens, each), (w_s, whole), (p_s, whole), (adaln_spatial, whole),
         (qknorm_spatial, whole)],
        [(shape((tokens, depth)), whole), (shape((rows, depth)), whole),
         (shape((steps, patches, depth)), each),
         (shape((steps, 3 * width, patches), F32), each),
         (shape((steps, heads, patches, patches)), each), (shape((width, tokens)), lane)],
        [((width, patches), F32)],
        17,
    )

    def turn(value):
        value = value.reshape(devices, steps * group, depth)
        value = lax.all_to_all(value, axes, split_axis=0, concat_axis=0, tiled=True)
        return value.reshape(rows, depth)

    flat_cot = cotangent.reshape(frames * per_device, depth)
    send1, lhs_s, turned, branch_t, dmixed_t, _ = call(
        functools.partial(between_kernel, (steps, per_device, group, count)),
        steps,
        [(me, scalar), (middle, whole), (normed_s, whole), (flat_cot, whole), (p_t, whole),
         (adaln_temporal, whole)],
        [(shape((rows, depth)), whole), (shape((depth, tokens)), whole),
         (shape((parts, rows, depth)), each), (shape((parts, rows, depth)), each),
         (shape((parts, width, rows), F32), each)],
        [((depth, tokens), F32)],
        6,
    )
    middles = [turn(send0), turn(send1)]

    received, saved = [], []
    for part in range(parts):
        dmid, *keep, _ = call(
            functools.partial(temporal_kernel, (heads, hd, group), part),
            (1,),
            [(middles[part], whole), (turned, part), (dmixed_t, part), (w_t, whole),
             (adaln_temporal, whole), (qknorm_temporal, whole)],
            [(shape((rows, depth)), whole), (shape((rows, depth)), whole),
             (shape((3 * width, rows)), whole), (shape((width, rows)), whole)],
            [((3 * width, rows), F32), ((width, rows), F32), ((3 * width, rows), F32)],
            13,
        )
        received.append(turn(dmid))
        saved.append(keep)
    (normed0, dqkv0, mixed0), (normed1, dqkv1, mixed1) = saved

    keep_t, send_t, done_t = call(
        functools.partial(temporal_grad_kernel, (width, count)),
        steps,
        [(me, scalar), (normed0, whole), (normed1, whole), (dqkv0, whole), (dqkv1, whole),
         (mixed0, whole), (mixed1, whole), (branch_t, whole)],
        [(both, whole)] * 2,
        [((depth, parts * rows), F32), ((depth, parts * rows), BF),
         ((3 * width, parts * rows), BF), ((width, parts * rows), BF)],
        0,
        [received[0]],
    )
    result, done_result = call(
        functools.partial(result_kernel, (per_device, group)),
        steps,
        [(middles[0], whole), (middles[1], whole), (mixed0, whole), (mixed1, whole), (p_t, whole),
         (adaln_temporal, whole)],
        [(shape((frames * per_device, depth)), whole)],
        [((parts * rows, depth), BF)],
        0,
        [done_t],
    )
    token = pl.pallas_call(
        lambda *refs: token_kernel(refs[-1]),
        in_specs=[pl.BlockSpec(memory_space=pl.ANY)] * 2,
        out_specs=pl.BlockSpec(memory_space=pltpu.VMEM),
        out_shape=shape((8, 128), F32),
        cost_estimate=pl.CostEstimate(
            flops=int(40 * FLOPS_PER_MICRO), bytes_accessed=0, transcendentals=0
        ),
    )(received[1], done_result)
    sum_t = Halving(keep_t, send_t, 2 * width)
    sum_t.step([token])
    dmid_s, dmixed_s, dv_s, keep_b, send_b, done_v = call(
        functools.partial(spatial_value_kernel, (heads, hd, steps, per_device, group, count)),
        steps,
        [(me, scalar), (received[0], whole), (received[1], whole), (att_s, each), (p_s, whole),
         (adaln_spatial, whole), (lhs_s, whole), (mixed_s, whole)],
        [(shape((steps, patches, depth)), each), (shape((steps, width, patches)), each),
         (shape((width, tokens)), lane), (half, whole), (half, whole)],
        [((width, patches), F32), ((width, patches), F32),
         ((depth, tokens), F32), ((depth, tokens), BF)],
        10,
        [sum_t.done],
    )
    cut = 128 * -(-2 * width // 256)
    sum_t.rest([done_v], 20)
    sum_b = Halving(keep_b, send_b, cut)
    sum_b.step([sum_t.done])
    dqk_s, keep_a, send_a, done_s = call(
        functools.partial(spatial_score_kernel, (heads, hd, steps)),
        steps,
        [(qkv_s, each), (att_s, each), (dmixed_s, each), (qknorm_spatial, whole), (lhs_s, whole)],
        [(shape((2 * width, tokens)), lane), (half, whole), (half, whole)],
        [((2 * width, patches), F32)],
        11,
        [sum_b.done],
    )
    narrow = lax.axis_size("narrow")
    factor = 1.0 / math.sqrt(frames * patches)
    share = depth // devices
    place = lax.axis_index("narrow").astype(jnp.int32).reshape(1)

    def pieces_of(total, after):
        pieces = small_call(
            functools.partial(piece_kernel, narrow), (1,),
            [(place, scalar)] + [(a, whole) for a in total.terms],
            [(shape((share, 2 * width)), whole)] * narrow, [], 20, after,
        )
        return pieces[0], [exchange(p, "narrow", i) if i else p for i, p in enumerate(pieces)]

    def clip_step(step, earlier, after):
        aliases = {6: 0} if earlier else {}
        return call(
            lambda *refs: grad_clip_kernel(*refs[:6], refs[-1]),
            steps,
            [(clip_tokens, step), (dmid_s, step), (dqk_s, (step,)), (dv_s, (step,)),
             (w_s, whole), (adaln_spatial, whole)],
            [(shape((steps, patches, depth)), step)],
            [],
            4,
            list(earlier) + list(after),
            aliases,
        )

    (stack,) = small_call(
        functools.partial(stack_kernel, narrow), (1,), [(a, whole) for a in sum_t.terms],
        [(shape((narrow, share, 4 * width)), whole)], [], 20, [done_s],
    )
    stack_terms = lax.all_to_all(stack, "narrow", split_axis=0, concat_axis=0, tiled=True)
    sum_b.rest([stack])
    sum_a = Halving(keep_a, send_a, cut)
    sum_a.step([sum_b.done])
    grad_clip, done_clip = clip_step(0, (), [sum_a.done])
    first_b, terms_b = pieces_of(sum_b, [done_clip])
    sum_a.rest([first_b])
    after = sum_a.done
    for step in range(1, steps):
        grad_clip, done_clip = clip_step(step, [grad_clip], [after])
        after = done_clip
    first_a, terms_a = pieces_of(sum_a, [done_clip])
    whole_grad, part_grad = shape((share, 3 * width), F32), shape((share, width), F32)
    grad_qkv_t, grad_proj_t = small_call(
        functools.partial(stacked_last_kernel, width, factor), (1,), [(stack_terms, whole)],
        [(whole_grad, whole), (part_grad, whole)], [], 2, [first_a],
    )
    grad_qkv_s, grad_proj_s = small_call(
        functools.partial(last_kernel, width, factor), (1,),
        [(a, whole) for a in terms_a + terms_b],
        [(whole_grad, whole), (part_grad, whole)], [], 2,
    )
    return (
        result.reshape(frames, per_device, depth),
        grad_clip,
        grad_qkv_s,
        grad_proj_s,
        grad_qkv_t,
        grad_proj_t,
    )


def solution(mesh):
    tokens = P(("wide", "narrow"), None, None)
    columns = P(None, ("wide", "narrow"), None)
    own = P(("wide", "narrow"), None)
    return jax.shard_map(
        body,
        mesh=mesh,
        in_specs=(tokens, columns) + (P(),) * 8,
        out_specs=(columns, tokens, own, own, own, own),
        check_vma=False,
    )
```

```python
import functools
import math

import jax
import jax.numpy as jnp
from jax import lax
from jax.experimental import pallas as pl
from jax.experimental.pallas import tpu as pltpu
from jax.sharding import PartitionSpec as P

EPS = 1e-06
BF = jnp.bfloat16
F32 = jnp.float32
VMEM_LIMIT = 56 * 1024 * 1024
SMALL_LIMIT = 24 * 1024 * 1024
FLOPS_PER_MICRO = 1.15e9
LOG2E = math.log2(math.e)


def nn(a, b):
    return lax.dot_general(a, b, (((1,), (0,)), ((), ())), preferred_element_type=F32)


def nt(a, b):
    return lax.dot_general(a, b, (((1,), (1,)), ((), ())), preferred_element_type=F32)


def tn(a, b):
    return lax.dot_general(a, b, (((0,), (0,)), ((), ())), preferred_element_type=F32)


def standardize(x):
    centre = x - jnp.mean(x, axis=-1, keepdims=True)
    rate = lax.rsqrt(jnp.mean(centre * centre, axis=-1, keepdims=True) + EPS)
    return centre * rate, rate


def modulated(x, mod_ref):
    return (standardize(x)[0] * (1.0 + mod_ref[1:2, :]) + mod_ref[0:1, :]).astype(BF)


def modulate_vjp(x, mod_ref, grad):
    unit, rate = standardize(x)
    scaled = grad * (1.0 + mod_ref[1:2, :])
    inner = jnp.mean(unit * scaled, axis=-1, keepdims=True)
    return rate * (scaled - jnp.mean(scaled, axis=-1, keepdims=True) - unit * inner)


def column(row):
    n = row.shape[1]
    same = lax.broadcasted_iota(jnp.int32, (n, n), 0) == lax.broadcasted_iota(jnp.int32, (n, n), 1)
    return jnp.sum(jnp.where(same, jnp.broadcast_to(row, (n, n)), 0.0), axis=1, keepdims=True)


def unit_rms(vectors):
    rate = lax.rsqrt(jnp.mean(vectors * vectors, axis=0, keepdims=True) + EPS)
    return vectors * rate, rate


def same_column(rows, stride):
    first = lax.broadcasted_iota(jnp.int32, (rows, rows), 0)
    second = lax.broadcasted_iota(jnp.int32, (rows, rows), 1)
    return lax.rem(first, stride) == lax.rem(second, stride)


def head_parts(qkv_ref, head, hd, width):
    at = head * hd
    return (
        qkv_ref[at : at + hd, :],
        qkv_ref[width + at : width + at + hd, :],
        qkv_ref[2 * width + at : 2 * width + at + hd, :],
    )


def head_weights(q_unit, k_unit, gq, gk, mask, hd):
    qn = (q_unit * (gq * (LOG2E / math.sqrt(hd)))).astype(BF)
    kn = (k_unit * gk).astype(BF)
    weights = jnp.exp2(tn(kn, qn))
    if mask is not None:
        weights = jnp.where(mask, weights, 0.0)
    return (weights * (1.0 / jnp.sum(weights, axis=0, keepdims=True))).astype(BF)


def score_vjp(q, k, v16, weights, grad16, gq, gk, hd):
    q_unit, q_rate = unit_rms(q)
    k_unit, k_rate = unit_rms(k)
    scale = 1.0 / math.sqrt(hd)
    w32 = weights.astype(F32)
    weighted = w32 * tn(v16, grad16)
    d_s = (weighted - w32 * jnp.sum(weighted, axis=0, keepdims=True)).astype(BF)
    d_q = nn((k_unit * gk).astype(BF), d_s) * (gq * scale)
    d_k = nt((q_unit * gq).astype(BF), d_s) * (gk * scale)
    d_q = q_rate * (d_q - q_unit * jnp.mean(q_unit * d_q, axis=0, keepdims=True))
    d_k = k_rate * (d_k - k_unit * jnp.mean(k_unit * d_k, axis=0, keepdims=True))
    return d_q, d_k


def arrange(tr_ref, lhs_ref, me, count):
    size = lhs_ref.shape[0] // count
    for slot in range(count):
        place = (slot % (count // 2)) * 2 + slot // (count // 2)
        start = pl.multiple_of(jnp.bitwise_xor(me, place) * size, 8)
        lhs_ref[slot * size : (slot + 1) * size, :] = tr_ref[pl.ds(start, size), :].astype(BF)


def put_halves(value, keep_ref, send_ref, columns):
    half, size = keep_ref.shape[0], keep_ref.shape[1]
    for slot in range(half):
        keep_ref[slot, :, columns] = value[slot * size : (slot + 1) * size].astype(BF)
        send_ref[slot, :, columns] = value[(half + slot) * size : (half + slot + 1) * size].astype(BF)


def pick_group(dims, part, mid_ref, send_ref):
    steps, per_device, group = dims
    out_rows, in_rows = send_ref.shape[0], mid_ref.shape[0]
    out = lax.broadcasted_iota(jnp.int32, (out_rows, in_rows), 0)
    src = lax.broadcasted_iota(jnp.int32, (out_rows, in_rows), 1)
    owner, rest = out // (steps * group), lax.rem(out, steps * group)
    base = (rest // group) * (in_rows // steps) + owner * per_device + lax.rem(rest, group)
    pick = (src == base + part * group).astype(F32).astype(BF)
    send_ref[...] = nn(pick, mid_ref[...]).astype(BF)


def spatial_forward_kernel(
    dims, x_ref, w_ref, p_ref, mod_ref, gain_ref,
    mid_ref, send_ref, normed_ref, qkv_ref, att_ref, mixed_ref, mixed_scr,
):
    steps, heads, hd, per_device, group = dims
    rows = x_ref.shape[1]
    width = heads * hd
    gq, gk = column(gain_ref[0:1, :]), column(gain_ref[1:2, :])
    for step in range(steps):
        x = x_ref[step].astype(F32)
        normed = modulated(x, mod_ref)
        normed_ref.put(step, normed)
        qkv_ref.put(step, nt(w_ref[...], normed))
        for head in range(heads):
            q, k, v = head_parts(qkv_ref.ref(step), head, hd, width)
            weights = head_weights(unit_rms(q)[0], unit_rms(k)[0], gq, gk, None, hd)
            att_ref[step, head] = weights
            mixed_scr[head * hd : (head + 1) * hd, :] = nn(v.astype(BF), weights)
        att_ref.flush(step)
        mixed = mixed_scr[...].astype(BF)
        mixed_ref[:, step * rows : (step + 1) * rows] = mixed
        mixed_ref.flush(step)
        mid_ref[step * rows : (step + 1) * rows, :] = (
            x + mod_ref[2:3, :] * tn(mixed, p_ref[...])
        ).astype(BF)
    mid_ref.flush()
    pick_group((steps, per_device, group), 0, mid_ref, send_ref)


def between_kernel(
    dims, me_ref, mid_ref, normed_ref, cot_ref, p_ref, mod_ref,
    send_ref, lhs_ref, turned_ref, branch_ref, grad_ref, tr_scr,
):
    steps, per_device, group, count = dims
    pick_group((steps, per_device, group), 1, mid_ref, send_ref)
    send_ref.flush()
    out_rows, in_rows = turned_ref.shape[1], cot_ref.shape[0]
    out = lax.broadcasted_iota(jnp.int32, (out_rows, in_rows), 0)
    src = lax.broadcasted_iota(jnp.int32, (out_rows, in_rows), 1)
    base = (out // group) * per_device + lax.rem(out, group)
    for part in range(turned_ref.shape[0]):
        turned = nn((src == base + part * group).astype(F32).astype(BF), cot_ref[...])
        turned_ref.put(part, turned.astype(BF))
        branch = (mod_ref[2:3, :] * turned).astype(BF)
        branch_ref.put(part, branch)
        grad_ref.put(part, nt(p_ref[...], branch))
    rows = normed_ref.shape[1]
    for step in range(steps):
        tr_scr[:, step * rows : (step + 1) * rows] = normed_ref[step].astype(F32).T
    arrange(tr_scr, lhs_ref, me_ref[0], count)


def temporal_kernel(
    dims, part, mid_ref, turned_ref, grad_ref, w_ref, mod_ref, gain_ref,
    dmid_ref, normed_ref, dqkv_ref, mixed_ref, qkv_scr, mixed_scr, dqkv_scr,
):
    heads, hd, group = dims
    width = heads * hd
    rows = mid_ref.shape[0]
    x = mid_ref[...].astype(F32)
    normed = modulated(x, mod_ref)
    normed_ref.put(..., normed)
    qkv_scr[...] = nt(w_ref[...], normed)
    gq, gk = column(gain_ref[0:1, :]), column(gain_ref[1:2, :])
    mask = same_column(rows, group) if group > 1 else None
    for head in range(heads):
        q, k, v = head_parts(qkv_scr, head, hd, width)
        at = head * hd
        v16 = v.astype(BF)
        weights = head_weights(unit_rms(q)[0], unit_rms(k)[0], gq, gk, mask, hd)
        mixed_scr[at : at + hd, :] = nn(v16, weights)
        grad16 = grad_ref[0, at : at + hd, :].astype(BF)
        d_q, d_k = score_vjp(q, k, v16, weights, grad16, gq, gk, hd)
        dqkv_scr[at : at + hd, :] = d_q
        dqkv_scr[width + at : width + at + hd, :] = d_k
        dqkv_scr[2 * width + at : 2 * width + at + hd, :] = nt(grad16, weights)
    mixed_ref.put(..., mixed_scr[...].astype(BF))
    dqkv = dqkv_scr[...].astype(BF)
    dqkv_ref.put(..., dqkv)
    grad = modulate_vjp(x, mod_ref, tn(dqkv, w_ref[...]))
    dmid_ref[...] = (turned_ref[0].astype(F32) + grad).astype(BF)


def temporal_grad_kernel(
    dims, me_ref, normed0_ref, normed1_ref, dqkv0_ref, dqkv1_ref, mixed0_ref, mixed1_ref,
    branch_ref, keep_ref, send_ref,
    tr_scr, lhs_scr, dqkv_scr, mixed_scr,
):
    width, count = dims
    rows = normed0_ref.shape[0]
    for part, (normed, dqkv, mixed) in enumerate(
        ((normed0_ref, dqkv0_ref, mixed0_ref), (normed1_ref, dqkv1_ref, mixed1_ref))
    ):
        at = slice(part * rows, (part + 1) * rows)
        tr_scr[:, at] = normed[...].astype(F32).T
        dqkv_scr[:, at] = dqkv[...]
        mixed_scr[:, at] = mixed[...]
    arrange(tr_scr, lhs_scr, me_ref[0], count)
    put_halves(nt(lhs_scr[...], dqkv_scr[...]), keep_ref, send_ref, slice(0, 3 * width))
    for part in range(2):
        tr_scr[:, part * rows : (part + 1) * rows] = branch_ref[part].astype(F32).T
    arrange(tr_scr, lhs_scr, me_ref[0], count)
    put_halves(nt(lhs_scr[...], mixed_scr[...]), keep_ref, send_ref, slice(3 * width, 4 * width))


def result_kernel(
    dims, mid0_ref, mid1_ref, mixed0_ref, mixed1_ref, p_ref, mod_ref, out_ref, scr
):
    per_device, group = dims
    rows = mid0_ref.shape[0]
    for part, (mid, mixed) in enumerate(((mid0_ref, mixed0_ref), (mid1_ref, mixed1_ref))):
        scr[part * rows : (part + 1) * rows, :] = (
            mid[...].astype(F32) + mod_ref[2:3, :] * tn(mixed[...], p_ref[...])
        ).astype(BF)
    out_rows = out_ref.shape[0]
    out = lax.broadcasted_iota(jnp.int32, (out_rows, out_rows), 0)
    src = lax.broadcasted_iota(jnp.int32, (out_rows, out_rows), 1)
    col = lax.rem(out, per_device)
    base = (col // group) * rows + (out // per_device) * group + lax.rem(col, group)
    out_ref[...] = nn((src == base).astype(F32).astype(BF), scr[...]).astype(BF)


def spatial_value_kernel(
    dims, me_ref, recv0_ref, recv1_ref, att_ref, p_ref, mod_ref, lhs_ref, mixed_ref,
    dmid_ref, grad_ref, dv_ref, keep_ref, send_ref,
    grad_scr, dv_scr, tr_scr, lhs_scr,
):
    heads, hd, steps, per_device, group, count = dims
    width = heads * hd
    rows, in_rows = dmid_ref.shape[1], recv0_ref.shape[0]
    out = lax.broadcasted_iota(jnp.int32, (rows, in_rows), 0)
    src = lax.broadcasted_iota(jnp.int32, (rows, in_rows), 1)
    owner, col = out // per_device, lax.rem(out, per_device)
    for step in range(steps):
        base = owner * (steps * group) + step * group + lax.rem(col, group)
        part = jnp.where(src == base, col // group, -1)
        dmid = nn((part == 0).astype(F32).astype(BF), recv0_ref[...])
        dmid += nn((part == 1).astype(F32).astype(BF), recv1_ref[...])
        dmid_ref.put(step, dmid.astype(BF))
        branch = (mod_ref[2:3, :] * dmid).astype(BF)
        here = slice(step * rows, (step + 1) * rows)
        tr_scr[:, here] = branch.astype(F32).T
        grad_scr[...] = nt(p_ref[...], branch)
        grad_ref.put(step, grad_scr[...].astype(BF))
        for head in range(heads):
            at = slice(head * hd, (head + 1) * hd)
            dv_scr[at, :] = nt(grad_scr[at, :].astype(BF), att_ref[step, head])
        dv_ref[:, here] = dv_scr[...].astype(BF)
        dv_ref.flush(step)
    put_halves(nt(lhs_ref[...], dv_ref[...]), keep_ref, send_ref, slice(0, width))
    arrange(tr_scr, lhs_scr, me_ref[0], count)
    put_halves(nt(lhs_scr[...], mixed_ref[...]), keep_ref, send_ref, slice(width, 2 * width))


def spatial_score_kernel(
    dims, qkv_ref, att_ref, grad_ref, gain_ref, lhs_ref,
    dqk_ref, keep_ref, send_ref, dqk_scr,
):
    heads, hd, steps = dims
    width = heads * hd
    rows = qkv_ref.shape[2]
    gq, gk = column(gain_ref[0:1, :]), column(gain_ref[1:2, :])
    for step in range(steps):
        for head in range(heads):
            q, k, v = head_parts(qkv_ref.ref(step), head, hd, width)
            at = head * hd
            grad16 = grad_ref[step, at : at + hd, :]
            d_q, d_k = score_vjp(q, k, v.astype(BF), att_ref[step, head], grad16, gq, gk, hd)
            dqk_scr[at : at + hd, :] = d_q
            dqk_scr[width + at : width + at + hd, :] = d_k
        dqk_ref[:, step * rows : (step + 1) * rows] = dqk_scr[...].astype(BF)
        dqk_ref.flush(step)
    put_halves(nt(lhs_ref[...], dqk_ref[...]), keep_ref, send_ref, slice(None))


def grad_clip_kernel(x_ref, dmid_ref, dqk_ref, dv_ref, w_ref, mod_ref, out_ref):
    cut = dqk_ref.shape[0]
    for step in range(x_ref.shape[0]):
        grad = tn(dqk_ref.lanes(step), w_ref[:cut, :]) + tn(dv_ref.lanes(step), w_ref[cut:, :])
        grad = modulate_vjp(x_ref[step].astype(F32), mod_ref, grad)
        out_ref.put(step, (dmid_ref[step].astype(F32) + grad).astype(BF))


def shape(dims, kind=BF):
    return jax.ShapeDtypeStruct(tuple(dims), kind)


def whole(array):
    n = len(array.shape)
    return pl.BlockSpec(array.shape, lambda *_: (0,) * n, pipeline_mode=pl.Buffered(1))


def each(array):
    pass


def lane(array):
    pass


def scalar(array):
    return pl.BlockSpec(memory_space=pltpu.SMEM)


def unused(array):
    return pl.BlockSpec(memory_space=pl.ANY)


def small_call(kernel, grid, ins, outs, scratch, micros, after=()):
    first, arrays = len(ins), [a for a, _ in ins]

    def run(*refs):
        kernel(*refs[:first], *refs[first + len(after) :])

    return pl.pallas_call(
        run,
        grid=grid,
        in_specs=[s(a) for a, s in ins] + [unused(a) for a in after],
        out_specs=[s(a) for a, s in outs],
        out_shape=[a for a, _ in outs],
        scratch_shapes=[pltpu.VMEM(d, k) for d, k in scratch],
        compiler_params=pltpu.CompilerParams(vmem_limit_bytes=SMALL_LIMIT),
        cost_estimate=pl.CostEstimate(
            flops=int(micros * FLOPS_PER_MICRO), bytes_accessed=0, transcendentals=0
        ),
    )(*arrays, *after)


class Plain:
    def __init__(self, held):
        self.held, self.shape = held, held.shape

    def __getitem__(self, index):
        return self.held[index]

    def __setitem__(self, index, value):
        self.held[index] = value

    def put(self, index, value):
        self.held[index] = value

    def flush(self, index=None):
        pass


def block_call(kernel, ins, outs, scratch, micros, after=()):
    def spec(array, kind):
        if kind is scalar:
            return scalar(array)
        n = len(array.shape)
        if isinstance(kind, int):
            return pl.BlockSpec((1,) + tuple(array.shape[1:]), lambda i: (kind,) + (0,) * (n - 1))
        return pl.BlockSpec(tuple(array.shape), lambda i: (0,) * n)

    def run(*refs):
        given, refs = refs[: len(ins)], refs[len(ins) + len(after) :]
        results, own = refs[: len(outs)], refs[len(outs) + 1 :]
        refs[len(outs)][...] = jnp.zeros_like(refs[len(outs)])
        given = [r if k is scalar else Plain(r) for r, (_, k) in zip(given, ins)]
        kernel(*given, *[Plain(r) for r in results], *own)

    token = shape((8, 128), F32)
    return pl.pallas_call(
        run,
        grid=(1,),
        in_specs=[spec(a, k) for a, k in ins] + [unused(a) for a in after],
        out_specs=[spec(a, None) for a, _ in outs] + [spec(token, None)],
        out_shape=[a for a, _ in outs] + [token],
        scratch_shapes=[pltpu.VMEM(d, k) for d, k in scratch],
        compiler_params=pltpu.CompilerParams(vmem_limit_bytes=VMEM_LIMIT),
        cost_estimate=pl.CostEstimate(
            flops=int(micros * FLOPS_PER_MICRO), bytes_accessed=0, transcendentals=0
        ),
    )(*[a for a, _ in ins], *after)


class Source:
    def __init__(self, hbm, buf, pairs, sems, first):
        self.buf, self.shape = buf, buf.shape
        self.copies = [pltpu.make_async_copy(a, b, sems.at[first + i]) for i, (a, b) in enumerate(pairs)]
        self.waiting = set(range(len(self.copies)))

    def wait(self, index):
        wanted = [index] if isinstance(index, int) and len(self.copies) > 1 else range(len(self.copies))
        for i in wanted:
            if i in self.waiting:
                self.copies[i].wait()
                self.waiting.remove(i)

    def __getitem__(self, index):
        self.wait(index[0] if isinstance(index, tuple) else index)
        return self.buf[index]

    def ref(self, index):
        self.wait(index)
        return self.buf.at[index]

    def lanes(self, index):
        self.wait(index)
        size = self.shape[1] // len(self.copies)
        return self.buf[:, index * size : (index + 1) * size]


class Sink:
    def __init__(self, hbm, buf, pairs, sems, first):
        self.buf, self.shape = buf, buf.shape
        self.copies = [pltpu.make_async_copy(b, a, sems.at[first + i]) for i, (a, b) in enumerate(pairs)]
        self.left = set(range(len(self.copies)))

    def __getitem__(self, index):
        return self.buf[index]

    def __setitem__(self, index, value):
        self.buf[index] = value

    def ref(self, index):
        return self.buf.at[index]

    def flush(self, index=None):
        for i in sorted(self.left) if index is None else [index]:
            self.copies[i].start()
            self.left.remove(i)

    def put(self, index, value):
        self.buf[index] = value
        self.flush(index if len(self.copies) > 1 else None)


def cuts(hbm, buf, kind, steps):
    if kind is each:
        return [(hbm.at[i], buf.at[i]) for i in range(buf.shape[0])]
    if kind is lane:
        size = buf.shape[1] // steps
        return [(hbm.at[:, pl.ds(i * size, size)], buf.at[:, pl.ds(i * size, size)]) for i in range(steps)]
    if isinstance(kind, int):
        return [(hbm.at[pl.ds(kind, 1)], buf)]
    if isinstance(kind, tuple):
        size = buf.shape[1]
        return [(hbm.at[:, pl.ds(kind[0] * size, size)], buf)]
    return [(hbm, buf)]


def count_cuts(array, kind, steps):
    return array.shape[0] if kind is each else steps if kind is lane else 1


def call(kernel, steps, ins, outs, scratch, micros, after=(), aliases=None):
    arrays = [a for a, _ in ins]
    moved = [(a, k) for a, k in ins if k is not scalar]
    first_of, total = [], 0
    for a, k in moved + list(outs):
        first_of.append(total)
        total += count_cuts(a, k, steps)

    def buffer(array, kind):
        dims = tuple(array.shape)
        if isinstance(kind, int):
            dims = (1,) + dims[1:]
        if isinstance(kind, tuple):
            dims = (dims[0], dims[1] // steps)
        return pltpu.VMEM(dims, array.dtype)

    def run(*refs):
        given, refs = refs[: len(ins)], refs[len(ins) + len(after) :]
        results, refs = refs[: len(outs)], refs[len(outs) :]
        refs[0][...] = jnp.zeros_like(refs[0])
        refs = refs[1:]
        own, refs = refs[: len(scratch)], refs[len(scratch) :]
        sems, bufs = refs[-1], list(refs[:-1])
        firsts = list(first_of)
        sources = []
        for ref, (_, kind) in zip(given, ins):
            if kind is scalar:
                sources.append(ref)
            else:
                buf = bufs.pop(0)
                sources.append(Source(ref, buf, cuts(ref, buf, kind, steps), sems, firsts.pop(0)))
        sinks = []
        for ref, (_, kind) in zip(results, outs):
            buf = bufs.pop(0)
            sinks.append(Sink(ref, buf, cuts(ref, buf, kind, steps), sems, firsts.pop(0)))
        live = [x for x in sources if isinstance(x, Source)]
        live.sort(key=lambda x: math.prod(x.shape) > 16384)
        for i in range(max(len(x.copies) for x in live)):
            for x in live:
                if i < len(x.copies):
                    x.copies[i].start()
        kernel(*sources, *sinks, *own)
        for x in live:
            for i in sorted(x.waiting):
                x.copies[i].wait()
        for x in sinks:
            x.flush()
        for x in sinks:
            for copy in x.copies:
                copy.wait()

    return pl.pallas_call(
        run,
        in_specs=[scalar(a) if k is scalar else unused(a) for a, k in ins] + [unused(a) for a in after],
        out_specs=[unused(a) for a, _ in outs] + [pl.BlockSpec(memory_space=pltpu.VMEM)],
        out_shape=[a for a, _ in outs] + [shape((8, 128), F32)],
        input_output_aliases=aliases or {},
        scratch_shapes=[pltpu.VMEM(d, k) for d, k in scratch]
        + [buffer(a, k) for a, k in moved + list(outs)]
        + [pltpu.SemaphoreType.DMA((total,))],
        compiler_params=pltpu.CompilerParams(vmem_limit_bytes=VMEM_LIMIT),
        cost_estimate=pl.CostEstimate(
            flops=int(micros * FLOPS_PER_MICRO), bytes_accessed=0, transcendentals=0
        ),
    )(*arrays, *after)


def exchange(value, axis, flip):
    count = lax.axis_size(axis)
    return lax.ppermute(value, axis, [(i, i ^ flip) for i in range(count)])


def added(first, second):
    return first.astype(F32) + second.astype(F32)


def halve_kernel(picks, *refs):
    count = len(refs) - 2 * len(picks)
    terms, outs = refs[:count], refs[count:]
    for at, (pair, columns, kept, sent) in enumerate(picks):
        first, second = terms[pair], terms[pair + 1]
        for out_ref, blocks in ((outs[2 * at], kept), (outs[2 * at + 1], sent)):
            for slot, block in enumerate(blocks):
                out_ref[slot] = added(first[block, :, columns], second[block, :, columns]).astype(BF)


def halved_total(refs):
    return jnp.concatenate(
        [added(refs[i][0], refs[i + 1][0]) for i in range(0, len(refs), 2)], axis=1
    )


def stack_kernel(count, *refs):
    total, out_ref = halved_total(refs[:-1]), refs[-1]
    size = out_ref.shape[1]
    for i in range(count):
        out_ref[i] = total[i * size : (i + 1) * size].astype(BF)


def piece_kernel(count, place_ref, *refs):
    total, outs = halved_total(refs[:-count]), refs[-count:]
    size = outs[0].shape[0]
    pieces = [total[i * size : (i + 1) * size] for i in range(count)]
    place = place_ref[0]
    for flip, out_ref in enumerate(outs):
        value = pieces[0]
        for i in range(1, count):
            value = jnp.where(jnp.bitwise_xor(place, flip) == i, pieces[i], value)
        out_ref[...] = value.astype(BF)


def scaled_sum(terms, factor):
    return sum((t.astype(F32) for t in terms[1:]), terms[0].astype(F32)) * factor


def stacked_last_kernel(width, factor, terms_ref, qkv_ref, proj_ref):
    total = scaled_sum([terms_ref[i] for i in range(terms_ref.shape[0])], factor)
    qkv_ref[...] = total[:, : 3 * width]
    proj_ref[...] = total[:, 3 * width :]


def last_kernel(width, factor, *refs):
    terms, (qkv_ref, proj_ref) = refs[:-2], refs[-2:]
    half = len(terms) // 2
    qkv_ref[:, : 2 * width] = scaled_sum([r[...] for r in terms[:half]], factor)
    other = scaled_sum([r[...] for r in terms[half:]], factor)
    qkv_ref[:, 2 * width :] = other[:, :width]
    proj_ref[...] = other[:, width:]


class Halving:
    def __init__(self, keep, send, cut):
        bits = int(math.log2(lax.axis_size("wide"))) - 1
        self.terms = [keep, exchange(send, "wide", 1)]
        self.pairs = [(0, slice(0, cut)), (0, slice(cut, keep.shape[2]))]
        self.left = [list(range(bits))[::-1]] * 2
        self.orders = [list(range(bits)), list(range(bits))[::-1]]
        self.size = keep.shape[1]

    def pending(self):
        return bool(self.orders[0])

    def step(self, after=(), micros=0):
        picks, outs, flips = [], [], []
        for at, (pair, columns) in enumerate(self.pairs):
            bit, left = self.orders[at][0], self.left[at]
            shift = len(left) - 1 - left.index(bit)
            blocks = range(2 ** len(left))
            kept = [i for i in blocks if not (i >> shift) & 1]
            sent = [i for i in blocks if (i >> shift) & 1]
            picks.append((pair, columns, kept, sent))
            wide = len(range(*columns.indices(self.terms[pair].shape[2])))
            outs += [(shape((len(kept), self.size, wide)), whole)] * 2
            flips.append(2 << bit)
        got = small_call(
            functools.partial(halve_kernel, picks), (1,), [(a, whole) for a in self.terms],
            outs, [], micros, after,
        )
        self.terms = []
        for at, flip in enumerate(flips):
            self.terms += [got[2 * at], exchange(got[2 * at + 1], "wide", flip)]
            bit = self.orders[at][0]
            self.left[at] = [b for b in self.left[at] if b != bit]
            self.orders[at] = self.orders[at][1:]
        self.pairs = [(0, slice(None)), (2, slice(None))]
        self.done = got[0]

    def rest(self, after=(), micros=0):
        while self.pending():
            self.step(after, micros)


def body(
    clip_tokens,
    cotangent,
    qkv_spatial,
    proj_spatial,
    adaln_spatial,
    qknorm_spatial,
    qkv_temporal,
    proj_temporal,
    adaln_temporal,
    qknorm_temporal,
):
    steps, patches, depth = clip_tokens.shape
    frames, per_device, _ = cotangent.shape
    hd = qknorm_spatial.shape[1]
    width = proj_spatial.shape[1]
    heads = width // hd
    axes = ("wide", "narrow")
    count = lax.axis_size("wide")
    devices = count * lax.axis_size("narrow")
    parts = 2
    group = per_device // parts
    rows = frames * group
    tokens = steps * patches
    w_s, p_s, w_t, p_t = qkv_spatial.T, proj_spatial.T, qkv_temporal.T, proj_temporal.T
    me = lax.axis_index("wide").astype(jnp.int32).reshape(1)
    half = shape((count // 2, depth // count, 2 * width))
    both = shape((count // 2, depth // count, 4 * width))

    middle, send0, normed_s, qkv_s, att_s, mixed_s, _ = call(
        functools.partial(spatial_forward_kernel, (steps, heads, hd, per_device, group)),
        steps,
        [(clip_tokens, each), (w_s, whole), (p_s, whole), (adaln_spatial, whole),
         (qknorm_spatial, whole)],
        [(shape((tokens, depth)), whole), (shape((rows, depth)), whole),
         (shape((steps, patches, depth)), each),
         (shape((steps, 3 * width, patches), F32), each),
         (shape((steps, heads, patches, patches)), each), (shape((width, tokens)), lane)],
        [((width, patches), F32)],
        17,
    )

    def turn(value):
        value = value.reshape(devices, steps * group, depth)
        value = lax.all_to_all(value, axes, split_axis=0, concat_axis=0, tiled=True)
        return value.reshape(rows, depth)

    flat_cot = cotangent.reshape(frames * per_device, depth)
    send1, lhs_s, turned, branch_t, dmixed_t, _ = block_call(
        functools.partial(between_kernel, (steps, per_device, group, count)),
        [(me, scalar), (middle, whole), (normed_s, whole), (flat_cot, whole), (p_t, whole),
         (adaln_temporal, whole)],
        [(shape((rows, depth)), whole), (shape((depth, tokens)), whole),
         (shape((parts, rows, depth)), each), (shape((parts, rows, depth)), each),
         (shape((parts, width, rows), F32), each)],
        [((depth, tokens), F32)],
        6,
    )
    middles = [turn(send0), turn(send1)]

    received, saved = [], []
    for part in range(parts):
        dmid, *keep, _ = block_call(
            functools.partial(temporal_kernel, (heads, hd, group), part),
            [(middles[part], whole), (turned, part), (dmixed_t, part), (w_t, whole),
             (adaln_temporal, whole), (qknorm_temporal, whole)],
            [(shape((rows, depth)), whole), (shape((rows, depth)), whole),
             (shape((3 * width, rows)), whole), (shape((width, rows)), whole)],
            [((3 * width, rows), F32), ((width, rows), F32), ((3 * width, rows), F32)],
            13,
        )
        received.append(turn(dmid))
        saved.append(keep)
    (normed0, dqkv0, mixed0), (normed1, dqkv1, mixed1) = saved

    keep_t, send_t, _ = block_call(
        functools.partial(temporal_grad_kernel, (width, count)),
        [(me, scalar), (normed0, whole), (normed1, whole), (dqkv0, whole), (dqkv1, whole),
         (mixed0, whole), (mixed1, whole), (branch_t, whole)],
        [(both, whole)] * 2,
        [((depth, parts * rows), F32), ((depth, parts * rows), BF),
         ((3 * width, parts * rows), BF), ((width, parts * rows), BF)],
        0,
        [received[0]],
    )
    sum_t = Halving(keep_t, send_t, 2 * width)
    sum_t.step()
    result, done_result = block_call(
        functools.partial(result_kernel, (per_device, group)),
        [(middles[0], whole), (middles[1], whole), (mixed0, whole), (mixed1, whole), (p_t, whole),
         (adaln_temporal, whole)],
        [(shape((frames * per_device, depth)), whole)],
        [((parts * rows, depth), BF)],
        0,
        [sum_t.done],
    )
    dmid_s, dmixed_s, dv_s, keep_b, send_b, done_v = call(
        functools.partial(spatial_value_kernel, (heads, hd, steps, per_device, group, count)),
        steps,
        [(me, scalar), (received[0], whole), (received[1], whole), (att_s, each), (p_s, whole),
         (adaln_spatial, whole), (lhs_s, whole), (mixed_s, whole)],
        [(shape((steps, patches, depth)), each), (shape((steps, width, patches)), each),
         (shape((width, tokens)), lane), (half, whole), (half, whole)],
        [((width, patches), F32), ((width, patches), F32),
         ((depth, tokens), F32), ((depth, tokens), BF)],
        1,
        [sum_t.done, done_result],
    )
    cut = 128 * -(-2 * width // 256)
    sum_t.rest([done_v], 20)
    sum_b = Halving(keep_b, send_b, cut)
    sum_b.step([sum_t.done])
    dqk_s, keep_a, send_a, done_s = call(
        functools.partial(spatial_score_kernel, (heads, hd, steps)),
        steps,
        [(qkv_s, each), (att_s, each), (dmixed_s, each), (qknorm_spatial, whole), (lhs_s, whole)],
        [(shape((2 * width, tokens)), lane), (half, whole), (half, whole)],
        [((2 * width, patches), F32)],
        11,
        [sum_b.done],
    )
    narrow = lax.axis_size("narrow")
    factor = 1.0 / math.sqrt(frames * patches)
    share = depth // devices
    place = lax.axis_index("narrow").astype(jnp.int32).reshape(1)

    def pieces_of(total, after):
        pieces = small_call(
            functools.partial(piece_kernel, narrow), (1,),
            [(place, scalar)] + [(a, whole) for a in total.terms],
            [(shape((share, 2 * width)), whole)] * narrow, [], 20, after,
        )
        return pieces[0], [exchange(p, "narrow", i) if i else p for i, p in enumerate(pieces)]

    (stack,) = small_call(
        functools.partial(stack_kernel, narrow), (1,), [(a, whole) for a in sum_t.terms],
        [(shape((narrow, share, 4 * width)), whole)], [], 20, [done_s],
    )
    stack_terms = lax.all_to_all(stack, "narrow", split_axis=0, concat_axis=0, tiled=True)
    sum_b.rest([stack])
    sum_a = Halving(keep_a, send_a, cut)
    sum_a.step([sum_b.done])
    first_b, terms_b = pieces_of(sum_b, [sum_a.done])
    sum_a.rest([first_b])
    grad_clip, done_clip = call(
        grad_clip_kernel,
        steps,
        [(clip_tokens, each), (dmid_s, each), (dqk_s, lane), (dv_s, lane), (w_s, whole),
         (adaln_spatial, whole)],
        [(shape((steps, patches, depth)), each)],
        [],
        4,
        [sum_a.done],
    )
    first_a, terms_a = pieces_of(sum_a, [done_clip])
    whole_grad, part_grad = shape((share, 3 * width), F32), shape((share, width), F32)
    grad_qkv_t, grad_proj_t = small_call(
        functools.partial(stacked_last_kernel, width, factor), (1,), [(stack_terms, whole)],
        [(whole_grad, whole), (part_grad, whole)], [], 2, [first_a],
    )
    grad_qkv_s, grad_proj_s = small_call(
        functools.partial(last_kernel, width, factor), (1,),
        [(a, whole) for a in terms_a + terms_b],
        [(whole_grad, whole), (part_grad, whole)], [], 2,
    )
    return (
        result.reshape(frames, per_device, depth),
        grad_clip,
        grad_qkv_s,
        grad_proj_s,
        grad_qkv_t,
        grad_proj_t,
    )


def solution(mesh):
    tokens = P(("wide", "narrow"), None, None)
    columns = P(None, ("wide", "narrow"), None)
    own = P(("wide", "narrow"), None)
    return jax.shard_map(
        body,
        mesh=mesh,
        in_specs=(tokens, columns) + (P(),) * 8,
        out_specs=(columns, tokens, own, own, own, own),
        check_vma=False,
    )
```

```python
import functools
import math

import jax
import jax.numpy as jnp
from jax import lax
from jax.experimental import pallas as pl
from jax.experimental.pallas import tpu as pltpu
from jax.sharding import PartitionSpec as P

EPS = 1e-06
BF = jnp.bfloat16
F32 = jnp.float32
VMEM_LIMIT = 56 * 1024 * 1024
SMALL_LIMIT = 24 * 1024 * 1024
FLOPS_PER_MICRO = 1.15e9
LOG2E = math.log2(math.e)


def nn(a, b):
    return lax.dot_general(a, b, (((1,), (0,)), ((), ())), preferred_element_type=F32)


def nt(a, b):
    return lax.dot_general(a, b, (((1,), (1,)), ((), ())), preferred_element_type=F32)


def tn(a, b):
    return lax.dot_general(a, b, (((0,), (0,)), ((), ())), preferred_element_type=F32)


def standardize(x):
    centre = x - jnp.mean(x, axis=-1, keepdims=True)
    rate = lax.rsqrt(jnp.mean(centre * centre, axis=-1, keepdims=True) + EPS)
    return centre * rate, rate


def modulated(x, mod_ref):
    return (standardize(x)[0] * (1.0 + mod_ref[1:2, :]) + mod_ref[0:1, :]).astype(BF)


def modulate_vjp(x, mod_ref, grad):
    unit, rate = standardize(x)
    scaled = grad * (1.0 + mod_ref[1:2, :])
    inner = jnp.mean(unit * scaled, axis=-1, keepdims=True)
    return rate * (scaled - jnp.mean(scaled, axis=-1, keepdims=True) - unit * inner)


def column(row):
    n = row.shape[1]
    same = lax.broadcasted_iota(jnp.int32, (n, n), 0) == lax.broadcasted_iota(jnp.int32, (n, n), 1)
    return jnp.sum(jnp.where(same, jnp.broadcast_to(row, (n, n)), 0.0), axis=1, keepdims=True)


def unit_rms(vectors):
    rate = lax.rsqrt(jnp.mean(vectors * vectors, axis=0, keepdims=True) + EPS)
    return vectors * rate, rate


def same_column(rows, stride):
    first = lax.broadcasted_iota(jnp.int32, (rows, rows), 0)
    second = lax.broadcasted_iota(jnp.int32, (rows, rows), 1)
    return lax.rem(first, stride) == lax.rem(second, stride)


def head_parts(qkv_ref, head, hd, width):
    at = head * hd
    return (
        qkv_ref[at : at + hd, :],
        qkv_ref[width + at : width + at + hd, :],
        qkv_ref[2 * width + at : 2 * width + at + hd, :],
    )


def head_weights(q_unit, k_unit, gq, gk, mask, hd):
    qn = (q_unit * (gq * (LOG2E / math.sqrt(hd)))).astype(BF)
    kn = (k_unit * gk).astype(BF)
    weights = jnp.exp2(tn(kn, qn))
    if mask is not None:
        weights = jnp.where(mask, weights, 0.0)
    return (weights * (1.0 / jnp.sum(weights, axis=0, keepdims=True))).astype(BF)


def score_vjp(q, k, v16, weights, grad16, gq, gk, hd):
    q_unit, q_rate = unit_rms(q)
    k_unit, k_rate = unit_rms(k)
    scale = 1.0 / math.sqrt(hd)
    w32 = weights.astype(F32)
    weighted = w32 * tn(v16, grad16)
    d_s = (weighted - w32 * jnp.sum(weighted, axis=0, keepdims=True)).astype(BF)
    d_q = nn((k_unit * gk).astype(BF), d_s) * (gq * scale)
    d_k = nt((q_unit * gq).astype(BF), d_s) * (gk * scale)
    d_q = q_rate * (d_q - q_unit * jnp.mean(q_unit * d_q, axis=0, keepdims=True))
    d_k = k_rate * (d_k - k_unit * jnp.mean(k_unit * d_k, axis=0, keepdims=True))
    return d_q, d_k


def arrange(tr_ref, lhs_ref, me, count):
    size = lhs_ref.shape[0] // count
    for slot in range(count):
        place = (slot % (count // 2)) * 2 + slot // (count // 2)
        start = pl.multiple_of(jnp.bitwise_xor(me, place) * size, 8)
        lhs_ref[slot * size : (slot + 1) * size, :] = tr_ref[pl.ds(start, size), :].astype(BF)


def put_halves(value, keep_ref, send_ref, columns):
    half, size = keep_ref.shape[0], keep_ref.shape[1]
    for slot in range(half):
        keep_ref[slot, :, columns] = value[slot * size : (slot + 1) * size].astype(BF)
        send_ref[slot, :, columns] = value[(half + slot) * size : (half + slot + 1) * size].astype(BF)


def pick_group(dims, part, mid_ref, send_ref):
    steps, per_device, group = dims
    out_rows, in_rows = send_ref.shape[0], mid_ref.shape[0]
    out = lax.broadcasted_iota(jnp.int32, (out_rows, in_rows), 0)
    src = lax.broadcasted_iota(jnp.int32, (out_rows, in_rows), 1)
    owner, rest = out // (steps * group), lax.rem(out, steps * group)
    base = (rest // group) * (in_rows // steps) + owner * per_device + lax.rem(rest, group)
    pick = (src == base + part * group).astype(F32).astype(BF)
    send_ref[...] = nn(pick, mid_ref[...]).astype(BF)


def spatial_forward_kernel(
    dims, x_ref, w_ref, p_ref, mod_ref, gain_ref,
    mid_ref, send_ref, normed_ref, qkv_ref, att_ref, mixed_ref, mixed_scr, qkv_scr,
):
    steps, heads, hd, per_device, group = dims
    rows = x_ref.shape[1]
    width = heads * hd
    gq, gk = column(gain_ref[0:1, :]), column(gain_ref[1:2, :])
    for step in range(steps):
        x = x_ref[step].astype(F32)
        normed = modulated(x, mod_ref)
        normed_ref.put(step, normed)
        qkv_scr[...] = nt(w_ref[...], normed)
        qkv_ref.put(step, qkv_scr[...].astype(BF))
        for head in range(heads):
            q, k, v = head_parts(qkv_scr, head, hd, width)
            weights = head_weights(unit_rms(q)[0], unit_rms(k)[0], gq, gk, None, hd)
            att_ref[step, head] = weights
            mixed_scr[head * hd : (head + 1) * hd, :] = nn(v.astype(BF), weights)
        att_ref.flush(step)
        mixed = mixed_scr[...].astype(BF)
        mixed_ref[:, step * rows : (step + 1) * rows] = mixed
        mixed_ref.flush(step)
        mid_ref[step * rows : (step + 1) * rows, :] = (
            x + mod_ref[2:3, :] * tn(mixed, p_ref[...])
        ).astype(BF)
    mid_ref.flush()
    pick_group((steps, per_device, group), 0, mid_ref, send_ref)


def between_kernel(
    dims, me_ref, mid_ref, normed_ref, cot_ref, p_ref, mod_ref,
    send_ref, lhs_ref, turned_ref, branch_ref, grad_ref, tr_scr,
):
    steps, per_device, group, count = dims
    pick_group((steps, per_device, group), 1, mid_ref, send_ref)
    send_ref.flush()
    out_rows, in_rows = turned_ref.shape[1], cot_ref.shape[0]
    out = lax.broadcasted_iota(jnp.int32, (out_rows, in_rows), 0)
    src = lax.broadcasted_iota(jnp.int32, (out_rows, in_rows), 1)
    base = (out // group) * per_device + lax.rem(out, group)
    for part in range(turned_ref.shape[0]):
        turned = nn((src == base + part * group).astype(F32).astype(BF), cot_ref[...])
        turned_ref.put(part, turned.astype(BF))
        branch = (mod_ref[2:3, :] * turned).astype(BF)
        branch_ref.put(part, branch)
        grad_ref.put(part, nt(p_ref[...], branch).astype(BF))
    rows = normed_ref.shape[1]
    for step in range(steps):
        tr_scr[:, step * rows : (step + 1) * rows] = normed_ref[step].astype(F32).T
    arrange(tr_scr, lhs_ref, me_ref[0], count)


def temporal_kernel(
    dims, part, mid_ref, turned_ref, grad_ref, w_ref, mod_ref, gain_ref,
    dmid_ref, normed_ref, dqkv_ref, mixed_ref, qkv_scr, mixed_scr, dqkv_scr,
):
    heads, hd, group = dims
    width = heads * hd
    rows = mid_ref.shape[0]
    x = mid_ref[...].astype(F32)
    normed = modulated(x, mod_ref)
    normed_ref.put(..., normed)
    qkv_scr[...] = nt(w_ref[...], normed)
    gq, gk = column(gain_ref[0:1, :]), column(gain_ref[1:2, :])
    mask = same_column(rows, group) if group > 1 else None
    for head in range(heads):
        q, k, v = head_parts(qkv_scr, head, hd, width)
        at = head * hd
        v16 = v.astype(BF)
        weights = head_weights(unit_rms(q)[0], unit_rms(k)[0], gq, gk, mask, hd)
        mixed_scr[at : at + hd, :] = nn(v16, weights)
        grad16 = grad_ref[0, at : at + hd, :]
        d_q, d_k = score_vjp(q, k, v16, weights, grad16, gq, gk, hd)
        dqkv_scr[at : at + hd, :] = d_q
        dqkv_scr[width + at : width + at + hd, :] = d_k
        dqkv_scr[2 * width + at : 2 * width + at + hd, :] = nt(grad16, weights)
    mixed_ref.put(..., mixed_scr[...].astype(BF))
    dqkv = dqkv_scr[...].astype(BF)
    dqkv_ref.put(..., dqkv)
    grad = modulate_vjp(x, mod_ref, tn(dqkv, w_ref[...]))
    dmid_ref[...] = (turned_ref[0].astype(F32) + grad).astype(BF)


def temporal_grad_kernel(
    dims, me_ref, normed0_ref, normed1_ref, dqkv0_ref, dqkv1_ref, mixed0_ref, mixed1_ref,
    branch_ref, keep_ref, send_ref,
    tr_scr, lhs_scr, dqkv_scr, mixed_scr,
):
    width, count = dims
    rows = normed0_ref.shape[0]
    for part, (normed, dqkv, mixed) in enumerate(
        ((normed0_ref, dqkv0_ref, mixed0_ref), (normed1_ref, dqkv1_ref, mixed1_ref))
    ):
        at = slice(part * rows, (part + 1) * rows)
        tr_scr[:, at] = normed[...].astype(F32).T
        dqkv_scr[:, at] = dqkv[...]
        mixed_scr[:, at] = mixed[...]
    arrange(tr_scr, lhs_scr, me_ref[0], count)
    put_halves(nt(lhs_scr[...], dqkv_scr[...]), keep_ref, send_ref, slice(0, 3 * width))
    for part in range(2):
        tr_scr[:, part * rows : (part + 1) * rows] = branch_ref[part].astype(F32).T
    arrange(tr_scr, lhs_scr, me_ref[0], count)
    put_halves(nt(lhs_scr[...], mixed_scr[...]), keep_ref, send_ref, slice(3 * width, 4 * width))


def result_kernel(
    dims, mid0_ref, mid1_ref, mixed0_ref, mixed1_ref, p_ref, mod_ref, out_ref, scr
):
    per_device, group = dims
    rows = mid0_ref.shape[0]
    for part, (mid, mixed) in enumerate(((mid0_ref, mixed0_ref), (mid1_ref, mixed1_ref))):
        scr[part * rows : (part + 1) * rows, :] = (
            mid[...].astype(F32) + mod_ref[2:3, :] * tn(mixed[...], p_ref[...])
        ).astype(BF)
    out_rows = out_ref.shape[0]
    out = lax.broadcasted_iota(jnp.int32, (out_rows, out_rows), 0)
    src = lax.broadcasted_iota(jnp.int32, (out_rows, out_rows), 1)
    col = lax.rem(out, per_device)
    base = (col // group) * rows + (out // per_device) * group + lax.rem(col, group)
    out_ref[...] = nn((src == base).astype(F32).astype(BF), scr[...]).astype(BF)


def spatial_value_kernel(
    dims, me_ref, recv0_ref, recv1_ref, att_ref, p_ref, mod_ref, lhs_ref, mixed_ref,
    dmid_ref, grad_ref, dv_ref, keep_ref, send_ref,
    grad_scr, dv_scr, tr_scr, lhs_scr,
):
    heads, hd, steps, per_device, group, count = dims
    width = heads * hd
    rows, in_rows = dmid_ref.shape[1], recv0_ref.shape[0]
    out = lax.broadcasted_iota(jnp.int32, (rows, in_rows), 0)
    src = lax.broadcasted_iota(jnp.int32, (rows, in_rows), 1)
    owner, col = out // per_device, lax.rem(out, per_device)
    for step in range(steps):
        base = owner * (steps * group) + step * group + lax.rem(col, group)
        part = jnp.where(src == base, col // group, -1)
        dmid = nn((part == 0).astype(F32).astype(BF), recv0_ref[...])
        dmid += nn((part == 1).astype(F32).astype(BF), recv1_ref[...])
        dmid_ref.put(step, dmid.astype(BF))
        branch = (mod_ref[2:3, :] * dmid).astype(BF)
        here = slice(step * rows, (step + 1) * rows)
        tr_scr[:, here] = branch.astype(F32).T
        grad_scr[...] = nt(p_ref[...], branch)
        grad_ref.put(step, grad_scr[...].astype(BF))
        for head in range(heads):
            at = slice(head * hd, (head + 1) * hd)
            dv_scr[at, :] = nt(grad_scr[at, :].astype(BF), att_ref[step, head])
        dv_ref[:, here] = dv_scr[...].astype(BF)
        dv_ref.flush(step)
    put_halves(nt(lhs_ref[...], dv_ref[...]), keep_ref, send_ref, slice(0, width))
    arrange(tr_scr, lhs_scr, me_ref[0], count)
    put_halves(nt(lhs_scr[...], mixed_ref[...]), keep_ref, send_ref, slice(width, 2 * width))


def spatial_score_kernel(
    dims, qkv_ref, att_ref, grad_ref, gain_ref, lhs_ref,
    dqk_ref, keep_ref, send_ref, dqk_scr, qkv_scr,
):
    heads, hd, steps = dims
    width = heads * hd
    rows = qkv_ref.shape[2]
    gq, gk = column(gain_ref[0:1, :]), column(gain_ref[1:2, :])
    for step in range(steps):
        qkv_scr[...] = qkv_ref[step].astype(F32)
        for head in range(heads):
            q, k, v = head_parts(qkv_scr, head, hd, width)
            at = head * hd
            grad16 = grad_ref[step, at : at + hd, :]
            d_q, d_k = score_vjp(q, k, v.astype(BF), att_ref[step, head], grad16, gq, gk, hd)
            dqk_scr[at : at + hd, :] = d_q
            dqk_scr[width + at : width + at + hd, :] = d_k
        dqk_ref[:, step * rows : (step + 1) * rows] = dqk_scr[...].astype(BF)
        dqk_ref.flush(step)
    put_halves(nt(lhs_ref[...], dqk_ref[...]), keep_ref, send_ref, slice(None))


def grad_clip_kernel(x_ref, dmid_ref, dqk_ref, dv_ref, w_ref, mod_ref, out_ref):
    cut = dqk_ref.shape[0]
    for step in range(x_ref.shape[0]):
        grad = tn(dqk_ref.lanes(step), w_ref[:cut, :]) + tn(dv_ref.lanes(step), w_ref[cut:, :])
        grad = modulate_vjp(x_ref[step].astype(F32), mod_ref, grad)
        out_ref.put(step, (dmid_ref[step].astype(F32) + grad).astype(BF))


def shape(dims, kind=BF):
    return jax.ShapeDtypeStruct(tuple(dims), kind)


def whole(array):
    n = len(array.shape)
    return pl.BlockSpec(array.shape, lambda *_: (0,) * n, pipeline_mode=pl.Buffered(1))


def each(array):
    pass


def lane(array):
    pass


def scalar(array):
    return pl.BlockSpec(memory_space=pltpu.SMEM)


def unused(array):
    return pl.BlockSpec(memory_space=pl.ANY)


def small_call(kernel, grid, ins, outs, scratch, micros, after=()):
    first, arrays = len(ins), [a for a, _ in ins]

    def run(*refs):
        kernel(*refs[:first], *refs[first + len(after) :])

    return pl.pallas_call(
        run,
        grid=grid,
        in_specs=[s(a) for a, s in ins] + [unused(a) for a in after],
        out_specs=[s(a) for a, s in outs],
        out_shape=[a for a, _ in outs],
        scratch_shapes=[pltpu.VMEM(d, k) for d, k in scratch],
        compiler_params=pltpu.CompilerParams(vmem_limit_bytes=SMALL_LIMIT),
        cost_estimate=pl.CostEstimate(
            flops=int(micros * FLOPS_PER_MICRO), bytes_accessed=0, transcendentals=0
        ),
    )(*arrays, *after)


class Plain:
    def __init__(self, held):
        self.held, self.shape = held, held.shape

    def __getitem__(self, index):
        return self.held[index]

    def __setitem__(self, index, value):
        self.held[index] = value

    def put(self, index, value):
        self.held[index] = value

    def flush(self, index=None):
        pass


def block_call(kernel, ins, outs, scratch, micros, after=()):
    def spec(array, kind):
        if kind is scalar:
            return scalar(array)
        n = len(array.shape)
        if isinstance(kind, int):
            return pl.BlockSpec((1,) + tuple(array.shape[1:]), lambda i: (kind,) + (0,) * (n - 1))
        return pl.BlockSpec(tuple(array.shape), lambda i: (0,) * n)

    def run(*refs):
        given, refs = refs[: len(ins)], refs[len(ins) + len(after) :]
        results, own = refs[: len(outs)], refs[len(outs) + 1 :]
        refs[len(outs)][...] = jnp.zeros_like(refs[len(outs)])
        given = [r if k is scalar else Plain(r) for r, (_, k) in zip(given, ins)]
        kernel(*given, *[Plain(r) for r in results], *own)

    token = shape((8, 128), F32)
    return pl.pallas_call(
        run,
        grid=(1,),
        in_specs=[spec(a, k) for a, k in ins] + [unused(a) for a in after],
        out_specs=[spec(a, None) for a, _ in outs] + [spec(token, None)],
        out_shape=[a for a, _ in outs] + [token],
        scratch_shapes=[pltpu.VMEM(d, k) for d, k in scratch],
        compiler_params=pltpu.CompilerParams(vmem_limit_bytes=VMEM_LIMIT),
        cost_estimate=pl.CostEstimate(
            flops=int(micros * FLOPS_PER_MICRO), bytes_accessed=0, transcendentals=0
        ),
    )(*[a for a, _ in ins], *after)


class Source:
    def __init__(self, hbm, buf, pairs, sems, first):
        self.buf, self.shape = buf, buf.shape
        self.copies = [pltpu.make_async_copy(a, b, sems.at[first + i]) for i, (a, b) in enumerate(pairs)]
        self.waiting = set(range(len(self.copies)))

    def wait(self, index):
        wanted = [index] if isinstance(index, int) and len(self.copies) > 1 else range(len(self.copies))
        for i in wanted:
            if i in self.waiting:
                self.copies[i].wait()
                self.waiting.remove(i)

    def __getitem__(self, index):
        self.wait(index[0] if isinstance(index, tuple) else index)
        return self.buf[index]

    def ref(self, index):
        self.wait(index)
        return self.buf.at[index]

    def lanes(self, index):
        self.wait(index)
        size = self.shape[1] // len(self.copies)
        return self.buf[:, index * size : (index + 1) * size]


class Sink:
    def __init__(self, hbm, buf, pairs, sems, first):
        self.buf, self.shape = buf, buf.shape
        self.copies = [pltpu.make_async_copy(b, a, sems.at[first + i]) for i, (a, b) in enumerate(pairs)]
        self.left = set(range(len(self.copies)))

    def __getitem__(self, index):
        return self.buf[index]

    def __setitem__(self, index, value):
        self.buf[index] = value

    def ref(self, index):
        return self.buf.at[index]

    def flush(self, index=None):
        for i in sorted(self.left) if index is None else [index]:
            self.copies[i].start()
            self.left.remove(i)

    def put(self, index, value):
        self.buf[index] = value
        self.flush(index if len(self.copies) > 1 else None)


def cuts(hbm, buf, kind, steps):
    if kind is each:
        return [(hbm.at[i], buf.at[i]) for i in range(buf.shape[0])]
    if kind is lane:
        size = buf.shape[1] // steps
        return [(hbm.at[:, pl.ds(i * size, size)], buf.at[:, pl.ds(i * size, size)]) for i in range(steps)]
    if isinstance(kind, int):
        return [(hbm.at[pl.ds(kind, 1)], buf)]
    if isinstance(kind, tuple):
        size = buf.shape[1]
        return [(hbm.at[:, pl.ds(kind[0] * size, size)], buf)]
    return [(hbm, buf)]


def count_cuts(array, kind, steps):
    return array.shape[0] if kind is each else steps if kind is lane else 1


def call(kernel, steps, ins, outs, scratch, micros, after=(), aliases=None):
    arrays = [a for a, _ in ins]
    moved = [(a, k) for a, k in ins if k is not scalar]
    first_of, total = [], 0
    for a, k in moved + list(outs):
        first_of.append(total)
        total += count_cuts(a, k, steps)

    def buffer(array, kind):
        dims = tuple(array.shape)
        if isinstance(kind, int):
            dims = (1,) + dims[1:]
        if isinstance(kind, tuple):
            dims = (dims[0], dims[1] // steps)
        return pltpu.VMEM(dims, array.dtype)

    def run(*refs):
        given, refs = refs[: len(ins)], refs[len(ins) + len(after) :]
        results, refs = refs[: len(outs)], refs[len(outs) :]
        refs[0][...] = jnp.zeros_like(refs[0])
        refs = refs[1:]
        own, refs = refs[: len(scratch)], refs[len(scratch) :]
        sems, bufs = refs[-1], list(refs[:-1])
        firsts = list(first_of)
        sources = []
        for ref, (_, kind) in zip(given, ins):
            if kind is scalar:
                sources.append(ref)
            else:
                buf = bufs.pop(0)
                sources.append(Source(ref, buf, cuts(ref, buf, kind, steps), sems, firsts.pop(0)))
        sinks = []
        for ref, (_, kind) in zip(results, outs):
            buf = bufs.pop(0)
            sinks.append(Sink(ref, buf, cuts(ref, buf, kind, steps), sems, firsts.pop(0)))
        live = [x for x in sources if isinstance(x, Source)]
        live.sort(key=lambda x: math.prod(x.shape) > 16384)
        for i in range(max(len(x.copies) for x in live)):
            for x in live:
                if i < len(x.copies):
                    x.copies[i].start()
        kernel(*sources, *sinks, *own)
        for x in live:
            for i in sorted(x.waiting):
                x.copies[i].wait()
        for x in sinks:
            x.flush()
        for x in sinks:
            for copy in x.copies:
                copy.wait()

    return pl.pallas_call(
        run,
        in_specs=[scalar(a) if k is scalar else unused(a) for a, k in ins] + [unused(a) for a in after],
        out_specs=[unused(a) for a, _ in outs] + [pl.BlockSpec(memory_space=pltpu.VMEM)],
        out_shape=[a for a, _ in outs] + [shape((8, 128), F32)],
        input_output_aliases=aliases or {},
        scratch_shapes=[pltpu.VMEM(d, k) for d, k in scratch]
        + [buffer(a, k) for a, k in moved + list(outs)]
        + [pltpu.SemaphoreType.DMA((total,))],
        compiler_params=pltpu.CompilerParams(vmem_limit_bytes=VMEM_LIMIT),
        cost_estimate=pl.CostEstimate(
            flops=int(micros * FLOPS_PER_MICRO), bytes_accessed=0, transcendentals=0
        ),
    )(*arrays, *after)


def exchange(value, axis, flip):
    count = lax.axis_size(axis)
    return lax.ppermute(value, axis, [(i, i ^ flip) for i in range(count)])


def added(first, second):
    return first.astype(F32) + second.astype(F32)


def halve_kernel(picks, *refs):
    count = len(refs) - 2 * len(picks)
    terms, outs = refs[:count], refs[count:]
    for at, (pair, columns, kept, sent) in enumerate(picks):
        first, second = terms[pair], terms[pair + 1]
        for out_ref, blocks in ((outs[2 * at], kept), (outs[2 * at + 1], sent)):
            for slot, block in enumerate(blocks):
                out_ref[slot] = added(first[block, :, columns], second[block, :, columns]).astype(BF)


def halved_total(refs):
    return jnp.concatenate(
        [added(refs[i][0], refs[i + 1][0]) for i in range(0, len(refs), 2)], axis=1
    )


def stack_kernel(count, *refs):
    total, out_ref = halved_total(refs[:-1]), refs[-1]
    size = out_ref.shape[1]
    for i in range(count):
        out_ref[i] = total[i * size : (i + 1) * size].astype(BF)


def piece_kernel(count, place_ref, *refs):
    total, outs = halved_total(refs[:-count]), refs[-count:]
    size = outs[0].shape[0]
    pieces = [total[i * size : (i + 1) * size] for i in range(count)]
    place = place_ref[0]
    for flip, out_ref in enumerate(outs):
        value = pieces[0]
        for i in range(1, count):
            value = jnp.where(jnp.bitwise_xor(place, flip) == i, pieces[i], value)
        out_ref[...] = value.astype(BF)


def scaled_sum(terms, factor):
    return sum((t.astype(F32) for t in terms[1:]), terms[0].astype(F32)) * factor


def stacked_last_kernel(width, factor, terms_ref, qkv_ref, proj_ref):
    total = scaled_sum([terms_ref[i] for i in range(terms_ref.shape[0])], factor)
    qkv_ref[...] = total[:, : 3 * width]
    proj_ref[...] = total[:, 3 * width :]


def last_kernel(width, factor, *refs):
    terms, (qkv_ref, proj_ref) = refs[:-2], refs[-2:]
    total = scaled_sum([r[...] for r in terms], factor)
    qkv_ref[...] = total[:, : 3 * width]
    proj_ref[...] = total[:, 3 * width :]


class Halving:
    def __init__(self, keep, send, cut):
        bits = int(math.log2(lax.axis_size("wide"))) - 1
        self.terms = [keep, exchange(send, "wide", 1)]
        self.pairs = [(0, slice(0, cut)), (0, slice(cut, keep.shape[2]))]
        self.left = [list(range(bits))[::-1]] * 2
        self.orders = [list(range(bits)), list(range(bits))[::-1]]
        self.size = keep.shape[1]

    def pending(self):
        return bool(self.orders[0])

    def step(self, after=(), micros=0):
        picks, outs, flips = [], [], []
        for at, (pair, columns) in enumerate(self.pairs):
            bit, left = self.orders[at][0], self.left[at]
            shift = len(left) - 1 - left.index(bit)
            blocks = range(2 ** len(left))
            kept = [i for i in blocks if not (i >> shift) & 1]
            sent = [i for i in blocks if (i >> shift) & 1]
            picks.append((pair, columns, kept, sent))
            wide = len(range(*columns.indices(self.terms[pair].shape[2])))
            outs += [(shape((len(kept), self.size, wide)), whole)] * 2
            flips.append(2 << bit)
        got = small_call(
            functools.partial(halve_kernel, picks), (1,), [(a, whole) for a in self.terms],
            outs, [], micros, after,
        )
        self.terms = []
        for at, flip in enumerate(flips):
            self.terms += [got[2 * at], exchange(got[2 * at + 1], "wide", flip)]
            bit = self.orders[at][0]
            self.left[at] = [b for b in self.left[at] if b != bit]
            self.orders[at] = self.orders[at][1:]
        self.pairs = [(0, slice(None)), (2, slice(None))]
        self.done = got[0]

    def rest(self, after=(), micros=0):
        while self.pending():
            self.step(after, micros)


def body(
    clip_tokens,
    cotangent,
    qkv_spatial,
    proj_spatial,
    adaln_spatial,
    qknorm_spatial,
    qkv_temporal,
    proj_temporal,
    adaln_temporal,
    qknorm_temporal,
):
    steps, patches, depth = clip_tokens.shape
    frames, per_device, _ = cotangent.shape
    hd = qknorm_spatial.shape[1]
    width = proj_spatial.shape[1]
    heads = width // hd
    axes = ("wide", "narrow")
    count = lax.axis_size("wide")
    devices = count * lax.axis_size("narrow")
    parts = 2
    group = per_device // parts
    rows = frames * group
    tokens = steps * patches
    w_s, p_s, w_t, p_t = qkv_spatial.T, proj_spatial.T, qkv_temporal.T, proj_temporal.T
    me = lax.axis_index("wide").astype(jnp.int32).reshape(1)
    half = shape((count // 2, depth // count, 2 * width))
    both = shape((count // 2, depth // count, 4 * width))

    middle, send0, normed_s, qkv_s, att_s, mixed_s, _ = call(
        functools.partial(spatial_forward_kernel, (steps, heads, hd, per_device, group)),
        steps,
        [(clip_tokens, each), (w_s, whole), (p_s, whole), (adaln_spatial, whole),
         (qknorm_spatial, whole)],
        [(shape((tokens, depth)), whole), (shape((rows, depth)), whole),
         (shape((steps, patches, depth)), each),
         (shape((steps, 3 * width, patches)), each),
         (shape((steps, heads, patches, patches)), each), (shape((width, tokens)), lane)],
        [((width, patches), F32), ((3 * width, patches), F32)],
        17,
    )

    def turn(value):
        value = value.reshape(devices, steps * group, depth)
        value = lax.all_to_all(value, axes, split_axis=0, concat_axis=0, tiled=True)
        return value.reshape(rows, depth)

    flat_cot = cotangent.reshape(frames * per_device, depth)
    send1, lhs_s, turned, branch_t, dmixed_t, _ = block_call(
        functools.partial(between_kernel, (steps, per_device, group, count)),
        [(me, scalar), (middle, whole), (normed_s, whole), (flat_cot, whole), (p_t, whole),
         (adaln_temporal, whole)],
        [(shape((rows, depth)), whole), (shape((depth, tokens)), whole),
         (shape((parts, rows, depth)), each), (shape((parts, rows, depth)), each),
         (shape((parts, width, rows)), each)],
        [((depth, tokens), F32)],
        6,
    )
    middles = [turn(send0), turn(send1)]

    received, saved = [], []
    for part in range(parts):
        dmid, *keep, _ = block_call(
            functools.partial(temporal_kernel, (heads, hd, group), part),
            [(middles[part], whole), (turned, part), (dmixed_t, part), (w_t, whole),
             (adaln_temporal, whole), (qknorm_temporal, whole)],
            [(shape((rows, depth)), whole), (shape((rows, depth)), whole),
             (shape((3 * width, rows)), whole), (shape((width, rows)), whole)],
            [((3 * width, rows), F32), ((width, rows), F32), ((3 * width, rows), F32)],
            13,
        )
        received.append(turn(dmid))
        saved.append(keep)
    (normed0, dqkv0, mixed0), (normed1, dqkv1, mixed1) = saved

    keep_t, send_t, _ = block_call(
        functools.partial(temporal_grad_kernel, (width, count)),
        [(me, scalar), (normed0, whole), (normed1, whole), (dqkv0, whole), (dqkv1, whole),
         (mixed0, whole), (mixed1, whole), (branch_t, whole)],
        [(both, whole)] * 2,
        [((depth, parts * rows), F32), ((depth, parts * rows), BF),
         ((3 * width, parts * rows), BF), ((width, parts * rows), BF)],
        0,
        [received[0]],
    )
    sum_t = Halving(keep_t, send_t, 2 * width)
    sum_t.step()
    result, done_result = block_call(
        functools.partial(result_kernel, (per_device, group)),
        [(middles[0], whole), (middles[1], whole), (mixed0, whole), (mixed1, whole), (p_t, whole),
         (adaln_temporal, whole)],
        [(shape((frames * per_device, depth)), whole)],
        [((parts * rows, depth), BF)],
        0,
        [sum_t.done],
    )
    dmid_s, dmixed_s, dv_s, keep_b, send_b, done_v = call(
        functools.partial(spatial_value_kernel, (heads, hd, steps, per_device, group, count)),
        steps,
        [(me, scalar), (received[0], whole), (received[1], whole), (att_s, each), (p_s, whole),
         (adaln_spatial, whole), (lhs_s, whole), (mixed_s, whole)],
        [(shape((steps, patches, depth)), each), (shape((steps, width, patches)), each),
         (shape((width, tokens)), lane), (half, whole), (half, whole)],
        [((width, patches), F32), ((width, patches), F32),
         ((depth, tokens), F32), ((depth, tokens), BF)],
        1,
        [sum_t.done, done_result],
    )
    cut = 128 * -(-2 * width // 256)
    sum_t.rest([done_v], 20)
    sum_b = Halving(keep_b, send_b, cut)
    sum_b.step([sum_t.done])
    dqk_s, keep_a, send_a, done_s = call(
        functools.partial(spatial_score_kernel, (heads, hd, steps)),
        steps,
        [(qkv_s, each), (att_s, each), (dmixed_s, each), (qknorm_spatial, whole), (lhs_s, whole)],
        [(shape((2 * width, tokens)), lane), (half, whole), (half, whole)],
        [((2 * width, patches), F32), ((3 * width, patches), F32)],
        11,
        [sum_b.done],
    )
    narrow = lax.axis_size("narrow")
    factor = 1.0 / math.sqrt(frames * patches)
    share = depth // devices
    place = lax.axis_index("narrow").astype(jnp.int32).reshape(1)

    def pieces_of(terms, columns):
        pieces = small_call(
            functools.partial(piece_kernel, narrow), (1,),
            [(place, scalar)] + [(a, whole) for a in terms],
            [(shape((share, columns)), whole)] * narrow, [], 20,
        )
        return pieces[0], [exchange(p, "narrow", i) if i else p for i, p in enumerate(pieces)]

    (stack,) = small_call(
        functools.partial(stack_kernel, narrow), (1,), [(a, whole) for a in sum_t.terms],
        [(shape((narrow, share, 4 * width)), whole)], [], 20, [done_s],
    )
    stack_terms = lax.all_to_all(stack, "narrow", split_axis=0, concat_axis=0, tiled=True)
    sum_a = Halving(keep_a, send_a, cut)
    sum_a.step([stack])
    sum_b.rest([sum_a.done])
    sum_a.rest([sum_b.done])
    first, terms = pieces_of(sum_a.terms + sum_b.terms, 4 * width)
    grad_clip, done_clip = call(
        grad_clip_kernel,
        steps,
        [(clip_tokens, each), (dmid_s, each), (dqk_s, lane), (dv_s, lane), (w_s, whole),
         (adaln_spatial, whole)],
        [(shape((steps, patches, depth)), each)],
        [],
        4,
        [first],
    )
    whole_grad, part_grad = shape((share, 3 * width), F32), shape((share, width), F32)
    grad_qkv_t, grad_proj_t = small_call(
        functools.partial(stacked_last_kernel, width, factor), (1,), [(stack_terms, whole)],
        [(whole_grad, whole), (part_grad, whole)], [], 2, [done_clip],
    )
    grad_qkv_s, grad_proj_s = small_call(
        functools.partial(last_kernel, width, factor), (1,), [(a, whole) for a in terms],
        [(whole_grad, whole), (part_grad, whole)], [], 2,
    )
    return (
        result.reshape(frames, per_device, depth),
        grad_clip,
        grad_qkv_s,
        grad_proj_s,
        grad_qkv_t,
        grad_proj_t,
    )


def solution(mesh):
    tokens = P(("wide", "narrow"), None, None)
    columns = P(None, ("wide", "narrow"), None)
    own = P(("wide", "narrow"), None)
    return jax.shard_map(
        body,
        mesh=mesh,
        in_specs=(tokens, columns) + (P(),) * 8,
        out_specs=(columns, tokens, own, own, own, own),
        check_vma=False,
    )
```

```python
import functools
import math

import jax
import jax.numpy as jnp
from jax import lax
from jax.experimental import pallas as pl
from jax.experimental.pallas import tpu as pltpu
from jax.sharding import PartitionSpec as P

EPS = 1e-06
BF = jnp.bfloat16
F32 = jnp.float32
VMEM_LIMIT = 56 * 1024 * 1024
SMALL_LIMIT = 24 * 1024 * 1024
FLOPS_PER_MICRO = 1.15e9
LOG2E = math.log2(math.e)


def nn(a, b):
    return lax.dot_general(a, b, (((1,), (0,)), ((), ())), preferred_element_type=F32)


def nt(a, b):
    return lax.dot_general(a, b, (((1,), (1,)), ((), ())), preferred_element_type=F32)


def tn(a, b):
    return lax.dot_general(a, b, (((0,), (0,)), ((), ())), preferred_element_type=F32)


def standardize(x):
    centre = x - jnp.mean(x, axis=-1, keepdims=True)
    rate = lax.rsqrt(jnp.mean(centre * centre, axis=-1, keepdims=True) + EPS)
    return centre * rate, rate


def modulated(x, mod_ref):
    return (standardize(x)[0] * (1.0 + mod_ref[1:2, :]) + mod_ref[0:1, :]).astype(BF)


def modulate_vjp(x, mod_ref, grad):
    unit, rate = standardize(x)
    scaled = grad * (1.0 + mod_ref[1:2, :])
    inner = jnp.mean(unit * scaled, axis=-1, keepdims=True)
    return rate * (scaled - jnp.mean(scaled, axis=-1, keepdims=True) - unit * inner)


def column(row):
    n = row.shape[1]
    same = lax.broadcasted_iota(jnp.int32, (n, n), 0) == lax.broadcasted_iota(jnp.int32, (n, n), 1)
    return jnp.sum(jnp.where(same, jnp.broadcast_to(row, (n, n)), 0.0), axis=1, keepdims=True)


def unit_rms(vectors):
    rate = lax.rsqrt(jnp.mean(vectors * vectors, axis=0, keepdims=True) + EPS)
    return vectors * rate, rate


def row_numbers(rows):
    return lax.broadcasted_iota(jnp.int32, (rows, 1), 0)


def one_hot(base, columns):
    src = lax.broadcasted_iota(jnp.int32, (base.shape[0], columns), 1)
    return (src == base).astype(F32).astype(BF)


def same_column(rows, stride):
    first = row_numbers(rows)
    second = lax.broadcasted_iota(jnp.int32, (1, rows), 1)
    return lax.rem(first, stride) == lax.rem(second, stride)


def head_parts(qkv_ref, head, hd, width):
    at = head * hd
    return (
        qkv_ref[at : at + hd, :],
        qkv_ref[width + at : width + at + hd, :],
        qkv_ref[2 * width + at : 2 * width + at + hd, :],
    )


def head_weights(q_unit, k_unit, gq, gk, mask, hd):
    qn = (q_unit * (gq * (LOG2E / math.sqrt(hd)))).astype(BF)
    kn = (k_unit * gk).astype(BF)
    weights = jnp.exp2(tn(kn, qn))
    if mask is not None:
        weights = jnp.where(mask, weights, 0.0)
    return (weights * (1.0 / jnp.sum(weights, axis=0, keepdims=True))).astype(BF)


def score_vjp(q, k, v16, weights, grad16, gq, gk, hd):
    q_unit, q_rate = unit_rms(q)
    k_unit, k_rate = unit_rms(k)
    scale = 1.0 / math.sqrt(hd)
    w32 = weights.astype(F32)
    weighted = w32 * tn(v16, grad16)
    d_s = (weighted - w32 * jnp.sum(weighted, axis=0, keepdims=True)).astype(BF)
    d_q = nn((k_unit * gk).astype(BF), d_s) * (gq * scale)
    d_k = nt((q_unit * gq).astype(BF), d_s) * (gk * scale)
    d_q = q_rate * (d_q - q_unit * jnp.mean(q_unit * d_q, axis=0, keepdims=True))
    d_k = k_rate * (d_k - k_unit * jnp.mean(k_unit * d_k, axis=0, keepdims=True))
    return d_q, d_k


def arrange(tr_ref, lhs_ref, me, count):
    size = lhs_ref.shape[0] // count
    for slot in range(count):
        place = (slot % (count // 2)) * 2 + slot // (count // 2)
        start = pl.multiple_of(jnp.bitwise_xor(me, place) * size, 8)
        lhs_ref[slot * size : (slot + 1) * size, :] = tr_ref[pl.ds(start, size), :].astype(BF)


def put_halves(value, keep_ref, send_ref, columns):
    half, size = keep_ref.shape[0], keep_ref.shape[1]
    for slot in range(half):
        keep_ref[slot, :, columns] = value[slot * size : (slot + 1) * size].astype(BF)
        send_ref[slot, :, columns] = value[(half + slot) * size : (half + slot + 1) * size].astype(BF)


def pick_group(dims, part, mid_ref, send_ref):
    steps, per_device, group = dims
    out_rows, in_rows = send_ref.shape[0], mid_ref.shape[0]
    out = row_numbers(out_rows)
    owner, rest = out // (steps * group), lax.rem(out, steps * group)
    base = (rest // group) * (in_rows // steps) + owner * per_device + lax.rem(rest, group)
    send_ref[...] = nn(one_hot(base + part * group, in_rows), mid_ref[...]).astype(BF)


def spatial_forward_kernel(
    dims, x_ref, w_ref, p_ref, mod_ref, gain_ref,
    mid_ref, send_ref, normed_ref, qkv_ref, att_ref, mixed_ref, mixed_scr,
):
    steps, heads, hd, per_device, group = dims
    rows = x_ref.shape[1]
    width = heads * hd
    gq, gk = column(gain_ref[0:1, :]), column(gain_ref[1:2, :])
    for step in range(steps):
        x = x_ref[step].astype(F32)
        normed = modulated(x, mod_ref)
        normed_ref.put(step, normed)
        qkv_ref.put(step, nt(w_ref[...], normed))
        for head in range(heads):
            q, k, v = head_parts(qkv_ref.ref(step), head, hd, width)
            weights = head_weights(unit_rms(q)[0], unit_rms(k)[0], gq, gk, None, hd)
            att_ref[step, head] = weights
            mixed_scr[head * hd : (head + 1) * hd, :] = nn(v.astype(BF), weights)
        att_ref.flush(step)
        mixed = mixed_scr[...].astype(BF)
        mixed_ref[:, step * rows : (step + 1) * rows] = mixed
        mixed_ref.flush(step)
        mid_ref[step * rows : (step + 1) * rows, :] = (
            x + mod_ref[2:3, :] * tn(mixed, p_ref[...])
        ).astype(BF)
    mid_ref.flush()
    pick_group((steps, per_device, group), 0, mid_ref, send_ref)


def between_kernel(
    dims, me_ref, mid_ref, normed_ref, cot_ref, p_ref, mod_ref,
    send_ref, lhs_ref, turned_ref, branch_ref, grad_ref, tr_scr,
):
    steps, per_device, group, count = dims
    pick_group((steps, per_device, group), 1, mid_ref, send_ref)
    send_ref.flush()
    out_rows, in_rows = turned_ref.shape[1], cot_ref.shape[0]
    out = row_numbers(out_rows)
    base = (out // group) * per_device + lax.rem(out, group)
    for part in range(turned_ref.shape[0]):
        turned = nn(one_hot(base + part * group, in_rows), cot_ref[...])
        turned_ref.put(part, turned.astype(BF))
        branch = (mod_ref[2:3, :] * turned).astype(BF)
        branch_ref.put(part, branch)
        grad_ref.put(part, nt(p_ref[...], branch))
    rows = normed_ref.shape[1]
    for step in range(steps):
        tr_scr[:, step * rows : (step + 1) * rows] = normed_ref[step].astype(F32).T
    arrange(tr_scr, lhs_ref, me_ref[0], count)


def temporal_kernel(
    dims, part, mid_ref, turned_ref, grad_ref, w_ref, mod_ref, gain_ref,
    dmid_ref, normed_ref, dqkv_ref, mixed_ref, qkv_scr, mixed_scr, dqkv_scr,
):
    heads, hd, group = dims
    width = heads * hd
    rows = mid_ref.shape[0]
    x = mid_ref[...].astype(F32)
    normed = modulated(x, mod_ref)
    normed_ref.put(..., normed)
    qkv_scr[...] = nt(w_ref[...], normed)
    gq, gk = column(gain_ref[0:1, :]), column(gain_ref[1:2, :])
    mask = same_column(rows, group) if group > 1 else None
    for head in range(heads):
        q, k, v = head_parts(qkv_scr, head, hd, width)
        at = head * hd
        v16 = v.astype(BF)
        weights = head_weights(unit_rms(q)[0], unit_rms(k)[0], gq, gk, mask, hd)
        mixed_scr[at : at + hd, :] = nn(v16, weights)
        grad16 = grad_ref[0, at : at + hd, :].astype(BF)
        d_q, d_k = score_vjp(q, k, v16, weights, grad16, gq, gk, hd)
        dqkv_scr[at : at + hd, :] = d_q
        dqkv_scr[width + at : width + at + hd, :] = d_k
        dqkv_scr[2 * width + at : 2 * width + at + hd, :] = nt(grad16, weights)
    mixed_ref.put(..., mixed_scr[...].astype(BF))
    dqkv = dqkv_scr[...].astype(BF)
    dqkv_ref.put(..., dqkv)
    grad = modulate_vjp(x, mod_ref, tn(dqkv, w_ref[...]))
    dmid_ref[...] = (turned_ref[0].astype(F32) + grad).astype(BF)


def temporal_grad_kernel(
    dims, me_ref, normed0_ref, normed1_ref, dqkv0_ref, dqkv1_ref, mixed0_ref, mixed1_ref,
    branch_ref, keep_ref, send_ref,
    tr_scr, lhs_scr, dqkv_scr, mixed_scr,
):
    width, count = dims
    rows = normed0_ref.shape[0]
    for part, (normed, dqkv, mixed) in enumerate(
        ((normed0_ref, dqkv0_ref, mixed0_ref), (normed1_ref, dqkv1_ref, mixed1_ref))
    ):
        at = slice(part * rows, (part + 1) * rows)
        tr_scr[:, at] = normed[...].astype(F32).T
        dqkv_scr[:, at] = dqkv[...]
        mixed_scr[:, at] = mixed[...]
    arrange(tr_scr, lhs_scr, me_ref[0], count)
    put_halves(nt(lhs_scr[...], dqkv_scr[...]), keep_ref, send_ref, slice(0, 3 * width))
    for part in range(2):
        tr_scr[:, part * rows : (part + 1) * rows] = branch_ref[part].astype(F32).T
    arrange(tr_scr, lhs_scr, me_ref[0], count)
    put_halves(nt(lhs_scr[...], mixed_scr[...]), keep_ref, send_ref, slice(3 * width, 4 * width))


def result_kernel(
    dims, mid0_ref, mid1_ref, mixed0_ref, mixed1_ref, p_ref, mod_ref, out_ref, scr
):
    per_device, group = dims
    rows = mid0_ref.shape[0]
    for part, (mid, mixed) in enumerate(((mid0_ref, mixed0_ref), (mid1_ref, mixed1_ref))):
        scr[part * rows : (part + 1) * rows, :] = (
            mid[...].astype(F32) + mod_ref[2:3, :] * tn(mixed[...], p_ref[...])
        ).astype(BF)
    out_rows = out_ref.shape[0]
    out = row_numbers(out_rows)
    col = lax.rem(out, per_device)
    base = (col // group) * rows + (out // per_device) * group + lax.rem(col, group)
    out_ref[...] = nn(one_hot(base, out_rows), scr[...]).astype(BF)


def spatial_value_kernel(
    dims, me_ref, recv0_ref, recv1_ref, att_ref, p_ref, mod_ref, lhs_ref, mixed_ref,
    dmid_ref, grad_ref, dv_ref, keep_ref, send_ref,
    grad_scr, dv_scr, tr_scr, lhs_scr,
):
    heads, hd, steps, per_device, group, count = dims
    width = heads * hd
    rows, in_rows = dmid_ref.shape[1], recv0_ref.shape[0]
    out = row_numbers(rows)
    owner, col = out // per_device, lax.rem(out, per_device)
    for step in range(steps):
        base = owner * (steps * group) + step * group + lax.rem(col, group)
        part = col // group
        dmid = nn(one_hot(jnp.where(part == 0, base, -1), in_rows), recv0_ref[...])
        dmid += nn(one_hot(jnp.where(part == 1, base, -1), in_rows), recv1_ref[...])
        dmid_ref.put(step, dmid.astype(BF))
        branch = (mod_ref[2:3, :] * dmid).astype(BF)
        here = slice(step * rows, (step + 1) * rows)
        tr_scr[:, here] = branch.astype(F32).T
        grad_scr[...] = nt(p_ref[...], branch)
        grad_ref.put(step, grad_scr[...].astype(BF))
        for head in range(heads):
            at = slice(head * hd, (head + 1) * hd)
            dv_scr[at, :] = nt(grad_scr[at, :].astype(BF), att_ref[step, head])
        dv_ref[:, here] = dv_scr[...].astype(BF)
        dv_ref.flush(step)
    put_halves(nt(lhs_ref[...], dv_ref[...]), keep_ref, send_ref, slice(0, width))
    arrange(tr_scr, lhs_scr, me_ref[0], count)
    put_halves(nt(lhs_scr[...], mixed_ref[...]), keep_ref, send_ref, slice(width, 2 * width))


def spatial_score_kernel(
    dims, qkv_ref, att_ref, grad_ref, gain_ref, lhs_ref,
    dqk_ref, keep_ref, send_ref, dqk_scr,
):
    heads, hd, steps = dims
    width = heads * hd
    rows = qkv_ref.shape[2]
    gq, gk = column(gain_ref[0:1, :]), column(gain_ref[1:2, :])
    for step in range(steps):
        for head in range(heads):
            q, k, v = head_parts(qkv_ref.ref(step), head, hd, width)
            at = head * hd
            grad16 = grad_ref[step, at : at + hd, :]
            d_q, d_k = score_vjp(q, k, v.astype(BF), att_ref[step, head], grad16, gq, gk, hd)
            dqk_scr[at : at + hd, :] = d_q
            dqk_scr[width + at : width + at + hd, :] = d_k
        dqk_ref[:, step * rows : (step + 1) * rows] = dqk_scr[...].astype(BF)
        dqk_ref.flush(step)
    put_halves(nt(lhs_ref[...], dqk_ref[...]), keep_ref, send_ref, slice(None))


def grad_clip_kernel(x_ref, dmid_ref, dqk_ref, dv_ref, w_ref, mod_ref, out_ref):
    cut = dqk_ref.shape[0]
    rows = x_ref.shape[1]
    both = tn(dqk_ref[...], w_ref[:cut, :]) + tn(dv_ref[...], w_ref[cut:, :])
    for step in range(x_ref.shape[0]):
        grad = both[step * rows : (step + 1) * rows]
        grad = modulate_vjp(x_ref[step].astype(F32), mod_ref, grad)
        out_ref.put(step, (dmid_ref[step].astype(F32) + grad).astype(BF))


def shape(dims, kind=BF):
    return jax.ShapeDtypeStruct(tuple(dims), kind)


def whole(array):
    n = len(array.shape)
    return pl.BlockSpec(array.shape, lambda *_: (0,) * n, pipeline_mode=pl.Buffered(1))


def each(array):
    pass


def lane(array):
    pass


def scalar(array):
    return pl.BlockSpec(memory_space=pltpu.SMEM)


def unused(array):
    return pl.BlockSpec(memory_space=pl.ANY)


def small_call(kernel, grid, ins, outs, scratch, micros, after=()):
    first, arrays = len(ins), [a for a, _ in ins]

    def run(*refs):
        kernel(*refs[:first], *refs[first + len(after) :])

    return pl.pallas_call(
        run,
        grid=grid,
        in_specs=[s(a) for a, s in ins] + [unused(a) for a in after],
        out_specs=[s(a) for a, s in outs],
        out_shape=[a for a, _ in outs],
        scratch_shapes=[pltpu.VMEM(d, k) for d, k in scratch],
        compiler_params=pltpu.CompilerParams(vmem_limit_bytes=SMALL_LIMIT),
        cost_estimate=pl.CostEstimate(
            flops=int(micros * FLOPS_PER_MICRO), bytes_accessed=0, transcendentals=0
        ),
    )(*arrays, *after)


class Plain:
    def __init__(self, held):
        self.held, self.shape = held, held.shape

    def __getitem__(self, index):
        return self.held[index]

    def __setitem__(self, index, value):
        self.held[index] = value

    def put(self, index, value):
        self.held[index] = value

    def flush(self, index=None):
        pass


def block_call(kernel, ins, outs, scratch, micros, after=()):
    def spec(array, kind):
        if kind is scalar:
            return scalar(array)
        n = len(array.shape)
        if isinstance(kind, int):
            return pl.BlockSpec((1,) + tuple(array.shape[1:]), lambda i: (kind,) + (0,) * (n - 1))
        return pl.BlockSpec(tuple(array.shape), lambda i: (0,) * n)

    def run(*refs):
        given, refs = refs[: len(ins)], refs[len(ins) + len(after) :]
        results, own = refs[: len(outs)], refs[len(outs) + 1 :]
        refs[len(outs)][...] = jnp.zeros_like(refs[len(outs)])
        given = [r if k is scalar else Plain(r) for r, (_, k) in zip(given, ins)]
        kernel(*given, *[Plain(r) for r in results], *own)

    token = shape((8, 128), F32)
    return pl.pallas_call(
        run,
        grid=(1,),
        in_specs=[spec(a, k) for a, k in ins] + [unused(a) for a in after],
        out_specs=[spec(a, None) for a, _ in outs] + [spec(token, None)],
        out_shape=[a for a, _ in outs] + [token],
        scratch_shapes=[pltpu.VMEM(d, k) for d, k in scratch],
        compiler_params=pltpu.CompilerParams(vmem_limit_bytes=VMEM_LIMIT),
        cost_estimate=pl.CostEstimate(
            flops=int(micros * FLOPS_PER_MICRO), bytes_accessed=0, transcendentals=0
        ),
    )(*[a for a, _ in ins], *after)


class Source:
    def __init__(self, hbm, buf, pairs, sems, first):
        self.buf, self.shape = buf, buf.shape
        self.copies = [pltpu.make_async_copy(a, b, sems.at[first + i]) for i, (a, b) in enumerate(pairs)]
        self.waiting = set(range(len(self.copies)))

    def wait(self, index):
        wanted = [index] if isinstance(index, int) and len(self.copies) > 1 else range(len(self.copies))
        for i in wanted:
            if i in self.waiting:
                self.copies[i].wait()
                self.waiting.remove(i)

    def __getitem__(self, index):
        self.wait(index[0] if isinstance(index, tuple) else index)
        return self.buf[index]

    def ref(self, index):
        self.wait(index)
        return self.buf.at[index]

    def lanes(self, index):
        self.wait(index)
        size = self.shape[1] // len(self.copies)
        return self.buf[:, index * size : (index + 1) * size]


class Sink:
    def __init__(self, hbm, buf, pairs, sems, first):
        self.buf, self.shape = buf, buf.shape
        self.copies = [pltpu.make_async_copy(b, a, sems.at[first + i]) for i, (a, b) in enumerate(pairs)]
        self.left = set(range(len(self.copies)))

    def __getitem__(self, index):
        return self.buf[index]

    def __setitem__(self, index, value):
        self.buf[index] = value

    def ref(self, index):
        return self.buf.at[index]

    def flush(self, index=None):
        for i in sorted(self.left) if index is None else [index]:
            self.copies[i].start()
            self.left.remove(i)

    def put(self, index, value):
        self.buf[index] = value
        self.flush(index if len(self.copies) > 1 else None)


def cuts(hbm, buf, kind, steps):
    if kind is each:
        return [(hbm.at[i], buf.at[i]) for i in range(buf.shape[0])]
    if kind is lane:
        size = buf.shape[1] // steps
        return [(hbm.at[:, pl.ds(i * size, size)], buf.at[:, pl.ds(i * size, size)]) for i in range(steps)]
    if isinstance(kind, int):
        return [(hbm.at[pl.ds(kind, 1)], buf)]
    if isinstance(kind, tuple):
        size = buf.shape[1]
        return [(hbm.at[:, pl.ds(kind[0] * size, size)], buf)]
    return [(hbm, buf)]


def count_cuts(array, kind, steps):
    return array.shape[0] if kind is each else steps if kind is lane else 1


def call(kernel, steps, ins, outs, scratch, micros, after=(), aliases=None):
    arrays = [a for a, _ in ins]
    moved = [(a, k) for a, k in ins if k is not scalar]
    first_of, total = [], 0
    for a, k in moved + list(outs):
        first_of.append(total)
        total += count_cuts(a, k, steps)

    def buffer(array, kind):
        dims = tuple(array.shape)
        if isinstance(kind, int):
            dims = (1,) + dims[1:]
        if isinstance(kind, tuple):
            dims = (dims[0], dims[1] // steps)
        return pltpu.VMEM(dims, array.dtype)

    def run(*refs):
        given, refs = refs[: len(ins)], refs[len(ins) + len(after) :]
        results, refs = refs[: len(outs)], refs[len(outs) :]
        refs[0][...] = jnp.zeros_like(refs[0])
        refs = refs[1:]
        own, refs = refs[: len(scratch)], refs[len(scratch) :]
        sems, bufs = refs[-1], list(refs[:-1])
        firsts = list(first_of)
        sources = []
        for ref, (_, kind) in zip(given, ins):
            if kind is scalar:
                sources.append(ref)
            else:
                buf = bufs.pop(0)
                sources.append(Source(ref, buf, cuts(ref, buf, kind, steps), sems, firsts.pop(0)))
        sinks = []
        for ref, (_, kind) in zip(results, outs):
            buf = bufs.pop(0)
            sinks.append(Sink(ref, buf, cuts(ref, buf, kind, steps), sems, firsts.pop(0)))
        live = [x for x in sources if isinstance(x, Source)]
        live.sort(key=lambda x: math.prod(x.shape) > 16384)
        for i in range(max(len(x.copies) for x in live)):
            for x in live:
                if i < len(x.copies):
                    x.copies[i].start()
        kernel(*sources, *sinks, *own)
        for x in live:
            for i in sorted(x.waiting):
                x.copies[i].wait()
        for x in sinks:
            x.flush()
        for x in sinks:
            for copy in x.copies:
                copy.wait()

    return pl.pallas_call(
        run,
        in_specs=[scalar(a) if k is scalar else unused(a) for a, k in ins] + [unused(a) for a in after],
        out_specs=[unused(a) for a, _ in outs] + [pl.BlockSpec(memory_space=pltpu.VMEM)],
        out_shape=[a for a, _ in outs] + [shape((8, 128), F32)],
        input_output_aliases=aliases or {},
        scratch_shapes=[pltpu.VMEM(d, k) for d, k in scratch]
        + [buffer(a, k) for a, k in moved + list(outs)]
        + [pltpu.SemaphoreType.DMA((total,))],
        compiler_params=pltpu.CompilerParams(vmem_limit_bytes=VMEM_LIMIT),
        cost_estimate=pl.CostEstimate(
            flops=int(micros * FLOPS_PER_MICRO), bytes_accessed=0, transcendentals=0
        ),
    )(*arrays, *after)


def exchange(value, axis, flip):
    count = lax.axis_size(axis)
    return lax.ppermute(value, axis, [(i, i ^ flip) for i in range(count)])


def added(first, second):
    return first.astype(F32) + second.astype(F32)


def halve_kernel(picks, *refs):
    count = len(refs) - 2 * len(picks)
    terms, outs = refs[:count], refs[count:]
    for at, (pair, columns, kept, sent) in enumerate(picks):
        first, second = terms[pair], terms[pair + 1]
        for out_ref, blocks in ((outs[2 * at], kept), (outs[2 * at + 1], sent)):
            for slot, block in enumerate(blocks):
                out_ref[slot] = added(first[block, :, columns], second[block, :, columns]).astype(BF)


def halved_total(refs):
    return jnp.concatenate(
        [added(refs[i][0], refs[i + 1][0]) for i in range(0, len(refs), 2)], axis=1
    )


def stack_kernel(count, *refs):
    total, out_ref = halved_total(refs[:-1]), refs[-1]
    size = out_ref.shape[1]
    for i in range(count):
        out_ref[i] = total[i * size : (i + 1) * size].astype(BF)


def piece_kernel(count, place_ref, *refs):
    total, outs = halved_total(refs[:-count]), refs[-count:]
    size = outs[0].shape[0]
    pieces = [total[i * size : (i + 1) * size] for i in range(count)]
    place = place_ref[0]
    for flip, out_ref in enumerate(outs):
        value = pieces[0]
        for i in range(1, count):
            value = jnp.where(jnp.bitwise_xor(place, flip) == i, pieces[i], value)
        out_ref[...] = value.astype(BF)


def scaled_sum(terms, factor):
    return sum((t.astype(F32) for t in terms[1:]), terms[0].astype(F32)) * factor


def stacked_last_kernel(width, factor, terms_ref, qkv_ref, proj_ref):
    total = scaled_sum([terms_ref[i] for i in range(terms_ref.shape[0])], factor)
    qkv_ref[...] = total[:, : 3 * width]
    proj_ref[...] = total[:, 3 * width :]


def last_kernel(width, factor, *refs):
    terms, (qkv_ref, proj_ref) = refs[:-2], refs[-2:]
    half = len(terms) // 2
    qkv_ref[:, : 2 * width] = scaled_sum([r[...] for r in terms[:half]], factor)
    other = scaled_sum([r[...] for r in terms[half:]], factor)
    qkv_ref[:, 2 * width :] = other[:, :width]
    proj_ref[...] = other[:, width:]


class Halving:
    def __init__(self, keep, send, cut):
        bits = int(math.log2(lax.axis_size("wide"))) - 1
        self.terms = [keep, exchange(send, "wide", 1)]
        self.pairs = [(0, slice(0, cut)), (0, slice(cut, keep.shape[2]))]
        self.left = [list(range(bits))[::-1]] * 2
        self.orders = [list(range(bits)), list(range(bits))[::-1]]
        self.size = keep.shape[1]

    def pending(self):
        return bool(self.orders[0])

    def step(self, after=(), micros=0):
        picks, outs, flips = [], [], []
        for at, (pair, columns) in enumerate(self.pairs):
            bit, left = self.orders[at][0], self.left[at]
            shift = len(left) - 1 - left.index(bit)
            blocks = range(2 ** len(left))
            kept = [i for i in blocks if not (i >> shift) & 1]
            sent = [i for i in blocks if (i >> shift) & 1]
            picks.append((pair, columns, kept, sent))
            wide = len(range(*columns.indices(self.terms[pair].shape[2])))
            outs += [(shape((len(kept), self.size, wide)), whole)] * 2
            flips.append(2 << bit)
        got = small_call(
            functools.partial(halve_kernel, picks), (1,), [(a, whole) for a in self.terms],
            outs, [], micros, after,
        )
        self.terms = []
        for at, flip in enumerate(flips):
            self.terms += [got[2 * at], exchange(got[2 * at + 1], "wide", flip)]
            bit = self.orders[at][0]
            self.left[at] = [b for b in self.left[at] if b != bit]
            self.orders[at] = self.orders[at][1:]
        self.pairs = [(0, slice(None)), (2, slice(None))]
        self.done = got[0]

    def rest(self, after=(), micros=0):
        while self.pending():
            self.step(after, micros)


def body(
    clip_tokens,
    cotangent,
    qkv_spatial,
    proj_spatial,
    adaln_spatial,
    qknorm_spatial,
    qkv_temporal,
    proj_temporal,
    adaln_temporal,
    qknorm_temporal,
):
    steps, patches, depth = clip_tokens.shape
    frames, per_device, _ = cotangent.shape
    hd = qknorm_spatial.shape[1]
    width = proj_spatial.shape[1]
    heads = width // hd
    axes = ("wide", "narrow")
    count = lax.axis_size("wide")
    devices = count * lax.axis_size("narrow")
    parts = 2
    group = per_device // parts
    rows = frames * group
    tokens = steps * patches
    w_s, p_s, w_t, p_t = qkv_spatial.T, proj_spatial.T, qkv_temporal.T, proj_temporal.T
    me = lax.axis_index("wide").astype(jnp.int32).reshape(1)
    half = shape((count // 2, depth // count, 2 * width))
    both = shape((count // 2, depth // count, 4 * width))

    middle, send0, normed_s, qkv_s, att_s, mixed_s, _ = call(
        functools.partial(spatial_forward_kernel, (steps, heads, hd, per_device, group)),
        steps,
        [(clip_tokens, each), (w_s, whole), (p_s, whole), (adaln_spatial, whole),
         (qknorm_spatial, whole)],
        [(shape((tokens, depth)), whole), (shape((rows, depth)), whole),
         (shape((steps, patches, depth)), each),
         (shape((steps, 3 * width, patches), F32), each),
         (shape((steps, heads, patches, patches)), each), (shape((width, tokens)), lane)],
        [((width, patches), F32)],
        17,
    )

    def turn(value):
        value = value.reshape(devices, steps * group, depth)
        value = lax.all_to_all(value, axes, split_axis=0, concat_axis=0, tiled=True)
        return value.reshape(rows, depth)

    flat_cot = cotangent.reshape(frames * per_device, depth)
    send1, lhs_s, turned, branch_t, dmixed_t, _ = block_call(
        functools.partial(between_kernel, (steps, per_device, group, count)),
        [(me, scalar), (middle, whole), (normed_s, whole), (flat_cot, whole), (p_t, whole),
         (adaln_temporal, whole)],
        [(shape((rows, depth)), whole), (shape((depth, tokens)), whole),
         (shape((parts, rows, depth)), each), (shape((parts, rows, depth)), each),
         (shape((parts, width, rows), F32), each)],
        [((depth, tokens), F32)],
        6,
    )
    middles = [turn(send0), turn(send1)]

    received, saved = [], []
    for part in range(parts):
        dmid, *keep, _ = block_call(
            functools.partial(temporal_kernel, (heads, hd, group), part),
            [(middles[part], whole), (turned, part), (dmixed_t, part), (w_t, whole),
             (adaln_temporal, whole), (qknorm_temporal, whole)],
            [(shape((rows, depth)), whole), (shape((rows, depth)), whole),
             (shape((3 * width, rows)), whole), (shape((width, rows)), whole)],
            [((3 * width, rows), F32), ((width, rows), F32), ((3 * width, rows), F32)],
            13,
        )
        received.append(turn(dmid))
        saved.append(keep)
    (normed0, dqkv0, mixed0), (normed1, dqkv1, mixed1) = saved

    keep_t, send_t, _ = block_call(
        functools.partial(temporal_grad_kernel, (width, count)),
        [(me, scalar), (normed0, whole), (normed1, whole), (dqkv0, whole), (dqkv1, whole),
         (mixed0, whole), (mixed1, whole), (branch_t, whole)],
        [(both, whole)] * 2,
        [((depth, parts * rows), F32), ((depth, parts * rows), BF),
         ((3 * width, parts * rows), BF), ((width, parts * rows), BF)],
        0,
        [received[0]],
    )
    sum_t = Halving(keep_t, send_t, 2 * width)
    sum_t.step()
    result, done_result = block_call(
        functools.partial(result_kernel, (per_device, group)),
        [(middles[0], whole), (middles[1], whole), (mixed0, whole), (mixed1, whole), (p_t, whole),
         (adaln_temporal, whole)],
        [(shape((frames * per_device, depth)), whole)],
        [((parts * rows, depth), BF)],
        0,
        [sum_t.done],
    )
    dmid_s, dmixed_s, dv_s, keep_b, send_b, done_v = call(
        functools.partial(spatial_value_kernel, (heads, hd, steps, per_device, group, count)),
        steps,
        [(me, scalar), (received[0], whole), (received[1], whole), (att_s, each), (p_s, whole),
         (adaln_spatial, whole), (lhs_s, whole), (mixed_s, whole)],
        [(shape((steps, patches, depth)), each), (shape((steps, width, patches)), each),
         (shape((width, tokens)), lane), (half, whole), (half, whole)],
        [((width, patches), F32), ((width, patches), F32),
         ((depth, tokens), F32), ((depth, tokens), BF)],
        1,
        [sum_t.done, done_result],
    )
    cut = 128 * -(-2 * width // 256)
    sum_t.rest([done_v], 20)
    sum_b = Halving(keep_b, send_b, cut)
    sum_b.step([sum_t.done])
    dqk_s, keep_a, send_a, done_s = call(
        functools.partial(spatial_score_kernel, (heads, hd, steps)),
        steps,
        [(qkv_s, each), (att_s, each), (dmixed_s, each), (qknorm_spatial, whole), (lhs_s, whole)],
        [(shape((2 * width, tokens)), lane), (half, whole), (half, whole)],
        [((2 * width, patches), F32)],
        11,
        [sum_b.done],
    )
    narrow = lax.axis_size("narrow")
    factor = 1.0 / math.sqrt(frames * patches)
    share = depth // devices
    place = lax.axis_index("narrow").astype(jnp.int32).reshape(1)

    def pieces_of(total, after):
        pieces = small_call(
            functools.partial(piece_kernel, narrow), (1,),
            [(place, scalar)] + [(a, whole) for a in total.terms],
            [(shape((share, 2 * width)), whole)] * narrow, [], 20, after,
        )
        return pieces[0], [exchange(p, "narrow", i) if i else p for i, p in enumerate(pieces)]

    (stack,) = small_call(
        functools.partial(stack_kernel, narrow), (1,), [(a, whole) for a in sum_t.terms],
        [(shape((narrow, share, 4 * width)), whole)], [], 20, [done_s],
    )
    stack_terms = lax.all_to_all(stack, "narrow", split_axis=0, concat_axis=0, tiled=True)
    sum_b.rest([stack])
    sum_a = Halving(keep_a, send_a, cut)
    sum_a.step([sum_b.done])
    first_b, terms_b = pieces_of(sum_b, [sum_a.done])
    sum_a.rest([first_b])
    grad_clip, done_clip = call(
        grad_clip_kernel,
        steps,
        [(clip_tokens, each), (dmid_s, each), (dqk_s, lane), (dv_s, lane), (w_s, whole),
         (adaln_spatial, whole)],
        [(shape((steps, patches, depth)), each)],
        [],
        4,
        [sum_a.done],
    )
    first_a, terms_a = pieces_of(sum_a, [done_clip])
    whole_grad, part_grad = shape((share, 3 * width), F32), shape((share, width), F32)
    grad_qkv_t, grad_proj_t = small_call(
        functools.partial(stacked_last_kernel, width, factor), (1,), [(stack_terms, whole)],
        [(whole_grad, whole), (part_grad, whole)], [], 2, [first_a],
    )
    grad_qkv_s, grad_proj_s = small_call(
        functools.partial(last_kernel, width, factor), (1,),
        [(a, whole) for a in terms_a + terms_b],
        [(whole_grad, whole), (part_grad, whole)], [], 2,
    )
    return (
        result.reshape(frames, per_device, depth),
        grad_clip,
        grad_qkv_s,
        grad_proj_s,
        grad_qkv_t,
        grad_proj_t,
    )


def solution(mesh):
    tokens = P(("wide", "narrow"), None, None)
    columns = P(None, ("wide", "narrow"), None)
    own = P(("wide", "narrow"), None)
    return jax.shard_map(
        body,
        mesh=mesh,
        in_specs=(tokens, columns) + (P(),) * 8,
        out_specs=(columns, tokens, own, own, own, own),
        check_vma=False,
    )
```

```python
import functools
import math

import jax
import jax.numpy as jnp
from jax import lax
from jax.experimental import pallas as pl
from jax.experimental.pallas import tpu as pltpu
from jax.sharding import PartitionSpec as P

EPS = 1e-06
BF = jnp.bfloat16
F32 = jnp.float32
VMEM_LIMIT = 56 * 1024 * 1024
SMALL_LIMIT = 24 * 1024 * 1024
FLOPS_PER_MICRO = 1.15e9
LOG2E = math.log2(math.e)


def nn(a, b):
    return lax.dot_general(a, b, (((1,), (0,)), ((), ())), preferred_element_type=F32)


def nt(a, b):
    return lax.dot_general(a, b, (((1,), (1,)), ((), ())), preferred_element_type=F32)


def tn(a, b):
    return lax.dot_general(a, b, (((0,), (0,)), ((), ())), preferred_element_type=F32)


def standardize(x):
    centre = x - jnp.mean(x, axis=-1, keepdims=True)
    rate = lax.rsqrt(jnp.mean(centre * centre, axis=-1, keepdims=True) + EPS)
    return centre * rate, rate


def modulated(x, mod_ref):
    return (standardize(x)[0] * (1.0 + mod_ref[1:2, :]) + mod_ref[0:1, :]).astype(BF)


def modulate_vjp(x, mod_ref, grad):
    unit, rate = standardize(x)
    scaled = grad * (1.0 + mod_ref[1:2, :])
    inner = jnp.mean(unit * scaled, axis=-1, keepdims=True)
    return rate * (scaled - jnp.mean(scaled, axis=-1, keepdims=True) - unit * inner)


def column(row):
    n = row.shape[1]
    same = lax.broadcasted_iota(jnp.int32, (n, n), 0) == lax.broadcasted_iota(jnp.int32, (n, n), 1)
    return jnp.sum(jnp.where(same, jnp.broadcast_to(row, (n, n)), 0.0), axis=1, keepdims=True)


def unit_rms(vectors):
    rate = lax.rsqrt(jnp.mean(vectors * vectors, axis=0, keepdims=True) + EPS)
    return vectors * rate, rate


def row_numbers(rows):
    return lax.broadcasted_iota(jnp.int32, (rows, 1), 0)


def one_hot(base, columns):
    src = lax.broadcasted_iota(jnp.int32, (base.shape[0], columns), 1)
    return (src == base).astype(F32).astype(BF)


def same_column(rows, stride):
    first = row_numbers(rows)
    second = lax.broadcasted_iota(jnp.int32, (1, rows), 1)
    return lax.rem(first, stride) == lax.rem(second, stride)


def head_parts(qkv_ref, head, hd, width):
    at = head * hd
    return (
        qkv_ref[at : at + hd, :],
        qkv_ref[width + at : width + at + hd, :],
        qkv_ref[2 * width + at : 2 * width + at + hd, :],
    )


def head_weights(q_unit, k_unit, gq, gk, mask, hd):
    qn = (q_unit * (gq * (LOG2E / math.sqrt(hd)))).astype(BF)
    kn = (k_unit * gk).astype(BF)
    weights = jnp.exp2(tn(kn, qn))
    if mask is not None:
        weights = jnp.where(mask, weights, 0.0)
    return (weights * (1.0 / jnp.sum(weights, axis=0, keepdims=True))).astype(BF)


def score_vjp(q, k, v16, weights, grad16, gq, gk, hd):
    q_unit, q_rate = unit_rms(q)
    k_unit, k_rate = unit_rms(k)
    scale = 1.0 / math.sqrt(hd)
    w32 = weights.astype(F32)
    weighted = w32 * tn(v16, grad16)
    d_s = (weighted - w32 * jnp.sum(weighted, axis=0, keepdims=True)).astype(BF)
    d_q = nn((k_unit * gk).astype(BF), d_s) * (gq * scale)
    d_k = nt((q_unit * gq).astype(BF), d_s) * (gk * scale)
    d_q = q_rate * (d_q - q_unit * jnp.mean(q_unit * d_q, axis=0, keepdims=True))
    d_k = k_rate * (d_k - k_unit * jnp.mean(k_unit * d_k, axis=0, keepdims=True))
    return d_q, d_k


def arrange(tr_ref, lhs_ref, me, count):
    size = lhs_ref.shape[0] // count
    for slot in range(count):
        place = (slot % (count // 2)) * 2 + slot // (count // 2)
        start = pl.multiple_of(jnp.bitwise_xor(me, place) * size, 8)
        lhs_ref[slot * size : (slot + 1) * size, :] = tr_ref[pl.ds(start, size), :].astype(BF)


def put_halves(value, keep_ref, send_ref, columns):
    half, size = keep_ref.shape[0], keep_ref.shape[1]
    for slot in range(half):
        keep_ref[slot, :, columns] = value[slot * size : (slot + 1) * size].astype(BF)
        send_ref[slot, :, columns] = value[(half + slot) * size : (half + slot + 1) * size].astype(BF)


def pick_group(dims, part, mid_ref, send_ref):
    steps, per_device, group = dims
    out_rows, in_rows = send_ref.shape[0], mid_ref.shape[0]
    out = row_numbers(out_rows)
    owner, rest = out // (steps * group), lax.rem(out, steps * group)
    base = (rest // group) * (in_rows // steps) + owner * per_device + lax.rem(rest, group)
    send_ref[...] = nn(one_hot(base + part * group, in_rows), mid_ref[...]).astype(BF)


def spatial_forward_kernel(
    dims, x_ref, w_ref, p_ref, mod_ref, gain_ref,
    mid_ref, send_ref, normed_ref, qkv_ref, att_ref, mixed_ref, mixed_scr,
):
    steps, heads, hd, per_device, group = dims
    rows = x_ref.shape[1]
    width = heads * hd
    gq, gk = column(gain_ref[0:1, :]), column(gain_ref[1:2, :])
    for step in range(steps):
        x = x_ref[step].astype(F32)
        normed = modulated(x, mod_ref)
        normed_ref.put(step, normed)
        qkv_ref.put(step, nt(w_ref[...], normed))
        for head in range(heads):
            q, k, v = head_parts(qkv_ref.ref(step), head, hd, width)
            weights = head_weights(unit_rms(q)[0], unit_rms(k)[0], gq, gk, None, hd)
            att_ref[step, head] = weights
            mixed_scr[head * hd : (head + 1) * hd, :] = nn(v.astype(BF), weights)
        att_ref.flush(step)
        mixed = mixed_scr[...].astype(BF)
        mixed_ref[:, step * rows : (step + 1) * rows] = mixed
        mixed_ref.flush(step)
        mid_ref[step * rows : (step + 1) * rows, :] = (
            x + mod_ref[2:3, :] * tn(mixed, p_ref[...])
        ).astype(BF)
    mid_ref.flush()
    pick_group((steps, per_device, group), 0, mid_ref, send_ref)


def between_kernel(
    dims, me_ref, mid_ref, normed_ref, cot_ref, p_ref, mod_ref,
    send_ref, lhs_ref, turned_ref, branch_ref, grad_ref, tr_scr,
):
    steps, per_device, group, count = dims
    pick_group((steps, per_device, group), 1, mid_ref, send_ref)
    send_ref.flush()
    out_rows, in_rows = turned_ref.shape[1], cot_ref.shape[0]
    out = row_numbers(out_rows)
    base = (out // group) * per_device + lax.rem(out, group)
    for part in range(turned_ref.shape[0]):
        turned = nn(one_hot(base + part * group, in_rows), cot_ref[...])
        turned_ref.put(part, turned.astype(BF))
        branch = (mod_ref[2:3, :] * turned).astype(BF)
        branch_ref.put(part, branch)
        grad_ref.put(part, nt(p_ref[...], branch))
    rows = normed_ref.shape[1]
    for step in range(steps):
        tr_scr[:, step * rows : (step + 1) * rows] = normed_ref[step].astype(F32).T
    arrange(tr_scr, lhs_ref, me_ref[0], count)


def temporal_kernel(
    dims, part, mid_ref, turned_ref, grad_ref, w_ref, mod_ref, gain_ref,
    dmid_ref, normed_ref, dqkv_ref, mixed_ref, qkv_scr, mixed_scr, dqkv_scr,
):
    heads, hd, group = dims
    width = heads * hd
    rows = mid_ref.shape[0]
    x = mid_ref[...].astype(F32)
    normed = modulated(x, mod_ref)
    normed_ref.put(..., normed)
    qkv_scr[...] = nt(w_ref[...], normed)
    gq, gk = column(gain_ref[0:1, :]), column(gain_ref[1:2, :])
    mask = same_column(rows, group) if group > 1 else None
    for head in range(heads):
        q, k, v = head_parts(qkv_scr, head, hd, width)
        at = head * hd
        v16 = v.astype(BF)
        weights = head_weights(unit_rms(q)[0], unit_rms(k)[0], gq, gk, mask, hd)
        mixed_scr[at : at + hd, :] = nn(v16, weights)
        grad16 = grad_ref[0, at : at + hd, :].astype(BF)
        d_q, d_k = score_vjp(q, k, v16, weights, grad16, gq, gk, hd)
        dqkv_scr[at : at + hd, :] = d_q
        dqkv_scr[width + at : width + at + hd, :] = d_k
        dqkv_scr[2 * width + at : 2 * width + at + hd, :] = nt(grad16, weights)
    mixed_ref.put(..., mixed_scr[...].astype(BF))
    dqkv = dqkv_scr[...].astype(BF)
    dqkv_ref.put(..., dqkv)
    grad = modulate_vjp(x, mod_ref, tn(dqkv, w_ref[...]))
    dmid_ref[...] = (turned_ref[0].astype(F32) + grad).astype(BF)


def temporal_grad_kernel(
    dims, me_ref, normed0_ref, normed1_ref, dqkv0_ref, dqkv1_ref, mixed0_ref, mixed1_ref,
    branch_ref, keep_ref, send_ref,
    tr_scr, lhs_scr, dqkv_scr, mixed_scr,
):
    width, count = dims
    rows = normed0_ref.shape[0]
    for part, (normed, dqkv, mixed) in enumerate(
        ((normed0_ref, dqkv0_ref, mixed0_ref), (normed1_ref, dqkv1_ref, mixed1_ref))
    ):
        at = slice(part * rows, (part + 1) * rows)
        tr_scr[:, at] = normed[...].astype(F32).T
        dqkv_scr[:, at] = dqkv[...]
        mixed_scr[:, at] = mixed[...]
    arrange(tr_scr, lhs_scr, me_ref[0], count)
    put_halves(nt(lhs_scr[...], dqkv_scr[...]), keep_ref, send_ref, slice(0, 3 * width))
    for part in range(2):
        tr_scr[:, part * rows : (part + 1) * rows] = branch_ref[part].astype(F32).T
    arrange(tr_scr, lhs_scr, me_ref[0], count)
    put_halves(nt(lhs_scr[...], mixed_scr[...]), keep_ref, send_ref, slice(3 * width, 4 * width))


def result_kernel(
    dims, mid0_ref, mid1_ref, mixed0_ref, mixed1_ref, p_ref, mod_ref, out_ref, scr
):
    per_device, group = dims
    rows = mid0_ref.shape[0]
    for part, (mid, mixed) in enumerate(((mid0_ref, mixed0_ref), (mid1_ref, mixed1_ref))):
        scr[part * rows : (part + 1) * rows, :] = (
            mid[...].astype(F32) + mod_ref[2:3, :] * tn(mixed[...], p_ref[...])
        ).astype(BF)
    out_rows = out_ref.shape[0]
    out = row_numbers(out_rows)
    col = lax.rem(out, per_device)
    base = (col // group) * rows + (out // per_device) * group + lax.rem(col, group)
    out_ref[...] = nn(one_hot(base, out_rows), scr[...]).astype(BF)


def spatial_value_kernel(
    dims, me_ref, recv0_ref, recv1_ref, att_ref, p_ref, mod_ref, lhs_ref, mixed_ref,
    dmid_ref, grad_ref, dv_ref, keep_ref, send_ref,
    grad_scr, dv_scr, tr_scr, lhs_scr,
):
    heads, hd, steps, per_device, group, count = dims
    width = heads * hd
    rows, in_rows = dmid_ref.shape[1], recv0_ref.shape[0]
    out = row_numbers(rows)
    owner, col = out // per_device, lax.rem(out, per_device)
    for step in range(steps):
        base = owner * (steps * group) + step * group + lax.rem(col, group)
        part = col // group
        dmid = nn(one_hot(jnp.where(part == 0, base, -1), in_rows), recv0_ref[...])
        dmid += nn(one_hot(jnp.where(part == 1, base, -1), in_rows), recv1_ref[...])
        dmid_ref.put(step, dmid.astype(BF))
        branch = (mod_ref[2:3, :] * dmid).astype(BF)
        here = slice(step * rows, (step + 1) * rows)
        tr_scr[:, here] = branch.astype(F32).T
        grad_scr[...] = nt(p_ref[...], branch)
        grad_ref.put(step, grad_scr[...].astype(BF))
        for head in range(heads):
            at = slice(head * hd, (head + 1) * hd)
            dv_scr[at, :] = nt(grad_scr[at, :].astype(BF), att_ref[step, head])
        dv_ref[:, here] = dv_scr[...].astype(BF)
        dv_ref.flush(step)
    put_halves(nt(lhs_ref[...], dv_ref[...]), keep_ref, send_ref, slice(0, width))
    arrange(tr_scr, lhs_scr, me_ref[0], count)
    put_halves(nt(lhs_scr[...], mixed_ref[...]), keep_ref, send_ref, slice(width, 2 * width))


def spatial_score_kernel(
    dims, qkv_ref, att_ref, grad_ref, gain_ref, lhs_ref,
    dqk_ref, keep_ref, send_ref, dqk_scr,
):
    heads, hd, steps = dims
    width = heads * hd
    rows = qkv_ref.shape[2]
    gq, gk = column(gain_ref[0:1, :]), column(gain_ref[1:2, :])
    for step in range(steps):
        for head in range(heads):
            q, k, v = head_parts(qkv_ref.ref(step), head, hd, width)
            at = head * hd
            grad16 = grad_ref[step, at : at + hd, :]
            d_q, d_k = score_vjp(q, k, v.astype(BF), att_ref[step, head], grad16, gq, gk, hd)
            dqk_scr[at : at + hd, :] = d_q
            dqk_scr[width + at : width + at + hd, :] = d_k
        dqk_ref[:, step * rows : (step + 1) * rows] = dqk_scr[...].astype(BF)
        dqk_ref.flush(step)
    put_halves(nt(lhs_ref[...], dqk_ref[...]), keep_ref, send_ref, slice(None))


def grad_clip_kernel(x_ref, dmid_ref, dqk_ref, dv_ref, w_ref, mod_ref, out_ref):
    cut = dqk_ref.shape[0]
    rows = x_ref.shape[1]
    both = tn(dqk_ref[...], w_ref[:cut, :]) + tn(dv_ref[...], w_ref[cut:, :])
    for step in range(x_ref.shape[0]):
        grad = both[step * rows : (step + 1) * rows]
        grad = modulate_vjp(x_ref[step].astype(F32), mod_ref, grad)
        out_ref.put(step, (dmid_ref[step].astype(F32) + grad).astype(BF))


def shape(dims, kind=BF):
    return jax.ShapeDtypeStruct(tuple(dims), kind)


def whole(array):
    n = len(array.shape)
    return pl.BlockSpec(array.shape, lambda *_: (0,) * n, pipeline_mode=pl.Buffered(1))


def each(array):
    pass


def lane(array):
    pass


def scalar(array):
    return pl.BlockSpec(memory_space=pltpu.SMEM)


def unused(array):
    return pl.BlockSpec(memory_space=pl.ANY)


def small_call(kernel, grid, ins, outs, scratch, micros, after=()):
    first, arrays = len(ins), [a for a, _ in ins]

    def run(*refs):
        kernel(*refs[:first], *refs[first + len(after) :])

    return pl.pallas_call(
        run,
        grid=grid,
        in_specs=[s(a) for a, s in ins] + [unused(a) for a in after],
        out_specs=[s(a) for a, s in outs],
        out_shape=[a for a, _ in outs],
        scratch_shapes=[pltpu.VMEM(d, k) for d, k in scratch],
        compiler_params=pltpu.CompilerParams(vmem_limit_bytes=SMALL_LIMIT),
        cost_estimate=pl.CostEstimate(
            flops=int(micros * FLOPS_PER_MICRO), bytes_accessed=0, transcendentals=0
        ),
    )(*arrays, *after)


class Plain:
    def __init__(self, held):
        self.held, self.shape = held, held.shape

    def __getitem__(self, index):
        return self.held[index]

    def __setitem__(self, index, value):
        self.held[index] = value

    def put(self, index, value):
        self.held[index] = value

    def flush(self, index=None):
        pass


def block_call(kernel, ins, outs, scratch, micros, after=()):
    def spec(array, kind):
        if kind is scalar:
            return scalar(array)
        n = len(array.shape)
        if isinstance(kind, int):
            return pl.BlockSpec((1,) + tuple(array.shape[1:]), lambda i: (kind,) + (0,) * (n - 1))
        return pl.BlockSpec(tuple(array.shape), lambda i: (0,) * n)

    def run(*refs):
        given, refs = refs[: len(ins)], refs[len(ins) + len(after) :]
        results, own = refs[: len(outs)], refs[len(outs) + 1 :]
        refs[len(outs)][...] = jnp.zeros_like(refs[len(outs)])
        given = [r if k is scalar else Plain(r) for r, (_, k) in zip(given, ins)]
        kernel(*given, *[Plain(r) for r in results], *own)

    token = shape((8, 128), F32)
    return pl.pallas_call(
        run,
        grid=(1,),
        in_specs=[spec(a, k) for a, k in ins] + [unused(a) for a in after],
        out_specs=[spec(a, None) for a, _ in outs] + [spec(token, None)],
        out_shape=[a for a, _ in outs] + [token],
        scratch_shapes=[pltpu.VMEM(d, k) for d, k in scratch],
        compiler_params=pltpu.CompilerParams(vmem_limit_bytes=VMEM_LIMIT),
        cost_estimate=pl.CostEstimate(
            flops=int(micros * FLOPS_PER_MICRO), bytes_accessed=0, transcendentals=0
        ),
    )(*[a for a, _ in ins], *after)


class Source:
    def __init__(self, hbm, buf, pairs, sems, first):
        self.buf, self.shape = buf, buf.shape
        self.copies = [pltpu.make_async_copy(a, b, sems.at[first + i]) for i, (a, b) in enumerate(pairs)]
        self.waiting = set(range(len(self.copies)))

    def wait(self, index):
        wanted = [index] if isinstance(index, int) and len(self.copies) > 1 else range(len(self.copies))
        for i in wanted:
            if i in self.waiting:
                self.copies[i].wait()
                self.waiting.remove(i)

    def __getitem__(self, index):
        self.wait(index[0] if isinstance(index, tuple) else index)
        return self.buf[index]

    def ref(self, index):
        self.wait(index)
        return self.buf.at[index]

    def lanes(self, index):
        self.wait(index)
        size = self.shape[1] // len(self.copies)
        return self.buf[:, index * size : (index + 1) * size]


class Sink:
    def __init__(self, hbm, buf, pairs, sems, first):
        self.buf, self.shape = buf, buf.shape
        self.copies = [pltpu.make_async_copy(b, a, sems.at[first + i]) for i, (a, b) in enumerate(pairs)]
        self.left = set(range(len(self.copies)))

    def __getitem__(self, index):
        return self.buf[index]

    def __setitem__(self, index, value):
        self.buf[index] = value

    def ref(self, index):
        return self.buf.at[index]

    def flush(self, index=None):
        for i in sorted(self.left) if index is None else [index]:
            self.copies[i].start()
            self.left.remove(i)

    def put(self, index, value):
        self.buf[index] = value
        self.flush(index if len(self.copies) > 1 else None)


def cuts(hbm, buf, kind, steps):
    if kind is each:
        return [(hbm.at[i], buf.at[i]) for i in range(buf.shape[0])]
    if kind is lane:
        size = buf.shape[1] // steps
        return [(hbm.at[:, pl.ds(i * size, size)], buf.at[:, pl.ds(i * size, size)]) for i in range(steps)]
    if isinstance(kind, int):
        return [(hbm.at[pl.ds(kind, 1)], buf)]
    if isinstance(kind, tuple):
        size = buf.shape[1]
        return [(hbm.at[:, pl.ds(kind[0] * size, size)], buf)]
    return [(hbm, buf)]


def count_cuts(array, kind, steps):
    return array.shape[0] if kind is each else steps if kind is lane else 1


def call(kernel, steps, ins, outs, scratch, micros, after=(), aliases=None):
    arrays = [a for a, _ in ins]
    moved = [(a, k) for a, k in ins if k is not scalar]
    first_of, total = [], 0
    for a, k in moved + list(outs):
        first_of.append(total)
        total += count_cuts(a, k, steps)

    def buffer(array, kind):
        dims = tuple(array.shape)
        if isinstance(kind, int):
            dims = (1,) + dims[1:]
        if isinstance(kind, tuple):
            dims = (dims[0], dims[1] // steps)
        return pltpu.VMEM(dims, array.dtype)

    def run(*refs):
        given, refs = refs[: len(ins)], refs[len(ins) + len(after) :]
        results, refs = refs[: len(outs)], refs[len(outs) :]
        refs[0][...] = jnp.zeros_like(refs[0])
        refs = refs[1:]
        own, refs = refs[: len(scratch)], refs[len(scratch) :]
        sems, bufs = refs[-1], list(refs[:-1])
        firsts = list(first_of)
        sources = []
        for ref, (_, kind) in zip(given, ins):
            if kind is scalar:
                sources.append(ref)
            else:
                buf = bufs.pop(0)
                sources.append(Source(ref, buf, cuts(ref, buf, kind, steps), sems, firsts.pop(0)))
        sinks = []
        for ref, (_, kind) in zip(results, outs):
            buf = bufs.pop(0)
            sinks.append(Sink(ref, buf, cuts(ref, buf, kind, steps), sems, firsts.pop(0)))
        live = [x for x in sources if isinstance(x, Source)]
        live.sort(key=lambda x: math.prod(x.shape) > 16384)
        for i in range(max(len(x.copies) for x in live)):
            for x in live:
                if i < len(x.copies):
                    x.copies[i].start()
        kernel(*sources, *sinks, *own)
        for x in live:
            for i in sorted(x.waiting):
                x.copies[i].wait()
        for x in sinks:
            x.flush()
        for x in sinks:
            for copy in x.copies:
                copy.wait()

    return pl.pallas_call(
        run,
        in_specs=[scalar(a) if k is scalar else unused(a) for a, k in ins] + [unused(a) for a in after],
        out_specs=[unused(a) for a, _ in outs] + [pl.BlockSpec(memory_space=pltpu.VMEM)],
        out_shape=[a for a, _ in outs] + [shape((8, 128), F32)],
        input_output_aliases=aliases or {},
        scratch_shapes=[pltpu.VMEM(d, k) for d, k in scratch]
        + [buffer(a, k) for a, k in moved + list(outs)]
        + [pltpu.SemaphoreType.DMA((total,))],
        compiler_params=pltpu.CompilerParams(vmem_limit_bytes=VMEM_LIMIT),
        cost_estimate=pl.CostEstimate(
            flops=int(micros * FLOPS_PER_MICRO), bytes_accessed=0, transcendentals=0
        ),
    )(*arrays, *after)


def exchange(value, axis, flip):
    count = lax.axis_size(axis)
    return lax.ppermute(value, axis, [(i, i ^ flip) for i in range(count)])


def added(first, second):
    return first.astype(F32) + second.astype(F32)


def halve_kernel(picks, *refs):
    count = len(refs) - 2 * len(picks)
    terms, outs = refs[:count], refs[count:]
    for at, (pair, columns, kept, sent) in enumerate(picks):
        first, second = terms[pair], terms[pair + 1]
        for out_ref, blocks in ((outs[2 * at], kept), (outs[2 * at + 1], sent)):
            for slot, block in enumerate(blocks):
                out_ref[slot] = added(first[block, :, columns], second[block, :, columns]).astype(BF)


def halved_total(refs):
    return jnp.concatenate(
        [added(refs[i][0], refs[i + 1][0]) for i in range(0, len(refs), 2)], axis=1
    )


def total_kernel(*refs):
    refs[-1][...] = halved_total(refs[:-1]).astype(BF)


def piece_kernel(count, place_ref, *refs):
    terms, outs = refs[:-count], refs[-count:]
    odd = len(terms) % 2
    total = halved_total(terms[odd:])
    if odd:
        total = jnp.concatenate([terms[0][...].astype(F32), total], axis=1)
    size = outs[0].shape[0]
    pieces = [total[i * size : (i + 1) * size] for i in range(count)]
    place = place_ref[0]
    for flip, out_ref in enumerate(outs):
        value = pieces[0]
        for i in range(1, count):
            value = jnp.where(jnp.bitwise_xor(place, flip) == i, pieces[i], value)
        out_ref[...] = value.astype(BF)


def scaled_sum(terms, factor):
    return sum((t.astype(F32) for t in terms[1:]), terms[0].astype(F32)) * factor


def first_last_kernel(width, factor, *refs):
    terms, (qkv_ref, proj_ref, part_ref) = refs[:-3], refs[-3:]
    total = scaled_sum([r[...] for r in terms], factor)
    qkv_ref[...] = total[:, : 3 * width]
    proj_ref[...] = total[:, 3 * width : 4 * width]
    part_ref[...] = total[:, 4 * width :]


def last_kernel(width, factor, part_ref, *refs):
    terms, (qkv_ref, proj_ref) = refs[:-2], refs[-2:]
    qkv_ref[:, : 2 * width] = scaled_sum([r[...] for r in terms], factor)
    qkv_ref[:, 2 * width :] = part_ref[:, :width]
    proj_ref[...] = part_ref[:, width:]


class Halving:
    def __init__(self, keep, send, cut):
        bits = int(math.log2(lax.axis_size("wide"))) - 1
        self.terms = [keep, exchange(send, "wide", 1)]
        self.pairs = [(0, slice(0, cut)), (0, slice(cut, keep.shape[2]))]
        self.left = [list(range(bits))[::-1]] * 2
        self.orders = [list(range(bits)), list(range(bits))[::-1]]
        self.size = keep.shape[1]

    def pending(self):
        return bool(self.orders[0])

    def step(self, after=(), micros=0):
        picks, outs, flips = [], [], []
        for at, (pair, columns) in enumerate(self.pairs):
            bit, left = self.orders[at][0], self.left[at]
            shift = len(left) - 1 - left.index(bit)
            blocks = range(2 ** len(left))
            kept = [i for i in blocks if not (i >> shift) & 1]
            sent = [i for i in blocks if (i >> shift) & 1]
            picks.append((pair, columns, kept, sent))
            wide = len(range(*columns.indices(self.terms[pair].shape[2])))
            outs += [(shape((len(kept), self.size, wide)), whole)] * 2
            flips.append(2 << bit)
        got = small_call(
            functools.partial(halve_kernel, picks), (1,), [(a, whole) for a in self.terms],
            outs, [], micros, after,
        )
        self.terms = []
        for at, flip in enumerate(flips):
            self.terms += [got[2 * at], exchange(got[2 * at + 1], "wide", flip)]
            bit = self.orders[at][0]
            self.left[at] = [b for b in self.left[at] if b != bit]
            self.orders[at] = self.orders[at][1:]
        self.pairs = [(0, slice(None)), (2, slice(None))]
        self.done = got[0]

    def rest(self, after=(), micros=0):
        while self.pending():
            self.step(after, micros)


def body(
    clip_tokens,
    cotangent,
    qkv_spatial,
    proj_spatial,
    adaln_spatial,
    qknorm_spatial,
    qkv_temporal,
    proj_temporal,
    adaln_temporal,
    qknorm_temporal,
):
    steps, patches, depth = clip_tokens.shape
    frames, per_device, _ = cotangent.shape
    hd = qknorm_spatial.shape[1]
    width = proj_spatial.shape[1]
    heads = width // hd
    axes = ("wide", "narrow")
    count = lax.axis_size("wide")
    devices = count * lax.axis_size("narrow")
    parts = 2
    group = per_device // parts
    rows = frames * group
    tokens = steps * patches
    w_s, p_s, w_t, p_t = qkv_spatial.T, proj_spatial.T, qkv_temporal.T, proj_temporal.T
    me = lax.axis_index("wide").astype(jnp.int32).reshape(1)
    half = shape((count // 2, depth // count, 2 * width))
    both = shape((count // 2, depth // count, 4 * width))

    middle, send0, normed_s, qkv_s, att_s, mixed_s, _ = call(
        functools.partial(spatial_forward_kernel, (steps, heads, hd, per_device, group)),
        steps,
        [(clip_tokens, each), (w_s, whole), (p_s, whole), (adaln_spatial, whole),
         (qknorm_spatial, whole)],
        [(shape((tokens, depth)), whole), (shape((rows, depth)), whole),
         (shape((steps, patches, depth)), each),
         (shape((steps, 3 * width, patches), F32), each),
         (shape((steps, heads, patches, patches)), each), (shape((width, tokens)), lane)],
        [((width, patches), F32)],
        17,
    )

    def turn(value):
        value = value.reshape(devices, steps * group, depth)
        value = lax.all_to_all(value, axes, split_axis=0, concat_axis=0, tiled=True)
        return value.reshape(rows, depth)

    flat_cot = cotangent.reshape(frames * per_device, depth)
    send1, lhs_s, turned, branch_t, dmixed_t, _ = block_call(
        functools.partial(between_kernel, (steps, per_device, group, count)),
        [(me, scalar), (middle, whole), (normed_s, whole), (flat_cot, whole), (p_t, whole),
         (adaln_temporal, whole)],
        [(shape((rows, depth)), whole), (shape((depth, tokens)), whole),
         (shape((parts, rows, depth)), each), (shape((parts, rows, depth)), each),
         (shape((parts, width, rows), F32), each)],
        [((depth, tokens), F32)],
        6,
    )
    middles = [turn(send0), turn(send1)]

    received, saved = [], []
    for part in range(parts):
        dmid, *keep, _ = block_call(
            functools.partial(temporal_kernel, (heads, hd, group), part),
            [(middles[part], whole), (turned, part), (dmixed_t, part), (w_t, whole),
             (adaln_temporal, whole), (qknorm_temporal, whole)],
            [(shape((rows, depth)), whole), (shape((rows, depth)), whole),
             (shape((3 * width, rows)), whole), (shape((width, rows)), whole)],
            [((3 * width, rows), F32), ((width, rows), F32), ((3 * width, rows), F32)],
            13,
        )
        received.append(turn(dmid))
        saved.append(keep)
    (normed0, dqkv0, mixed0), (normed1, dqkv1, mixed1) = saved

    keep_t, send_t, _ = block_call(
        functools.partial(temporal_grad_kernel, (width, count)),
        [(me, scalar), (normed0, whole), (normed1, whole), (dqkv0, whole), (dqkv1, whole),
         (mixed0, whole), (mixed1, whole), (branch_t, whole)],
        [(both, whole)] * 2,
        [((depth, parts * rows), F32), ((depth, parts * rows), BF),
         ((3 * width, parts * rows), BF), ((width, parts * rows), BF)],
        0,
        [received[0]],
    )
    sum_t = Halving(keep_t, send_t, 2 * width)
    sum_t.step()
    result, done_result = block_call(
        functools.partial(result_kernel, (per_device, group)),
        [(middles[0], whole), (middles[1], whole), (mixed0, whole), (mixed1, whole), (p_t, whole),
         (adaln_temporal, whole)],
        [(shape((frames * per_device, depth)), whole)],
        [((parts * rows, depth), BF)],
        0,
        [sum_t.done],
    )
    dmid_s, dmixed_s, dv_s, keep_b, send_b, done_v = call(
        functools.partial(spatial_value_kernel, (heads, hd, steps, per_device, group, count)),
        steps,
        [(me, scalar), (received[0], whole), (received[1], whole), (att_s, each), (p_s, whole),
         (adaln_spatial, whole), (lhs_s, whole), (mixed_s, whole)],
        [(shape((steps, patches, depth)), each), (shape((steps, width, patches)), each),
         (shape((width, tokens)), lane), (half, whole), (half, whole)],
        [((width, patches), F32), ((width, patches), F32),
         ((depth, tokens), F32), ((depth, tokens), BF)],
        1,
        [sum_t.done, done_result],
    )
    cut = 128 * -(-2 * width // 256)
    sum_t.rest([done_v], 20)
    sum_b = Halving(keep_b, send_b, cut)
    sum_b.step([sum_t.done])
    dqk_s, keep_a, send_a, done_s = call(
        functools.partial(spatial_score_kernel, (heads, hd, steps)),
        steps,
        [(qkv_s, each), (att_s, each), (dmixed_s, each), (qknorm_spatial, whole), (lhs_s, whole)],
        [(shape((2 * width, tokens)), lane), (half, whole), (half, whole)],
        [((2 * width, patches), F32)],
        11,
        [sum_b.done],
    )
    narrow = lax.axis_size("narrow")
    factor = 1.0 / math.sqrt(frames * patches)
    share = depth // devices
    place = lax.axis_index("narrow").astype(jnp.int32).reshape(1)

    def pieces_of(terms, columns, after):
        pieces = small_call(
            functools.partial(piece_kernel, narrow), (1,),
            [(place, scalar)] + [(a, whole) for a in terms],
            [(shape((share, columns)), whole)] * narrow, [], 20, after,
        )
        return pieces[0], [exchange(p, "narrow", i) if i else p for i, p in enumerate(pieces)]

    (total_t,) = small_call(
        total_kernel, (1,), [(a, whole) for a in sum_t.terms],
        [(shape((depth // count, 4 * width)), whole)], [], 20, [done_s],
    )
    sum_b.rest([total_t])
    sum_a = Halving(keep_a, send_a, cut)
    sum_a.step([sum_b.done], 10)
    first_b, terms_b = pieces_of([total_t] + sum_b.terms, 6 * width, [sum_a.done])
    sum_a.rest([first_b])
    grad_clip, done_clip = call(
        grad_clip_kernel,
        steps,
        [(clip_tokens, each), (dmid_s, each), (dqk_s, lane), (dv_s, lane), (w_s, whole),
         (adaln_spatial, whole)],
        [(shape((steps, patches, depth)), each)],
        [],
        4,
        [sum_a.done],
    )
    first_a, terms_a = pieces_of(sum_a.terms, 2 * width, [done_clip])
    whole_grad, part_grad = shape((share, 3 * width), F32), shape((share, width), F32)
    grad_qkv_t, grad_proj_t, rest = small_call(
        functools.partial(first_last_kernel, width, factor), (1,), [(a, whole) for a in terms_b],
        [(whole_grad, whole), (part_grad, whole), (shape((share, 2 * width), F32), whole)], [], 2,
        [first_a],
    )
    grad_qkv_s, grad_proj_s = small_call(
        functools.partial(last_kernel, width, factor), (1,),
        [(rest, whole)] + [(a, whole) for a in terms_a],
        [(whole_grad, whole), (part_grad, whole)], [], 2,
    )
    return (
        result.reshape(frames, per_device, depth),
        grad_clip,
        grad_qkv_s,
        grad_proj_s,
        grad_qkv_t,
        grad_proj_t,
    )


def solution(mesh):
    tokens = P(("wide", "narrow"), None, None)
    columns = P(None, ("wide", "narrow"), None)
    own = P(("wide", "narrow"), None)
    return jax.shard_map(
        body,
        mesh=mesh,
        in_specs=(tokens, columns) + (P(),) * 8,
        out_specs=(columns, tokens, own, own, own, own),
        check_vma=False,
    )
```

```python
import functools
import math

import jax
import jax.numpy as jnp
from jax import lax
from jax.experimental import pallas as pl
from jax.experimental.pallas import tpu as pltpu
from jax.sharding import PartitionSpec as P

EPS = 1e-06
BF = jnp.bfloat16
F32 = jnp.float32
VMEM_LIMIT = 56 * 1024 * 1024
SMALL_LIMIT = 24 * 1024 * 1024
FLOPS_PER_MICRO = 1.15e9
LOG2E = math.log2(math.e)


def nn(a, b):
    return lax.dot_general(a, b, (((1,), (0,)), ((), ())), preferred_element_type=F32)


def nt(a, b):
    return lax.dot_general(a, b, (((1,), (1,)), ((), ())), preferred_element_type=F32)


def tn(a, b):
    return lax.dot_general(a, b, (((0,), (0,)), ((), ())), preferred_element_type=F32)


def standardize(x):
    centre = x - jnp.mean(x, axis=-1, keepdims=True)
    rate = lax.rsqrt(jnp.mean(centre * centre, axis=-1, keepdims=True) + EPS)
    return centre * rate, rate


def modulated(x, mod_ref):
    return (standardize(x)[0] * (1.0 + mod_ref[1:2, :]) + mod_ref[0:1, :]).astype(BF)


def modulate_vjp(x, mod_ref, grad):
    unit, rate = standardize(x)
    scaled = grad * (1.0 + mod_ref[1:2, :])
    inner = jnp.mean(unit * scaled, axis=-1, keepdims=True)
    return rate * (scaled - jnp.mean(scaled, axis=-1, keepdims=True) - unit * inner)


def column(row):
    n = row.shape[1]
    same = lax.broadcasted_iota(jnp.int32, (n, n), 0) == lax.broadcasted_iota(jnp.int32, (n, n), 1)
    return jnp.sum(jnp.where(same, jnp.broadcast_to(row, (n, n)), 0.0), axis=1, keepdims=True)


def unit_rms(vectors):
    rate = lax.rsqrt(jnp.mean(vectors * vectors, axis=0, keepdims=True) + EPS)
    return vectors * rate, rate


def row_numbers(rows):
    return lax.broadcasted_iota(jnp.int32, (rows, 1), 0)


def one_hot(base, columns):
    src = lax.broadcasted_iota(jnp.int32, (base.shape[0], columns), 1)
    return (src == base).astype(F32).astype(BF)


def same_column(rows, stride):
    first = row_numbers(rows)
    second = lax.broadcasted_iota(jnp.int32, (1, rows), 1)
    return lax.rem(first, stride) == lax.rem(second, stride)


def head_parts(qkv_ref, head, hd, width):
    at = head * hd
    return (
        qkv_ref[at : at + hd, :],
        qkv_ref[width + at : width + at + hd, :],
        qkv_ref[2 * width + at : 2 * width + at + hd, :],
    )


def head_weights(q_unit, k_unit, gq, gk, mask, hd):
    qn = (q_unit * (gq * (LOG2E / math.sqrt(hd)))).astype(BF)
    kn = (k_unit * gk).astype(BF)
    weights = jnp.exp2(tn(kn, qn))
    if mask is not None:
        weights = jnp.where(mask, weights, 0.0)
    return (weights * (1.0 / jnp.sum(weights, axis=0, keepdims=True))).astype(BF)


def score_vjp(q, k, v16, weights, grad16, gq, gk, hd):
    q_unit, q_rate = unit_rms(q)
    k_unit, k_rate = unit_rms(k)
    scale = 1.0 / math.sqrt(hd)
    w32 = weights.astype(F32)
    weighted = w32 * tn(v16, grad16)
    d_s = (weighted - w32 * jnp.sum(weighted, axis=0, keepdims=True)).astype(BF)
    d_q = nn((k_unit * gk).astype(BF), d_s) * (gq * scale)
    d_k = nt((q_unit * gq).astype(BF), d_s) * (gk * scale)
    d_q = q_rate * (d_q - q_unit * jnp.mean(q_unit * d_q, axis=0, keepdims=True))
    d_k = k_rate * (d_k - k_unit * jnp.mean(k_unit * d_k, axis=0, keepdims=True))
    return d_q, d_k


def arrange(tr_ref, lhs_ref, me, count):
    size = lhs_ref.shape[0] // count
    for slot in range(count):
        place = (slot % (count // 2)) * 2 + slot // (count // 2)
        start = pl.multiple_of(jnp.bitwise_xor(me, place) * size, 8)
        lhs_ref[slot * size : (slot + 1) * size, :] = tr_ref[pl.ds(start, size), :].astype(BF)


def put_halves(value, keep_ref, send_ref, columns):
    half, size = keep_ref.shape[0], keep_ref.shape[1]
    for slot in range(half):
        keep_ref[slot, :, columns] = value[slot * size : (slot + 1) * size].astype(BF)
        send_ref[slot, :, columns] = value[(half + slot) * size : (half + slot + 1) * size].astype(BF)


def pick_group(dims, part, mid_ref, send_ref):
    steps, per_device, group = dims
    out_rows, in_rows = send_ref.shape[0], mid_ref.shape[0]
    out = row_numbers(out_rows)
    owner, rest = out // (steps * group), lax.rem(out, steps * group)
    base = (rest // group) * (in_rows // steps) + owner * per_device + lax.rem(rest, group)
    send_ref[...] = nn(one_hot(base + part * group, in_rows), mid_ref[...]).astype(BF)


def spatial_forward_kernel(
    dims, x_ref, w_ref, p_ref, mod_ref, gain_ref,
    mid_ref, send_ref, normed_ref, qkv_ref, att_ref, mixed_ref, mixed_scr,
):
    steps, heads, hd, per_device, group = dims
    rows = x_ref.shape[1]
    width = heads * hd
    gq, gk = column(gain_ref[0:1, :]), column(gain_ref[1:2, :])
    for step in range(steps):
        x = x_ref[step].astype(F32)
        normed = modulated(x, mod_ref)
        normed_ref.put(step, normed)
        qkv_ref.put(step, nt(w_ref[...], normed))
        for head in range(heads):
            q, k, v = head_parts(qkv_ref.ref(step), head, hd, width)
            weights = head_weights(unit_rms(q)[0], unit_rms(k)[0], gq, gk, None, hd)
            att_ref[step, head] = weights
            mixed_scr[head * hd : (head + 1) * hd, :] = nn(v.astype(BF), weights)
        att_ref.flush(step)
        mixed = mixed_scr[...].astype(BF)
        mixed_ref[:, step * rows : (step + 1) * rows] = mixed
        mixed_ref.flush(step)
        mid_ref[step * rows : (step + 1) * rows, :] = (
            x + mod_ref[2:3, :] * tn(mixed, p_ref[...])
        ).astype(BF)
    mid_ref.flush()
    pick_group((steps, per_device, group), 0, mid_ref, send_ref)


def between_kernel(
    dims, me_ref, mid_ref, normed_ref, cot_ref, p_ref, mod_ref,
    send_ref, lhs_ref, turned_ref, branch_ref, grad_ref, tr_scr,
):
    steps, per_device, group, count = dims
    pick_group((steps, per_device, group), 1, mid_ref, send_ref)
    send_ref.flush()
    out_rows, in_rows = turned_ref.shape[1], cot_ref.shape[0]
    out = row_numbers(out_rows)
    base = (out // group) * per_device + lax.rem(out, group)
    for part in range(turned_ref.shape[0]):
        turned = nn(one_hot(base + part * group, in_rows), cot_ref[...])
        turned_ref.put(part, turned.astype(BF))
        branch = (mod_ref[2:3, :] * turned).astype(BF)
        branch_ref.put(part, branch)
        grad_ref.put(part, nt(p_ref[...], branch))
    rows = normed_ref.shape[1]
    for step in range(steps):
        tr_scr[:, step * rows : (step + 1) * rows] = normed_ref[step].astype(F32).T
    arrange(tr_scr, lhs_ref, me_ref[0], count)


def temporal_kernel(
    dims, part, mid_ref, turned_ref, grad_ref, w_ref, mod_ref, gain_ref,
    dmid_ref, normed_ref, dqkv_ref, mixed_ref, qkv_scr, mixed_scr, dqkv_scr,
):
    heads, hd, group = dims
    width = heads * hd
    rows = mid_ref.shape[0]
    x = mid_ref[...].astype(F32)
    normed = modulated(x, mod_ref)
    normed_ref.put(..., normed)
    qkv_scr[...] = nt(w_ref[...], normed)
    gq, gk = column(gain_ref[0:1, :]), column(gain_ref[1:2, :])
    mask = same_column(rows, group) if group > 1 else None
    for head in range(heads):
        q, k, v = head_parts(qkv_scr, head, hd, width)
        at = head * hd
        v16 = v.astype(BF)
        weights = head_weights(unit_rms(q)[0], unit_rms(k)[0], gq, gk, mask, hd)
        mixed_scr[at : at + hd, :] = nn(v16, weights)
        grad16 = grad_ref[0, at : at + hd, :].astype(BF)
        d_q, d_k = score_vjp(q, k, v16, weights, grad16, gq, gk, hd)
        dqkv_scr[at : at + hd, :] = d_q
        dqkv_scr[width + at : width + at + hd, :] = d_k
        dqkv_scr[2 * width + at : 2 * width + at + hd, :] = nt(grad16, weights)
    mixed_ref.put(..., mixed_scr[...].astype(BF))
    dqkv = dqkv_scr[...].astype(BF)
    dqkv_ref.put(..., dqkv)
    grad = modulate_vjp(x, mod_ref, tn(dqkv, w_ref[...]))
    dmid_ref[...] = (turned_ref[0].astype(F32) + grad).astype(BF)


def temporal_grad_kernel(
    dims, me_ref, normed0_ref, normed1_ref, dqkv0_ref, dqkv1_ref, mixed0_ref, mixed1_ref,
    branch_ref, keep_ref, send_ref,
    tr_scr, lhs_scr, dqkv_scr, mixed_scr,
):
    width, count = dims
    rows = normed0_ref.shape[0]
    for part, (normed, dqkv, mixed) in enumerate(
        ((normed0_ref, dqkv0_ref, mixed0_ref), (normed1_ref, dqkv1_ref, mixed1_ref))
    ):
        at = slice(part * rows, (part + 1) * rows)
        tr_scr[:, at] = normed[...].astype(F32).T
        dqkv_scr[:, at] = dqkv[...]
        mixed_scr[:, at] = mixed[...]
    arrange(tr_scr, lhs_scr, me_ref[0], count)
    put_halves(nt(lhs_scr[...], dqkv_scr[...]), keep_ref, send_ref, slice(0, 3 * width))
    for part in range(2):
        tr_scr[:, part * rows : (part + 1) * rows] = branch_ref[part].astype(F32).T
    arrange(tr_scr, lhs_scr, me_ref[0], count)
    put_halves(nt(lhs_scr[...], mixed_scr[...]), keep_ref, send_ref, slice(3 * width, 4 * width))


def result_kernel(
    dims, mid0_ref, mid1_ref, mixed0_ref, mixed1_ref, p_ref, mod_ref, out_ref, scr
):
    per_device, group = dims
    rows = mid0_ref.shape[0]
    for part, (mid, mixed) in enumerate(((mid0_ref, mixed0_ref), (mid1_ref, mixed1_ref))):
        scr[part * rows : (part + 1) * rows, :] = (
            mid[...].astype(F32) + mod_ref[2:3, :] * tn(mixed[...], p_ref[...])
        ).astype(BF)
    out_rows = out_ref.shape[0]
    out = row_numbers(out_rows)
    col = lax.rem(out, per_device)
    base = (col // group) * rows + (out // per_device) * group + lax.rem(col, group)
    out_ref[...] = nn(one_hot(base, out_rows), scr[...]).astype(BF)


def spatial_value_kernel(
    dims, me_ref, recv0_ref, recv1_ref, att_ref, p_ref, mod_ref, lhs_ref, mixed_ref,
    dmid_ref, grad_ref, dv_ref, keep_ref, send_ref,
    grad_scr, dv_scr, tr_scr, lhs_scr,
):
    heads, hd, steps, per_device, group, count = dims
    width = heads * hd
    rows, in_rows = dmid_ref.shape[1], recv0_ref.shape[0]
    out = row_numbers(rows)
    owner, col = out // per_device, lax.rem(out, per_device)
    for step in range(steps):
        base = owner * (steps * group) + step * group + lax.rem(col, group)
        part = col // group
        dmid = nn(one_hot(jnp.where(part == 0, base, -1), in_rows), recv0_ref[...])
        dmid += nn(one_hot(jnp.where(part == 1, base, -1), in_rows), recv1_ref[...])
        dmid_ref.put(step, dmid.astype(BF))
        branch = (mod_ref[2:3, :] * dmid).astype(BF)
        here = slice(step * rows, (step + 1) * rows)
        tr_scr[:, here] = branch.astype(F32).T
        grad_scr[...] = nt(p_ref[...], branch)
        grad_ref.put(step, grad_scr[...].astype(BF))
        for head in range(heads):
            at = slice(head * hd, (head + 1) * hd)
            dv_scr[at, :] = nt(grad_scr[at, :].astype(BF), att_ref[step, head])
        dv_ref[:, here] = dv_scr[...].astype(BF)
        dv_ref.flush(step)
    put_halves(nt(lhs_ref[...], dv_ref[...]), keep_ref, send_ref, slice(0, width))
    arrange(tr_scr, lhs_scr, me_ref[0], count)
    put_halves(nt(lhs_scr[...], mixed_ref[...]), keep_ref, send_ref, slice(width, 2 * width))


def spatial_score_kernel(
    dims, qkv_ref, att_ref, grad_ref, gain_ref, lhs_ref,
    dqk_ref, keep_ref, send_ref, dqk_scr,
):
    heads, hd, steps = dims
    width = heads * hd
    rows = qkv_ref.shape[2]
    gq, gk = column(gain_ref[0:1, :]), column(gain_ref[1:2, :])
    for step in range(steps):
        for head in range(heads):
            q, k, v = head_parts(qkv_ref.ref(step), head, hd, width)
            at = head * hd
            grad16 = grad_ref[step, at : at + hd, :]
            d_q, d_k = score_vjp(q, k, v.astype(BF), att_ref[step, head], grad16, gq, gk, hd)
            dqk_scr[at : at + hd, :] = d_q
            dqk_scr[width + at : width + at + hd, :] = d_k
        dqk_ref[:, step * rows : (step + 1) * rows] = dqk_scr[...].astype(BF)
        dqk_ref.flush(step)
    put_halves(nt(lhs_ref[...], dqk_ref[...]), keep_ref, send_ref, slice(None))


def grad_clip_kernel(x_ref, dmid_ref, dqk_ref, dv_ref, w_ref, mod_ref, out_ref):
    cut = dqk_ref.shape[0]
    rows = x_ref.shape[1]
    both = tn(dqk_ref[...], w_ref[:cut, :]) + tn(dv_ref[...], w_ref[cut:, :])
    for step in range(x_ref.shape[0]):
        grad = both[step * rows : (step + 1) * rows]
        grad = modulate_vjp(x_ref[step].astype(F32), mod_ref, grad)
        out_ref.put(step, (dmid_ref[step].astype(F32) + grad).astype(BF))


def shape(dims, kind=BF):
    return jax.ShapeDtypeStruct(tuple(dims), kind)


def whole(array):
    n = len(array.shape)
    return pl.BlockSpec(array.shape, lambda *_: (0,) * n, pipeline_mode=pl.Buffered(1))


def each(array):
    pass


def lane(array):
    pass


def scalar(array):
    return pl.BlockSpec(memory_space=pltpu.SMEM)


def unused(array):
    return pl.BlockSpec(memory_space=pl.ANY)


def small_call(kernel, grid, ins, outs, scratch, micros, after=()):
    first, arrays = len(ins), [a for a, _ in ins]

    def run(*refs):
        kernel(*refs[:first], *refs[first + len(after) :])

    return pl.pallas_call(
        run,
        grid=grid,
        in_specs=[s(a) for a, s in ins] + [unused(a) for a in after],
        out_specs=[s(a) for a, s in outs],
        out_shape=[a for a, _ in outs],
        scratch_shapes=[pltpu.VMEM(d, k) for d, k in scratch],
        compiler_params=pltpu.CompilerParams(vmem_limit_bytes=SMALL_LIMIT),
        cost_estimate=pl.CostEstimate(
            flops=int(micros * FLOPS_PER_MICRO), bytes_accessed=0, transcendentals=0
        ),
    )(*arrays, *after)


class Plain:
    def __init__(self, held):
        self.held, self.shape = held, held.shape

    def __getitem__(self, index):
        return self.held[index]

    def __setitem__(self, index, value):
        self.held[index] = value

    def put(self, index, value):
        self.held[index] = value

    def flush(self, index=None):
        pass


def block_call(kernel, ins, outs, scratch, micros, after=()):
    def spec(array, kind):
        if kind is scalar:
            return scalar(array)
        n = len(array.shape)
        if isinstance(kind, int):
            return pl.BlockSpec((1,) + tuple(array.shape[1:]), lambda i: (kind,) + (0,) * (n - 1))
        return pl.BlockSpec(tuple(array.shape), lambda i: (0,) * n)

    def run(*refs):
        given, refs = refs[: len(ins)], refs[len(ins) + len(after) :]
        results, own = refs[: len(outs)], refs[len(outs) + 1 :]
        refs[len(outs)][...] = jnp.zeros_like(refs[len(outs)])
        given = [r if k is scalar else Plain(r) for r, (_, k) in zip(given, ins)]
        kernel(*given, *[Plain(r) for r in results], *own)

    token = shape((8, 128), F32)
    return pl.pallas_call(
        run,
        grid=(1,),
        in_specs=[spec(a, k) for a, k in ins] + [unused(a) for a in after],
        out_specs=[spec(a, None) for a, _ in outs] + [spec(token, None)],
        out_shape=[a for a, _ in outs] + [token],
        scratch_shapes=[pltpu.VMEM(d, k) for d, k in scratch],
        compiler_params=pltpu.CompilerParams(vmem_limit_bytes=VMEM_LIMIT),
        cost_estimate=pl.CostEstimate(
            flops=int(micros * FLOPS_PER_MICRO), bytes_accessed=0, transcendentals=0
        ),
    )(*[a for a, _ in ins], *after)


class Source:
    def __init__(self, hbm, buf, pairs, sems, first):
        self.buf, self.shape = buf, buf.shape
        self.copies = [pltpu.make_async_copy(a, b, sems.at[first + i]) for i, (a, b) in enumerate(pairs)]
        self.waiting = set(range(len(self.copies)))

    def wait(self, index):
        wanted = [index] if isinstance(index, int) and len(self.copies) > 1 else range(len(self.copies))
        for i in wanted:
            if i in self.waiting:
                self.copies[i].wait()
                self.waiting.remove(i)

    def __getitem__(self, index):
        self.wait(index[0] if isinstance(index, tuple) else index)
        return self.buf[index]

    def ref(self, index):
        self.wait(index)
        return self.buf.at[index]

    def lanes(self, index):
        self.wait(index)
        size = self.shape[1] // len(self.copies)
        return self.buf[:, index * size : (index + 1) * size]


class Sink:
    def __init__(self, hbm, buf, pairs, sems, first):
        self.buf, self.shape = buf, buf.shape
        self.copies = [pltpu.make_async_copy(b, a, sems.at[first + i]) for i, (a, b) in enumerate(pairs)]
        self.left = set(range(len(self.copies)))

    def __getitem__(self, index):
        return self.buf[index]

    def __setitem__(self, index, value):
        self.buf[index] = value

    def ref(self, index):
        return self.buf.at[index]

    def flush(self, index=None):
        for i in sorted(self.left) if index is None else [index]:
            self.copies[i].start()
            self.left.remove(i)

    def put(self, index, value):
        self.buf[index] = value
        self.flush(index if len(self.copies) > 1 else None)


def cuts(hbm, buf, kind, steps):
    if kind is each:
        return [(hbm.at[i], buf.at[i]) for i in range(buf.shape[0])]
    if kind is lane:
        size = buf.shape[1] // steps
        return [(hbm.at[:, pl.ds(i * size, size)], buf.at[:, pl.ds(i * size, size)]) for i in range(steps)]
    if isinstance(kind, int):
        return [(hbm.at[pl.ds(kind, 1)], buf)]
    if isinstance(kind, tuple):
        size = buf.shape[1]
        return [(hbm.at[:, pl.ds(kind[0] * size, size)], buf)]
    return [(hbm, buf)]


def count_cuts(array, kind, steps):
    return array.shape[0] if kind is each else steps if kind is lane else 1


def call(kernel, steps, ins, outs, scratch, micros, after=(), aliases=None):
    arrays = [a for a, _ in ins]
    moved = [(a, k) for a, k in ins if k is not scalar]
    first_of, total = [], 0
    for a, k in moved + list(outs):
        first_of.append(total)
        total += count_cuts(a, k, steps)

    def buffer(array, kind):
        dims = tuple(array.shape)
        if isinstance(kind, int):
            dims = (1,) + dims[1:]
        if isinstance(kind, tuple):
            dims = (dims[0], dims[1] // steps)
        return pltpu.VMEM(dims, array.dtype)

    def run(*refs):
        given, refs = refs[: len(ins)], refs[len(ins) + len(after) :]
        results, refs = refs[: len(outs)], refs[len(outs) :]
        refs[0][...] = jnp.zeros_like(refs[0])
        refs = refs[1:]
        own, refs = refs[: len(scratch)], refs[len(scratch) :]
        sems, bufs = refs[-1], list(refs[:-1])
        firsts = list(first_of)
        sources = []
        for ref, (_, kind) in zip(given, ins):
            if kind is scalar:
                sources.append(ref)
            else:
                buf = bufs.pop(0)
                sources.append(Source(ref, buf, cuts(ref, buf, kind, steps), sems, firsts.pop(0)))
        sinks = []
        for ref, (_, kind) in zip(results, outs):
            buf = bufs.pop(0)
            sinks.append(Sink(ref, buf, cuts(ref, buf, kind, steps), sems, firsts.pop(0)))
        live = [x for x in sources if isinstance(x, Source)]
        live.sort(key=lambda x: math.prod(x.shape) > 16384)
        for i in range(max(len(x.copies) for x in live)):
            for x in live:
                if i < len(x.copies):
                    x.copies[i].start()
        kernel(*sources, *sinks, *own)
        for x in live:
            for i in sorted(x.waiting):
                x.copies[i].wait()
        for x in sinks:
            x.flush()
        for x in sinks:
            for copy in x.copies:
                copy.wait()

    return pl.pallas_call(
        run,
        in_specs=[scalar(a) if k is scalar else unused(a) for a, k in ins] + [unused(a) for a in after],
        out_specs=[unused(a) for a, _ in outs] + [pl.BlockSpec(memory_space=pltpu.VMEM)],
        out_shape=[a for a, _ in outs] + [shape((8, 128), F32)],
        input_output_aliases=aliases or {},
        scratch_shapes=[pltpu.VMEM(d, k) for d, k in scratch]
        + [buffer(a, k) for a, k in moved + list(outs)]
        + [pltpu.SemaphoreType.DMA((total,))],
        compiler_params=pltpu.CompilerParams(vmem_limit_bytes=VMEM_LIMIT),
        cost_estimate=pl.CostEstimate(
            flops=int(micros * FLOPS_PER_MICRO), bytes_accessed=0, transcendentals=0
        ),
    )(*arrays, *after)


def exchange(value, axis, flip):
    count = lax.axis_size(axis)
    return lax.ppermute(value, axis, [(i, i ^ flip) for i in range(count)])


def added(first, second):
    return first.astype(F32) + second.astype(F32)


def halve_kernel(picks, *refs):
    count = len(refs) - 2 * len(picks)
    terms, outs = refs[:count], refs[count:]
    for at, (pair, columns, kept, sent) in enumerate(picks):
        first, second = terms[pair], terms[pair + 1]
        for out_ref, blocks in ((outs[2 * at], kept), (outs[2 * at + 1], sent)):
            for slot, block in enumerate(blocks):
                out_ref[slot] = added(first[block, :, columns], second[block, :, columns]).astype(BF)


def halved_total(refs):
    return jnp.concatenate(
        [added(refs[i][0], refs[i + 1][0]) for i in range(0, len(refs), 2)], axis=1
    )


def total_kernel(*refs):
    refs[-1][...] = halved_total(refs[:-1]).astype(BF)


def piece_kernel(count, place_ref, *refs):
    terms, outs = refs[:-count], refs[-count:]
    odd = len(terms) % 2
    total = halved_total(terms[odd:])
    if odd:
        total = jnp.concatenate([terms[0][...].astype(F32), total], axis=1)
    size = outs[0].shape[0]
    pieces = [total[i * size : (i + 1) * size] for i in range(count)]
    place = place_ref[0]
    for flip, out_ref in enumerate(outs):
        value = pieces[0]
        for i in range(1, count):
            value = jnp.where(jnp.bitwise_xor(place, flip) == i, pieces[i], value)
        out_ref[...] = value.astype(BF)


def scaled_sum(terms, factor):
    return sum((t.astype(F32) for t in terms[1:]), terms[0].astype(F32)) * factor


def first_last_kernel(width, factor, *refs):
    terms, (qkv_ref, proj_ref, part_ref) = refs[:-3], refs[-3:]
    total = scaled_sum([r[...] for r in terms], factor)
    qkv_ref[...] = total[:, : 3 * width]
    proj_ref[...] = total[:, 3 * width : 4 * width]
    part_ref[...] = total[:, 4 * width :]


def last_kernel(width, factor, part_ref, *refs):
    terms, (qkv_ref, proj_ref) = refs[:-2], refs[-2:]
    qkv_ref[:, : 2 * width] = scaled_sum([r[...] for r in terms], factor)
    qkv_ref[:, 2 * width :] = part_ref[:, :width]
    proj_ref[...] = part_ref[:, width:]


class Halving:
    def __init__(self, keep, send, cut):
        bits = int(math.log2(lax.axis_size("wide"))) - 1
        self.terms = [keep, exchange(send, "wide", 1)]
        self.pairs = [(0, slice(0, cut)), (0, slice(cut, keep.shape[2]))]
        self.left = [list(range(bits))[::-1]] * 2
        self.orders = [list(range(bits)), list(range(bits))[::-1]]
        self.size = keep.shape[1]

    def pending(self):
        return bool(self.orders[0])

    def step(self, after=(), micros=0):
        picks, outs, flips = [], [], []
        for at, (pair, columns) in enumerate(self.pairs):
            bit, left = self.orders[at][0], self.left[at]
            shift = len(left) - 1 - left.index(bit)
            blocks = range(2 ** len(left))
            kept = [i for i in blocks if not (i >> shift) & 1]
            sent = [i for i in blocks if (i >> shift) & 1]
            picks.append((pair, columns, kept, sent))
            wide = len(range(*columns.indices(self.terms[pair].shape[2])))
            outs += [(shape((len(kept), self.size, wide)), whole)] * 2
            flips.append(2 << bit)
        got = small_call(
            functools.partial(halve_kernel, picks), (1,), [(a, whole) for a in self.terms],
            outs, [], micros, after,
        )
        self.terms = []
        for at, flip in enumerate(flips):
            self.terms += [got[2 * at], exchange(got[2 * at + 1], "wide", flip)]
            bit = self.orders[at][0]
            self.left[at] = [b for b in self.left[at] if b != bit]
            self.orders[at] = self.orders[at][1:]
        self.pairs = [(0, slice(None)), (2, slice(None))]
        self.done = got[0]

    def rest(self, after=(), micros=0):
        while self.pending():
            self.step(after, micros)


def body(
    clip_tokens,
    cotangent,
    qkv_spatial,
    proj_spatial,
    adaln_spatial,
    qknorm_spatial,
    qkv_temporal,
    proj_temporal,
    adaln_temporal,
    qknorm_temporal,
):
    steps, patches, depth = clip_tokens.shape
    frames, per_device, _ = cotangent.shape
    hd = qknorm_spatial.shape[1]
    width = proj_spatial.shape[1]
    heads = width // hd
    axes = ("wide", "narrow")
    count = lax.axis_size("wide")
    devices = count * lax.axis_size("narrow")
    parts = 2
    group = per_device // parts
    rows = frames * group
    tokens = steps * patches
    w_s, p_s, w_t, p_t = qkv_spatial.T, proj_spatial.T, qkv_temporal.T, proj_temporal.T
    me = lax.axis_index("wide").astype(jnp.int32).reshape(1)
    half = shape((count // 2, depth // count, 2 * width))
    both = shape((count // 2, depth // count, 4 * width))

    middle, send0, normed_s, qkv_s, att_s, mixed_s, _ = call(
        functools.partial(spatial_forward_kernel, (steps, heads, hd, per_device, group)),
        steps,
        [(clip_tokens, each), (w_s, whole), (p_s, whole), (adaln_spatial, whole),
         (qknorm_spatial, whole)],
        [(shape((tokens, depth)), whole), (shape((rows, depth)), whole),
         (shape((steps, patches, depth)), each),
         (shape((steps, 3 * width, patches), F32), each),
         (shape((steps, heads, patches, patches)), each), (shape((width, tokens)), lane)],
        [((width, patches), F32)],
        17,
    )

    def turn(value):
        value = value.reshape(devices, steps * group, depth)
        value = lax.all_to_all(value, axes, split_axis=0, concat_axis=0, tiled=True)
        return value.reshape(rows, depth)

    flat_cot = cotangent.reshape(frames * per_device, depth)
    send1, lhs_s, turned, branch_t, dmixed_t, _ = block_call(
        functools.partial(between_kernel, (steps, per_device, group, count)),
        [(me, scalar), (middle, whole), (normed_s, whole), (flat_cot, whole), (p_t, whole),
         (adaln_temporal, whole)],
        [(shape((rows, depth)), whole), (shape((depth, tokens)), whole),
         (shape((parts, rows, depth)), each), (shape((parts, rows, depth)), each),
         (shape((parts, width, rows), F32), each)],
        [((depth, tokens), F32)],
        6,
    )
    middles = [turn(send0), turn(send1)]

    received, saved = [], []
    for part in range(parts):
        dmid, *keep, _ = block_call(
            functools.partial(temporal_kernel, (heads, hd, group), part),
            [(middles[part], whole), (turned, part), (dmixed_t, part), (w_t, whole),
             (adaln_temporal, whole), (qknorm_temporal, whole)],
            [(shape((rows, depth)), whole), (shape((rows, depth)), whole),
             (shape((3 * width, rows)), whole), (shape((width, rows)), whole)],
            [((3 * width, rows), F32), ((width, rows), F32), ((3 * width, rows), F32)],
            13,
        )
        received.append(turn(dmid))
        saved.append(keep)
    (normed0, dqkv0, mixed0), (normed1, dqkv1, mixed1) = saved

    keep_t, send_t, _ = block_call(
        functools.partial(temporal_grad_kernel, (width, count)),
        [(me, scalar), (normed0, whole), (normed1, whole), (dqkv0, whole), (dqkv1, whole),
         (mixed0, whole), (mixed1, whole), (branch_t, whole)],
        [(both, whole)] * 2,
        [((depth, parts * rows), F32), ((depth, parts * rows), BF),
         ((3 * width, parts * rows), BF), ((width, parts * rows), BF)],
        0,
        [received[0]],
    )
    sum_t = Halving(keep_t, send_t, 2 * width)
    sum_t.step()
    result, done_result = block_call(
        functools.partial(result_kernel, (per_device, group)),
        [(middles[0], whole), (middles[1], whole), (mixed0, whole), (mixed1, whole), (p_t, whole),
         (adaln_temporal, whole)],
        [(shape((frames * per_device, depth)), whole)],
        [((parts * rows, depth), BF)],
        0,
        [sum_t.done],
    )
    dmid_s, dmixed_s, dv_s, keep_b, send_b, done_v = call(
        functools.partial(spatial_value_kernel, (heads, hd, steps, per_device, group, count)),
        steps,
        [(me, scalar), (received[0], whole), (received[1], whole), (att_s, each), (p_s, whole),
         (adaln_spatial, whole), (lhs_s, whole), (mixed_s, whole)],
        [(shape((steps, patches, depth)), each), (shape((steps, width, patches)), each),
         (shape((width, tokens)), lane), (half, whole), (half, whole)],
        [((width, patches), F32), ((width, patches), F32),
         ((depth, tokens), F32), ((depth, tokens), BF)],
        1,
        [sum_t.done, done_result],
    )
    cut = 128 * -(-2 * width // 256)
    sum_t.rest([done_v], 20)
    sum_b = Halving(keep_b, send_b, cut)
    sum_b.step([sum_t.done])
    dqk_s, keep_a, send_a, done_s = call(
        functools.partial(spatial_score_kernel, (heads, hd, steps)),
        steps,
        [(qkv_s, each), (att_s, each), (dmixed_s, each), (qknorm_spatial, whole), (lhs_s, whole)],
        [(shape((2 * width, tokens)), lane), (half, whole), (half, whole)],
        [((2 * width, patches), F32)],
        11,
        [sum_b.done],
    )
    narrow = lax.axis_size("narrow")
    factor = 1.0 / math.sqrt(frames * patches)
    share = depth // devices
    place = lax.axis_index("narrow").astype(jnp.int32).reshape(1)

    def pieces_of(terms, columns, after):
        pieces = small_call(
            functools.partial(piece_kernel, narrow), (1,),
            [(place, scalar)] + [(a, whole) for a in terms],
            [(shape((share, columns)), whole)] * narrow, [], 20, after,
        )
        return pieces[0], [exchange(p, "narrow", i) if i else p for i, p in enumerate(pieces)]

    (total_t,) = small_call(
        total_kernel, (1,), [(a, whole) for a in sum_t.terms],
        [(shape((depth // count, 4 * width)), whole)], [], 20, [done_s],
    )
    sum_b.rest([total_t])
    sum_a = Halving(keep_a, send_a, cut)
    sum_a.step([sum_b.done], 10)
    first_b, terms_b = pieces_of([total_t] + sum_b.terms, 6 * width, [sum_a.done])
    sum_a.rest([first_b])
    first_a, terms_a = pieces_of(sum_a.terms, 2 * width, [])
    grad_clip, done_clip = call(
        grad_clip_kernel,
        steps,
        [(clip_tokens, each), (dmid_s, each), (dqk_s, lane), (dv_s, lane), (w_s, whole),
         (adaln_spatial, whole)],
        [(shape((steps, patches, depth)), each)],
        [],
        4,
        [first_a],
    )
    whole_grad, part_grad = shape((share, 3 * width), F32), shape((share, width), F32)
    grad_qkv_t, grad_proj_t, rest = small_call(
        functools.partial(first_last_kernel, width, factor), (1,), [(a, whole) for a in terms_b],
        [(whole_grad, whole), (part_grad, whole), (shape((share, 2 * width), F32), whole)], [], 2,
        [done_clip],
    )
    grad_qkv_s, grad_proj_s = small_call(
        functools.partial(last_kernel, width, factor), (1,),
        [(rest, whole)] + [(a, whole) for a in terms_a],
        [(whole_grad, whole), (part_grad, whole)], [], 2,
    )
    return (
        result.reshape(frames, per_device, depth),
        grad_clip,
        grad_qkv_s,
        grad_proj_s,
        grad_qkv_t,
        grad_proj_t,
    )


def solution(mesh):
    tokens = P(("wide", "narrow"), None, None)
    columns = P(None, ("wide", "narrow"), None)
    own = P(("wide", "narrow"), None)
    return jax.shard_map(
        body,
        mesh=mesh,
        in_specs=(tokens, columns) + (P(),) * 8,
        out_specs=(columns, tokens, own, own, own, own),
        check_vma=False,
    )
```

```python
import functools
import math

import jax
import jax.numpy as jnp
from jax import lax
from jax.experimental import pallas as pl
from jax.experimental.pallas import tpu as pltpu
from jax.sharding import PartitionSpec as P

EPS = 1e-06
BF = jnp.bfloat16
F32 = jnp.float32
VMEM_LIMIT = 56 * 1024 * 1024
SMALL_LIMIT = 24 * 1024 * 1024
FLOPS_PER_MICRO = 1.15e9
LOG2E = math.log2(math.e)


def nn(a, b):
    return lax.dot_general(a, b, (((1,), (0,)), ((), ())), preferred_element_type=F32)


def nt(a, b):
    return lax.dot_general(a, b, (((1,), (1,)), ((), ())), preferred_element_type=F32)


def tn(a, b):
    return lax.dot_general(a, b, (((0,), (0,)), ((), ())), preferred_element_type=F32)


def standardize(x):
    centre = x - jnp.mean(x, axis=-1, keepdims=True)
    rate = lax.rsqrt(jnp.mean(centre * centre, axis=-1, keepdims=True) + EPS)
    return centre * rate, rate


def modulated(x, mod_ref):
    return (standardize(x)[0] * (1.0 + mod_ref[1:2, :]) + mod_ref[0:1, :]).astype(BF)


def modulate_vjp(x, mod_ref, grad):
    unit, rate = standardize(x)
    scaled = grad * (1.0 + mod_ref[1:2, :])
    inner = jnp.mean(unit * scaled, axis=-1, keepdims=True)
    return rate * (scaled - jnp.mean(scaled, axis=-1, keepdims=True) - unit * inner)


def column(row):
    n = row.shape[1]
    same = lax.broadcasted_iota(jnp.int32, (n, n), 0) == lax.broadcasted_iota(jnp.int32, (n, n), 1)
    return jnp.sum(jnp.where(same, jnp.broadcast_to(row, (n, n)), 0.0), axis=1, keepdims=True)


def unit_rms(vectors):
    rate = lax.rsqrt(jnp.mean(vectors * vectors, axis=0, keepdims=True) + EPS)
    return vectors * rate, rate


def row_numbers(rows):
    return lax.broadcasted_iota(jnp.int32, (rows, 1), 0)


def one_hot(base, columns):
    src = lax.broadcasted_iota(jnp.int32, (base.shape[0], columns), 1)
    return (src == base).astype(F32).astype(BF)


def same_column(rows, stride):
    first = row_numbers(rows)
    second = lax.broadcasted_iota(jnp.int32, (1, rows), 1)
    return lax.rem(first, stride) == lax.rem(second, stride)


def head_parts(qkv_ref, head, hd, width):
    at = head * hd
    return (
        qkv_ref[at : at + hd, :],
        qkv_ref[width + at : width + at + hd, :],
        qkv_ref[2 * width + at : 2 * width + at + hd, :],
    )


def head_weights(q_unit, k_unit, gq, gk, mask, hd):
    qn = (q_unit * (gq * (LOG2E / math.sqrt(hd)))).astype(BF)
    kn = (k_unit * gk).astype(BF)
    weights = jnp.exp2(tn(kn, qn))
    if mask is not None:
        weights = jnp.where(mask, weights, 0.0)
    return (weights * (1.0 / jnp.sum(weights, axis=0, keepdims=True))).astype(BF)


def score_vjp(q, k, v16, weights, grad16, gq, gk, hd):
    q_unit, q_rate = unit_rms(q)
    k_unit, k_rate = unit_rms(k)
    scale = 1.0 / math.sqrt(hd)
    w32 = weights.astype(F32)
    weighted = w32 * tn(v16, grad16)
    d_s = (weighted - w32 * jnp.sum(weighted, axis=0, keepdims=True)).astype(BF)
    d_q = nn((k_unit * gk).astype(BF), d_s) * (gq * scale)
    d_k = nt((q_unit * gq).astype(BF), d_s) * (gk * scale)
    d_q = q_rate * (d_q - q_unit * jnp.mean(q_unit * d_q, axis=0, keepdims=True))
    d_k = k_rate * (d_k - k_unit * jnp.mean(k_unit * d_k, axis=0, keepdims=True))
    return d_q, d_k


def arrange(tr_ref, lhs_ref, me, count):
    size = lhs_ref.shape[0] // count
    for slot in range(count):
        place = (slot % (count // 2)) * 2 + slot // (count // 2)
        start = pl.multiple_of(jnp.bitwise_xor(me, place) * size, 8)
        lhs_ref[slot * size : (slot + 1) * size, :] = tr_ref[pl.ds(start, size), :].astype(BF)


def put_halves(value, keep_ref, send_ref, columns):
    half, size = keep_ref.shape[0], keep_ref.shape[1]
    for slot in range(half):
        keep_ref[slot, :, columns] = value[slot * size : (slot + 1) * size].astype(BF)
        send_ref[slot, :, columns] = value[(half + slot) * size : (half + slot + 1) * size].astype(BF)


def pick_group(dims, part, mid_ref, send_ref):
    steps, per_device, group = dims
    out_rows, in_rows = send_ref.shape[0], mid_ref.shape[0]
    out = row_numbers(out_rows)
    owner, rest = out // (steps * group), lax.rem(out, steps * group)
    base = (rest // group) * (in_rows // steps) + owner * per_device + lax.rem(rest, group)
    send_ref[...] = nn(one_hot(base + part * group, in_rows), mid_ref[...]).astype(BF)


def spatial_forward_kernel(
    dims, x_ref, w_ref, p_ref, mod_ref, gain_ref,
    mid_ref, send_ref, normed_ref, qkv_ref, att_ref, mixed_ref, mixed_scr,
):
    steps, heads, hd, per_device, group = dims
    rows = x_ref.shape[1]
    width = heads * hd
    gq, gk = column(gain_ref[0:1, :]), column(gain_ref[1:2, :])
    for step in range(steps):
        x = x_ref[step].astype(F32)
        normed = modulated(x, mod_ref)
        normed_ref.put(step, normed)
        qkv_ref.put(step, nt(w_ref[...], normed))
        for head in range(heads):
            q, k, v = head_parts(qkv_ref.ref(step), head, hd, width)
            weights = head_weights(unit_rms(q)[0], unit_rms(k)[0], gq, gk, None, hd)
            att_ref[step, head] = weights
            mixed_scr[head * hd : (head + 1) * hd, :] = nn(v.astype(BF), weights)
        att_ref.flush(step)
        mixed = mixed_scr[...].astype(BF)
        mixed_ref[:, step * rows : (step + 1) * rows] = mixed
        mixed_ref.flush(step)
        mid_ref[step * rows : (step + 1) * rows, :] = (
            x + mod_ref[2:3, :] * tn(mixed, p_ref[...])
        ).astype(BF)
    mid_ref.flush()
    pick_group((steps, per_device, group), 0, mid_ref, send_ref)


def between_kernel(
    dims, me_ref, mid_ref, normed_ref, cot_ref, p_ref, mod_ref,
    send_ref, lhs_ref, turned_ref, branch_ref, grad_ref, tr_scr,
):
    steps, per_device, group, count = dims
    pick_group((steps, per_device, group), 1, mid_ref, send_ref)
    send_ref.flush()
    out_rows, in_rows = turned_ref.shape[1], cot_ref.shape[0]
    out = row_numbers(out_rows)
    base = (out // group) * per_device + lax.rem(out, group)
    for part in range(turned_ref.shape[0]):
        turned = nn(one_hot(base + part * group, in_rows), cot_ref[...])
        turned_ref.put(part, turned.astype(BF))
        branch = (mod_ref[2:3, :] * turned).astype(BF)
        branch_ref.put(part, branch)
        grad_ref.put(part, nt(p_ref[...], branch))
    rows = normed_ref.shape[1]
    for step in range(steps):
        tr_scr[:, step * rows : (step + 1) * rows] = normed_ref[step].astype(F32).T
    arrange(tr_scr, lhs_ref, me_ref[0], count)


def temporal_kernel(
    dims, part, mid_ref, turned_ref, grad_ref, w_ref, mod_ref, gain_ref,
    dmid_ref, normed_ref, dqkv_ref, mixed_ref, qkv_scr, mixed_scr, dqkv_scr,
):
    heads, hd, group = dims
    width = heads * hd
    rows = mid_ref.shape[0]
    x = mid_ref[...].astype(F32)
    normed = modulated(x, mod_ref)
    normed_ref.put(..., normed)
    qkv_scr[...] = nt(w_ref[...], normed)
    gq, gk = column(gain_ref[0:1, :]), column(gain_ref[1:2, :])
    mask = same_column(rows, group) if group > 1 else None
    for head in range(heads):
        q, k, v = head_parts(qkv_scr, head, hd, width)
        at = head * hd
        v16 = v.astype(BF)
        weights = head_weights(unit_rms(q)[0], unit_rms(k)[0], gq, gk, mask, hd)
        mixed_scr[at : at + hd, :] = nn(v16, weights)
        grad16 = grad_ref[0, at : at + hd, :].astype(BF)
        d_q, d_k = score_vjp(q, k, v16, weights, grad16, gq, gk, hd)
        dqkv_scr[at : at + hd, :] = d_q
        dqkv_scr[width + at : width + at + hd, :] = d_k
        dqkv_scr[2 * width + at : 2 * width + at + hd, :] = nt(grad16, weights)
    mixed_ref.put(..., mixed_scr[...].astype(BF))
    dqkv = dqkv_scr[...].astype(BF)
    dqkv_ref.put(..., dqkv)
    grad = modulate_vjp(x, mod_ref, tn(dqkv, w_ref[...]))
    dmid_ref[...] = (turned_ref[0].astype(F32) + grad).astype(BF)


def temporal_grad_kernel(
    dims, me_ref, normed0_ref, normed1_ref, dqkv0_ref, dqkv1_ref, mixed0_ref, mixed1_ref,
    branch_ref, keep_ref, send_ref,
    tr_scr, lhs_scr, dqkv_scr, mixed_scr,
):
    width, count = dims
    rows = normed0_ref.shape[0]
    for part, (normed, dqkv, mixed) in enumerate(
        ((normed0_ref, dqkv0_ref, mixed0_ref), (normed1_ref, dqkv1_ref, mixed1_ref))
    ):
        at = slice(part * rows, (part + 1) * rows)
        tr_scr[:, at] = normed[...].astype(F32).T
        dqkv_scr[:, at] = dqkv[...]
        mixed_scr[:, at] = mixed[...]
    arrange(tr_scr, lhs_scr, me_ref[0], count)
    put_halves(nt(lhs_scr[...], dqkv_scr[...]), keep_ref, send_ref, slice(0, 3 * width))
    for part in range(2):
        tr_scr[:, part * rows : (part + 1) * rows] = branch_ref[part].astype(F32).T
    arrange(tr_scr, lhs_scr, me_ref[0], count)
    put_halves(nt(lhs_scr[...], mixed_scr[...]), keep_ref, send_ref, slice(3 * width, 4 * width))


def result_kernel(
    dims, mid0_ref, mid1_ref, mixed0_ref, mixed1_ref, p_ref, mod_ref, out_ref, scr
):
    per_device, group = dims
    rows = mid0_ref.shape[0]
    for part, (mid, mixed) in enumerate(((mid0_ref, mixed0_ref), (mid1_ref, mixed1_ref))):
        scr[part * rows : (part + 1) * rows, :] = (
            mid[...].astype(F32) + mod_ref[2:3, :] * tn(mixed[...], p_ref[...])
        ).astype(BF)
    out_rows = out_ref.shape[0]
    out = row_numbers(out_rows)
    col = lax.rem(out, per_device)
    base = (col // group) * rows + (out // per_device) * group + lax.rem(col, group)
    out_ref[...] = nn(one_hot(base, out_rows), scr[...]).astype(BF)


def spatial_value_kernel(
    dims, me_ref, recv0_ref, recv1_ref, att_ref, p_ref, mod_ref, lhs_ref, mixed_ref,
    dmid_ref, grad_ref, dv_ref, keep_ref, send_ref,
    grad_scr, dv_scr, tr_scr, lhs_scr,
):
    heads, hd, steps, per_device, group, count = dims
    width = heads * hd
    rows, in_rows = dmid_ref.shape[1], recv0_ref.shape[0]
    out = row_numbers(rows)
    owner, col = out // per_device, lax.rem(out, per_device)
    for step in range(steps):
        base = owner * (steps * group) + step * group + lax.rem(col, group)
        part = col // group
        dmid = nn(one_hot(jnp.where(part == 0, base, -1), in_rows), recv0_ref[...])
        dmid += nn(one_hot(jnp.where(part == 1, base, -1), in_rows), recv1_ref[...])
        dmid_ref.put(step, dmid.astype(BF))
        branch = (mod_ref[2:3, :] * dmid).astype(BF)
        here = slice(step * rows, (step + 1) * rows)
        tr_scr[:, here] = branch.astype(F32).T
        grad_scr[...] = nt(p_ref[...], branch)
        grad_ref.put(step, grad_scr[...].astype(BF))
        for head in range(heads):
            at = slice(head * hd, (head + 1) * hd)
            dv_scr[at, :] = nt(grad_scr[at, :].astype(BF), att_ref[step, head])
        dv_ref[:, here] = dv_scr[...].astype(BF)
        dv_ref.flush(step)
    put_halves(nt(lhs_ref[...], dv_ref[...]), keep_ref, send_ref, slice(0, width))
    arrange(tr_scr, lhs_scr, me_ref[0], count)
    put_halves(nt(lhs_scr[...], mixed_ref[...]), keep_ref, send_ref, slice(width, 2 * width))


def spatial_score_kernel(
    dims, qkv_ref, att_ref, grad_ref, gain_ref, lhs_ref,
    dqk_ref, keep_ref, send_ref, dqk_scr,
):
    heads, hd, steps = dims
    width = heads * hd
    rows = qkv_ref.shape[2]
    gq, gk = column(gain_ref[0:1, :]), column(gain_ref[1:2, :])
    for step in range(steps):
        for head in range(heads):
            q, k, v = head_parts(qkv_ref.ref(step), head, hd, width)
            at = head * hd
            grad16 = grad_ref[step, at : at + hd, :]
            d_q, d_k = score_vjp(q, k, v.astype(BF), att_ref[step, head], grad16, gq, gk, hd)
            dqk_scr[at : at + hd, :] = d_q
            dqk_scr[width + at : width + at + hd, :] = d_k
        dqk_ref[:, step * rows : (step + 1) * rows] = dqk_scr[...].astype(BF)
        dqk_ref.flush(step)
    put_halves(nt(lhs_ref[...], dqk_ref[...]), keep_ref, send_ref, slice(None))


def grad_clip_kernel(x_ref, dmid_ref, dqk_ref, dv_ref, w_ref, mod_ref, out_ref):
    cut = dqk_ref.shape[0]
    rows = x_ref.shape[1]
    both = tn(dqk_ref[...], w_ref[:cut, :]) + tn(dv_ref[...], w_ref[cut:, :])
    for step in range(x_ref.shape[0]):
        grad = both[step * rows : (step + 1) * rows]
        grad = modulate_vjp(x_ref[step].astype(F32), mod_ref, grad)
        out_ref.put(step, (dmid_ref[step].astype(F32) + grad).astype(BF))


def shape(dims, kind=BF):
    return jax.ShapeDtypeStruct(tuple(dims), kind)


def whole(array):
    n = len(array.shape)
    return pl.BlockSpec(array.shape, lambda *_: (0,) * n, pipeline_mode=pl.Buffered(1))


def each(array):
    pass


def lane(array):
    pass


def scalar(array):
    return pl.BlockSpec(memory_space=pltpu.SMEM)


def unused(array):
    return pl.BlockSpec(memory_space=pl.ANY)


def small_call(kernel, grid, ins, outs, scratch, micros, after=()):
    first, arrays = len(ins), [a for a, _ in ins]

    def run(*refs):
        kernel(*refs[:first], *refs[first + len(after) :])

    return pl.pallas_call(
        run,
        grid=grid,
        in_specs=[s(a) for a, s in ins] + [unused(a) for a in after],
        out_specs=[s(a) for a, s in outs],
        out_shape=[a for a, _ in outs],
        scratch_shapes=[pltpu.VMEM(d, k) for d, k in scratch],
        compiler_params=pltpu.CompilerParams(vmem_limit_bytes=SMALL_LIMIT),
        cost_estimate=pl.CostEstimate(
            flops=int(micros * FLOPS_PER_MICRO), bytes_accessed=0, transcendentals=0
        ),
    )(*arrays, *after)


class Plain:
    def __init__(self, held):
        self.held, self.shape = held, held.shape

    def __getitem__(self, index):
        return self.held[index]

    def __setitem__(self, index, value):
        self.held[index] = value

    def put(self, index, value):
        self.held[index] = value

    def flush(self, index=None):
        pass


def block_call(kernel, ins, outs, scratch, micros, after=()):
    def spec(array, kind):
        if kind is scalar:
            return scalar(array)
        n = len(array.shape)
        if isinstance(kind, int):
            return pl.BlockSpec((1,) + tuple(array.shape[1:]), lambda i: (kind,) + (0,) * (n - 1))
        return pl.BlockSpec(tuple(array.shape), lambda i: (0,) * n)

    def run(*refs):
        given, refs = refs[: len(ins)], refs[len(ins) + len(after) :]
        results, own = refs[: len(outs)], refs[len(outs) + 1 :]
        refs[len(outs)][...] = jnp.zeros_like(refs[len(outs)])
        given = [r if k is scalar else Plain(r) for r, (_, k) in zip(given, ins)]
        kernel(*given, *[Plain(r) for r in results], *own)

    token = shape((8, 128), F32)
    return pl.pallas_call(
        run,
        grid=(1,),
        in_specs=[spec(a, k) for a, k in ins] + [unused(a) for a in after],
        out_specs=[spec(a, None) for a, _ in outs] + [spec(token, None)],
        out_shape=[a for a, _ in outs] + [token],
        scratch_shapes=[pltpu.VMEM(d, k) for d, k in scratch],
        compiler_params=pltpu.CompilerParams(vmem_limit_bytes=VMEM_LIMIT),
        cost_estimate=pl.CostEstimate(
            flops=int(micros * FLOPS_PER_MICRO), bytes_accessed=0, transcendentals=0
        ),
    )(*[a for a, _ in ins], *after)


class Source:
    def __init__(self, hbm, buf, pairs, sems, first):
        self.buf, self.shape = buf, buf.shape
        self.copies = [pltpu.make_async_copy(a, b, sems.at[first + i]) for i, (a, b) in enumerate(pairs)]
        self.waiting = set(range(len(self.copies)))

    def wait(self, index):
        wanted = [index] if isinstance(index, int) and len(self.copies) > 1 else range(len(self.copies))
        for i in wanted:
            if i in self.waiting:
                self.copies[i].wait()
                self.waiting.remove(i)

    def __getitem__(self, index):
        self.wait(index[0] if isinstance(index, tuple) else index)
        return self.buf[index]

    def ref(self, index):
        self.wait(index)
        return self.buf.at[index]

    def lanes(self, index):
        self.wait(index)
        size = self.shape[1] // len(self.copies)
        return self.buf[:, index * size : (index + 1) * size]


class Sink:
    def __init__(self, hbm, buf, pairs, sems, first):
        self.buf, self.shape = buf, buf.shape
        self.copies = [pltpu.make_async_copy(b, a, sems.at[first + i]) for i, (a, b) in enumerate(pairs)]
        self.left = set(range(len(self.copies)))

    def __getitem__(self, index):
        return self.buf[index]

    def __setitem__(self, index, value):
        self.buf[index] = value

    def ref(self, index):
        return self.buf.at[index]

    def flush(self, index=None):
        for i in sorted(self.left) if index is None else [index]:
            self.copies[i].start()
            self.left.remove(i)

    def put(self, index, value):
        self.buf[index] = value
        self.flush(index if len(self.copies) > 1 else None)


def cuts(hbm, buf, kind, steps):
    if kind is each:
        return [(hbm.at[i], buf.at[i]) for i in range(buf.shape[0])]
    if kind is lane:
        size = buf.shape[1] // steps
        return [(hbm.at[:, pl.ds(i * size, size)], buf.at[:, pl.ds(i * size, size)]) for i in range(steps)]
    if isinstance(kind, int):
        return [(hbm.at[pl.ds(kind, 1)], buf)]
    if isinstance(kind, tuple):
        size = buf.shape[1]
        return [(hbm.at[:, pl.ds(kind[0] * size, size)], buf)]
    return [(hbm, buf)]


def count_cuts(array, kind, steps):
    return array.shape[0] if kind is each else steps if kind is lane else 1


def call(kernel, steps, ins, outs, scratch, micros, after=(), aliases=None):
    arrays = [a for a, _ in ins]
    moved = [(a, k) for a, k in ins if k is not scalar]
    first_of, total = [], 0
    for a, k in moved + list(outs):
        first_of.append(total)
        total += count_cuts(a, k, steps)

    def buffer(array, kind):
        dims = tuple(array.shape)
        if isinstance(kind, int):
            dims = (1,) + dims[1:]
        if isinstance(kind, tuple):
            dims = (dims[0], dims[1] // steps)
        return pltpu.VMEM(dims, array.dtype)

    def run(*refs):
        given, refs = refs[: len(ins)], refs[len(ins) + len(after) :]
        results, refs = refs[: len(outs)], refs[len(outs) :]
        refs[0][...] = jnp.zeros_like(refs[0])
        refs = refs[1:]
        own, refs = refs[: len(scratch)], refs[len(scratch) :]
        sems, bufs = refs[-1], list(refs[:-1])
        firsts = list(first_of)
        sources = []
        for ref, (_, kind) in zip(given, ins):
            if kind is scalar:
                sources.append(ref)
            else:
                buf = bufs.pop(0)
                sources.append(Source(ref, buf, cuts(ref, buf, kind, steps), sems, firsts.pop(0)))
        sinks = []
        for ref, (_, kind) in zip(results, outs):
            buf = bufs.pop(0)
            sinks.append(Sink(ref, buf, cuts(ref, buf, kind, steps), sems, firsts.pop(0)))
        live = [x for x in sources if isinstance(x, Source)]
        live.sort(key=lambda x: math.prod(x.shape) > 16384)
        for i in range(max(len(x.copies) for x in live)):
            for x in live:
                if i < len(x.copies):
                    x.copies[i].start()
        kernel(*sources, *sinks, *own)
        for x in live:
            for i in sorted(x.waiting):
                x.copies[i].wait()
        for x in sinks:
            x.flush()
        for x in sinks:
            for copy in x.copies:
                copy.wait()

    return pl.pallas_call(
        run,
        in_specs=[scalar(a) if k is scalar else unused(a) for a, k in ins] + [unused(a) for a in after],
        out_specs=[unused(a) for a, _ in outs] + [pl.BlockSpec(memory_space=pltpu.VMEM)],
        out_shape=[a for a, _ in outs] + [shape((8, 128), F32)],
        input_output_aliases=aliases or {},
        scratch_shapes=[pltpu.VMEM(d, k) for d, k in scratch]
        + [buffer(a, k) for a, k in moved + list(outs)]
        + [pltpu.SemaphoreType.DMA((total,))],
        compiler_params=pltpu.CompilerParams(vmem_limit_bytes=VMEM_LIMIT),
        cost_estimate=pl.CostEstimate(
            flops=int(micros * FLOPS_PER_MICRO), bytes_accessed=0, transcendentals=0
        ),
    )(*arrays, *after)


def exchange(value, axis, flip):
    count = lax.axis_size(axis)
    return lax.ppermute(value, axis, [(i, i ^ flip) for i in range(count)])


def added(first, second):
    return first.astype(F32) + second.astype(F32)


def halve_kernel(picks, *refs):
    count = len(refs) - 2 * len(picks)
    terms, outs = refs[:count], refs[count:]
    for at, (pair, columns, kept, sent) in enumerate(picks):
        first, second = terms[pair], terms[pair + 1]
        for out_ref, blocks in ((outs[2 * at], kept), (outs[2 * at + 1], sent)):
            for slot, block in enumerate(blocks):
                out_ref[slot] = added(first[block, :, columns], second[block, :, columns]).astype(BF)


def halved_total(refs):
    return jnp.concatenate(
        [added(refs[i][0], refs[i + 1][0]) for i in range(0, len(refs), 2)], axis=1
    )


def total_kernel(*refs):
    refs[-1][...] = halved_total(refs[:-1]).astype(BF)


def piece_kernel(count, place_ref, *refs):
    terms, outs = refs[:-count], refs[-count:]
    odd = len(terms) % 2
    total = halved_total(terms[odd:])
    if odd:
        total = jnp.concatenate([terms[0][...].astype(F32), total], axis=1)
    size = outs[0].shape[0]
    pieces = [total[i * size : (i + 1) * size] for i in range(count)]
    place = place_ref[0]
    for flip, out_ref in enumerate(outs):
        value = pieces[0]
        for i in range(1, count):
            value = jnp.where(jnp.bitwise_xor(place, flip) == i, pieces[i], value)
        out_ref[...] = value.astype(BF)


def scaled_sum(terms, factor):
    return sum((t.astype(F32) for t in terms[1:]), terms[0].astype(F32)) * factor


def first_last_kernel(width, factor, *refs):
    terms, (qkv_ref, proj_ref, part_ref) = refs[:-3], refs[-3:]
    total = scaled_sum([r[...] for r in terms], factor)
    qkv_ref[...] = total[:, : 3 * width]
    proj_ref[...] = total[:, 3 * width : 4 * width]
    part_ref[...] = total[:, 4 * width :]


def last_kernel(width, factor, part_ref, *refs):
    terms, (qkv_ref, proj_ref) = refs[:-2], refs[-2:]
    qkv_ref[:, : 2 * width] = scaled_sum([r[...] for r in terms], factor)
    qkv_ref[:, 2 * width :] = part_ref[:, :width]
    proj_ref[...] = part_ref[:, width:]


class Halving:
    def __init__(self, keep, send, cut):
        bits = int(math.log2(lax.axis_size("wide"))) - 1
        self.terms = [keep, exchange(send, "wide", 1)]
        self.pairs = [(0, slice(0, cut)), (0, slice(cut, keep.shape[2]))]
        self.left = [list(range(bits))[::-1]] * 2
        self.orders = [list(range(bits)), list(range(bits))[::-1]]
        self.size = keep.shape[1]

    def pending(self):
        return bool(self.orders[0])

    def step(self, after=(), micros=0):
        picks, outs, flips = [], [], []
        for at, (pair, columns) in enumerate(self.pairs):
            bit, left = self.orders[at][0], self.left[at]
            shift = len(left) - 1 - left.index(bit)
            blocks = range(2 ** len(left))
            kept = [i for i in blocks if not (i >> shift) & 1]
            sent = [i for i in blocks if (i >> shift) & 1]
            picks.append((pair, columns, kept, sent))
            wide = len(range(*columns.indices(self.terms[pair].shape[2])))
            outs += [(shape((len(kept), self.size, wide)), whole)] * 2
            flips.append(2 << bit)
        got = small_call(
            functools.partial(halve_kernel, picks), (1,), [(a, whole) for a in self.terms],
            outs, [], micros, after,
        )
        self.terms = []
        for at, flip in enumerate(flips):
            self.terms += [got[2 * at], exchange(got[2 * at + 1], "wide", flip)]
            bit = self.orders[at][0]
            self.left[at] = [b for b in self.left[at] if b != bit]
            self.orders[at] = self.orders[at][1:]
        self.pairs = [(0, slice(None)), (2, slice(None))]
        self.done = got[0]

    def rest(self, after=(), micros=0):
        while self.pending():
            self.step(after, micros)


def body(
    clip_tokens,
    cotangent,
    qkv_spatial,
    proj_spatial,
    adaln_spatial,
    qknorm_spatial,
    qkv_temporal,
    proj_temporal,
    adaln_temporal,
    qknorm_temporal,
):
    steps, patches, depth = clip_tokens.shape
    frames, per_device, _ = cotangent.shape
    hd = qknorm_spatial.shape[1]
    width = proj_spatial.shape[1]
    heads = width // hd
    axes = ("wide", "narrow")
    count = lax.axis_size("wide")
    devices = count * lax.axis_size("narrow")
    parts = 2
    group = per_device // parts
    rows = frames * group
    tokens = steps * patches
    w_s, p_s, w_t, p_t = qkv_spatial.T, proj_spatial.T, qkv_temporal.T, proj_temporal.T
    me = lax.axis_index("wide").astype(jnp.int32).reshape(1)
    half = shape((count // 2, depth // count, 2 * width))
    both = shape((count // 2, depth // count, 4 * width))

    middle, send0, normed_s, qkv_s, att_s, mixed_s, _ = call(
        functools.partial(spatial_forward_kernel, (steps, heads, hd, per_device, group)),
        steps,
        [(clip_tokens, each), (w_s, whole), (p_s, whole), (adaln_spatial, whole),
         (qknorm_spatial, whole)],
        [(shape((tokens, depth)), whole), (shape((rows, depth)), whole),
         (shape((steps, patches, depth)), each),
         (shape((steps, 3 * width, patches), F32), each),
         (shape((steps, heads, patches, patches)), each), (shape((width, tokens)), lane)],
        [((width, patches), F32)],
        17,
    )

    def turn(value):
        value = value.reshape(devices, steps * group, depth)
        value = lax.all_to_all(value, axes, split_axis=0, concat_axis=0, tiled=True)
        return value.reshape(rows, depth)

    flat_cot = cotangent.reshape(frames * per_device, depth)
    send1, lhs_s, turned, branch_t, dmixed_t, _ = block_call(
        functools.partial(between_kernel, (steps, per_device, group, count)),
        [(me, scalar), (middle, whole), (normed_s, whole), (flat_cot, whole), (p_t, whole),
         (adaln_temporal, whole)],
        [(shape((rows, depth)), whole), (shape((depth, tokens)), whole),
         (shape((parts, rows, depth)), each), (shape((parts, rows, depth)), each),
         (shape((parts, width, rows), F32), each)],
        [((depth, tokens), F32)],
        6,
    )
    middles = [turn(send0), turn(send1)]

    received, saved = [], []
    for part in range(parts):
        dmid, *keep, _ = block_call(
            functools.partial(temporal_kernel, (heads, hd, group), part),
            [(middles[part], whole), (turned, part), (dmixed_t, part), (w_t, whole),
             (adaln_temporal, whole), (qknorm_temporal, whole)],
            [(shape((rows, depth)), whole), (shape((rows, depth)), whole),
             (shape((3 * width, rows)), whole), (shape((width, rows)), whole)],
            [((3 * width, rows), F32), ((width, rows), F32), ((3 * width, rows), F32)],
            13,
        )
        received.append(turn(dmid))
        saved.append(keep)
    (normed0, dqkv0, mixed0), (normed1, dqkv1, mixed1) = saved

    keep_t, send_t, _ = block_call(
        functools.partial(temporal_grad_kernel, (width, count)),
        [(me, scalar), (normed0, whole), (normed1, whole), (dqkv0, whole), (dqkv1, whole),
         (mixed0, whole), (mixed1, whole), (branch_t, whole)],
        [(both, whole)] * 2,
        [((depth, parts * rows), F32), ((depth, parts * rows), BF),
         ((3 * width, parts * rows), BF), ((width, parts * rows), BF)],
        0,
        [received[0]],
    )
    sum_t = Halving(keep_t, send_t, 2 * width)
    sum_t.step()
    result, done_result = block_call(
        functools.partial(result_kernel, (per_device, group)),
        [(middles[0], whole), (middles[1], whole), (mixed0, whole), (mixed1, whole), (p_t, whole),
         (adaln_temporal, whole)],
        [(shape((frames * per_device, depth)), whole)],
        [((parts * rows, depth), BF)],
        0,
        [sum_t.done],
    )
    dmid_s, dmixed_s, dv_s, keep_b, send_b, done_v = call(
        functools.partial(spatial_value_kernel, (heads, hd, steps, per_device, group, count)),
        steps,
        [(me, scalar), (received[0], whole), (received[1], whole), (att_s, each), (p_s, whole),
         (adaln_spatial, whole), (lhs_s, whole), (mixed_s, whole)],
        [(shape((steps, patches, depth)), each), (shape((steps, width, patches)), each),
         (shape((width, tokens)), lane), (half, whole), (half, whole)],
        [((width, patches), F32), ((width, patches), F32),
         ((depth, tokens), F32), ((depth, tokens), BF)],
        1,
        [sum_t.done, done_result],
    )
    cut = 128 * -(-2 * width // 256)
    sum_t.rest([done_v], 20)
    sum_b = Halving(keep_b, send_b, cut)
    sum_b.step([sum_t.done])
    dqk_s, keep_a, send_a, done_s = call(
        functools.partial(spatial_score_kernel, (heads, hd, steps)),
        steps,
        [(qkv_s, each), (att_s, each), (dmixed_s, each), (qknorm_spatial, whole), (lhs_s, whole)],
        [(shape((2 * width, tokens)), lane), (half, whole), (half, whole)],
        [((2 * width, patches), F32)],
        11,
        [sum_b.done],
    )
    narrow = lax.axis_size("narrow")
    factor = 1.0 / math.sqrt(frames * patches)
    share = depth // devices
    place = lax.axis_index("narrow").astype(jnp.int32).reshape(1)

    def pieces_of(terms, columns, after):
        pieces = small_call(
            functools.partial(piece_kernel, narrow), (1,),
            [(place, scalar)] + [(a, whole) for a in terms],
            [(shape((share, columns)), whole)] * narrow, [], 20, after,
        )
        return pieces[0], [exchange(p, "narrow", i) if i else p for i, p in enumerate(pieces)]

    (total_t,) = small_call(
        total_kernel, (1,), [(a, whole) for a in sum_t.terms],
        [(shape((depth // count, 4 * width)), whole)], [], 20, [done_s],
    )
    sum_b.rest([total_t])
    sum_a = Halving(keep_a, send_a, cut)
    sum_a.step([sum_b.done], 10)
    first_b, terms_b = pieces_of([total_t] + sum_b.terms, 6 * width, [sum_a.done])
    sum_a.rest([first_b])
    grad_clip, done_clip = block_call(
        grad_clip_kernel,
        [(clip_tokens, each), (dmid_s, each), (dqk_s, lane), (dv_s, lane), (w_s, whole),
         (adaln_spatial, whole)],
        [(shape((steps, patches, depth)), each)],
        [],
        4,
        [sum_a.done],
    )
    first_a, terms_a = pieces_of(sum_a.terms, 2 * width, [done_clip])
    whole_grad, part_grad = shape((share, 3 * width), F32), shape((share, width), F32)
    grad_qkv_t, grad_proj_t, rest = small_call(
        functools.partial(first_last_kernel, width, factor), (1,), [(a, whole) for a in terms_b],
        [(whole_grad, whole), (part_grad, whole), (shape((share, 2 * width), F32), whole)], [], 2,
        [first_a],
    )
    grad_qkv_s, grad_proj_s = small_call(
        functools.partial(last_kernel, width, factor), (1,),
        [(rest, whole)] + [(a, whole) for a in terms_a],
        [(whole_grad, whole), (part_grad, whole)], [], 2,
    )
    return (
        result.reshape(frames, per_device, depth),
        grad_clip,
        grad_qkv_s,
        grad_proj_s,
        grad_qkv_t,
        grad_proj_t,
    )


def solution(mesh):
    tokens = P(("wide", "narrow"), None, None)
    columns = P(None, ("wide", "narrow"), None)
    own = P(("wide", "narrow"), None)
    return jax.shard_map(
        body,
        mesh=mesh,
        in_specs=(tokens, columns) + (P(),) * 8,
        out_specs=(columns, tokens, own, own, own, own),
        check_vma=False,
    )
```
